128 devices in a mesh: side: 2 (over core), dev: 64 (over y, x, z).
Axes of the slice: x: 4, y: 4, z: 4, core: 2. Of those that a mesh axis runs over, the one named last changes fastest.
Arguments:
- queries: bfloat16 [1024, 128, 576], P(('side', 'dev'))
- cache: bfloat16 [1024, 512, 576], P(('side', 'dev'))
- lengths: int32 [1024], P(('side', 'dev')), may hold values from 2 to 512, as said below
- w_uv: bfloat16 [128, 512, 128], P(('side', 'dev')), may hold values from -0.25 to 0.25
- w_out: bfloat16 [16384, 7168], P(('side', 'dev')), may hold values from -0.046875 to 0.046875
- resid: bfloat16 [1024, 7168], P(('side', 'dev')), may hold values from -6 to 6
- norm_gain: float32 [7168], replicated, may hold values from 0.1 to 1.9
- expert_ids: int32 [1024, 4], P(('side', 'dev')), may hold values from 0 to 23, all different within a row; in each aligned block of 8 rows (0 to 7, 8 to 15, ...) at most 2 rows name the same one
- gate_weights: bfloat16 [1024, 4], P(('side', 'dev')), may hold values from 0.099609375 to 1
- replica_slot: int32 [24, 2], replicated, may hold values from 0 to 31, as said below
- w_gate: bfloat16 [128, 7168, 256], P(('side', 'dev')), as said below
- w_up: bfloat16 [128, 7168, 256], P(('side', 'dev')), as said below
- w_down: bfloat16 [128, 256, 7168], P(('side', 'dev')), as said below
Outputs:
- attended: bfloat16 [1024, 7168], P(('side', 'dev'))
- layer_out: bfloat16 [1024, 7168], P(('side', 'dev'))
The draws below stay inside these ranges and needn't reach their ends.
Inputs may be any that keep to these rules, and one draw needn't show every extreme that they name: `lengths`: each request has at least two valid slots; some request uses all 512. `expert_ids`: among the 8 requests of one device (aligned blocks) no expert is chosen more than 2 times, and some expert is chosen exactly 2 times. `replica_slot`: column 0 of expert e is slot e. 8 experts have a second replica in the slots 24 to 31, one each; for the others column 1 equals column 0. `w_gate`: entries of two slots that hold the same expert are equal, quarter by quarter. `w_up`: as for w_gate. `w_down`: as for w_gate.
All inputs are finite; a program needn't handle non-finite values.
Results may differ from the reference program's by a relative error of at most 0.015.
Values may be sent and summed in bfloat16 or wider, within the bound.
A program may use at most 192 MiB of HBM per device.

```python
import math
import jax
import jax.numpy as jnp
import numpy as np
from jax import lax

D = 7168
H = 128
LAT = 512
ROPE = 64
VD = 128
FF = 1024
GROUP = 4
TOP = 4
R_DEV = 8
LEN = 512
REQUESTS = 1024
FF_DEV = 256
SLOTS = 32
HOT = 8
EXPERTS = 24
CAP = 2
DEVICES = 128


def cache_base(key):
    return jax.random.normal(jax.random.fold_in(key, 201), (REQUESTS, LEN, LAT + ROPE), jnp.float32)


def hot_list(key):
    return jax.random.permutation(jax.random.fold_in(key, 301), EXPERTS)[:HOT].astype(jnp.int32)


def expert_block(key, own_key, row_count, col_count, spread_scale):
    hot_set = hot_list(key)
    holder = jnp.concatenate([jnp.arange(EXPERTS, dtype=jnp.int32), hot_set])
    device_ids = jnp.arange(DEVICES, dtype=jnp.int32)
    owner = holder[device_ids // GROUP] * GROUP + device_ids % GROUP

    def draw_slice(owner_index):
        return jax.random.normal(jax.random.fold_in(own_key, owner_index), (row_count, col_count), jnp.float32) * spread_scale
    return jax.vmap(draw_slice)(owner)


def draw_cache(key, part):
    values = cache_base(key)
    return values.astype(jnp.bfloat16)


def draw_queries(key, part):
    key = jax.random.fold_in(key, 7)
    return jax.random.normal(key, (REQUESTS, H, LAT + ROPE), jnp.float32).astype(jnp.bfloat16)


def draw_lengths(key, part):
    key = jax.random.fold_in(key, 3)
    values = jax.random.randint(key, (REQUESTS,), 2, LEN + 1, jnp.int32)
    position = jax.random.randint(jax.random.fold_in(key, 1), (), 0, REQUESTS, jnp.int32)
    return values.at[position].set(LEN)


def draw_replica_slot(key, part):
    hot_set = hot_list(key)
    primary = jnp.arange(EXPERTS, dtype=jnp.int32)
    table = jnp.stack([primary, primary], axis=1)
    return table.at[hot_set, 1].set(EXPERTS + jnp.arange(HOT, dtype=jnp.int32))


def draw_w_gate(key, part):
    own_key = jax.random.fold_in(key, 11)
    return expert_block(key, own_key, D, FF_DEV, D ** (-0.5)).astype(jnp.bfloat16)


def draw_w_up(key, part):
    own_key = jax.random.fold_in(key, 12)
    return expert_block(key, own_key, D, FF_DEV, D ** (-0.5)).astype(jnp.bfloat16)


def draw_w_down(key, part):
    own_key = jax.random.fold_in(key, 13)
    return expert_block(key, own_key, FF_DEV, D, FF ** (-0.5)).astype(jnp.bfloat16)


def shard_levels(key, extent, pieces, least, top_value):
    level, own = 1.0, jax.random.fold_in(key, 6)
    for dim, blocks in pieces:
        steps = jnp.exp(jax.random.uniform(jax.random.fold_in(own, dim), (blocks,), jnp.float32, least / len(pieces), top_value / len(pieces)))
        level = level * jnp.repeat(steps, extent[dim] // blocks).reshape([-1 if axis == dim else 1 for axis in range(len(extent))])
    return level


def assign_block(stream_key, own, number, rows, amount, top, most, lean):
    sequence = jax.random.permutation(stream_key, amount)
    crowded, ordinary = load_shares(amount, rows * top, most, lean, True), load_shares(amount, rows * top, most, lean, False)
    places = jnp.arange(amount)

    def named(sizes, offset_by):
        used = int((sizes > 0).sum())
        fixed = max(1, used // 4)
        moved = fixed + (places - fixed + offset_by * (used - fixed)) % max(1, amount - fixed)
        return jnp.zeros((amount,), jnp.int32).at[sequence[jnp.where(places < fixed, places, moved)]].set(jnp.asarray(sizes, jnp.int32))

    sizes = jnp.where(number % 4 == 0, named(crowded, number // 4), named(ordinary, number - number // 4 - 1))
    mixed = jax.random.permutation(jax.random.fold_in(own, 3), amount)
    giver, receiver = mixed[0:amount // 2 * 2:2], mixed[1:amount // 2 * 2:2]
    slack = jnp.minimum(sizes[giver] - 1, most - sizes[receiver]) // 2
    slack = jnp.where((giver == sequence[0]) | (receiver == sequence[0]) | (sizes[receiver] == 0), 0, jnp.maximum(slack, 0))
    moved = jax.random.randint(jax.random.fold_in(own, 4), (amount // 2,), 0, 1 << 20) % (slack + 1)
    sizes = sizes.at[giver].add(-moved).at[receiver].add(moved)
    members = jnp.searchsorted(jnp.cumsum(sizes), jnp.arange(rows * top), side="right").astype(jnp.int32)
    table = members.reshape(top, rows).T
    table = table[jax.random.permutation(jax.random.fold_in(own, 1), rows)]
    offset_by = jax.random.randint(jax.random.fold_in(own, 2), (rows, 1), 0, top)
    return jnp.take_along_axis(table, (jnp.arange(top)[None, :] + offset_by) % top, axis=1)


def load_shares(number_of, total, limit, lean, full):
    weights = [(1 << 20) // math.isqrt(standing ** lean) + 1 for standing in range(1, number_of + 1)]
    largest = limit if full else min(limit, max(-(-total // number_of), total * weights[0] // sum(weights)))
    least = 1 if total - largest >= number_of - 1 else 0
    given, spare = [largest] + [least] * (number_of - 1), total - largest - least * (number_of - 1)
    while spare > 0:
        movable = [i for i in range(1, number_of) if given[i] < largest] or [i for i in range(1, number_of) if given[i] < limit]
        whole, left = sum([weights[i] for i in movable]), spare
        for i in movable:
            addition = min(limit - given[i], max(1, left * weights[i] // whole), spare)
            given[i] = given[i] + addition
            spare = spare - addition
    return np.array(given)


def centred(rng, dims, deviation, bound, split=(), kind=jnp.bfloat16):
    entries = deviation * jax.random.normal(rng, dims, jnp.float32)
    if split:
        entries = entries * shard_levels(rng, dims, split, -0.22, 0.18)
    return jnp.clip(entries, -bound, bound).astype(kind)


def setup_inputs(seed: int = 0) -> dict:
    seeds = jax.random.split(jax.random.key(seed), 14)
    queries = draw_queries(jax.random.fold_in(seeds[13], 71), 0)
    cache = draw_cache(jax.random.fold_in(seeds[13], 71), 0)
    lengths = draw_lengths(jax.random.fold_in(seeds[13], 71), 0)
    w_uv = centred(seeds[3], (H, LAT, VD), LAT ** -0.5, 0.25, ((0, 128),))
    w_out = centred(seeds[4], (H * VD, D), (H * VD) ** -0.5, 0.046875, ((0, 128),))
    resid = centred(seeds[5], (REQUESTS, D), 1.0, 6.0, ((0, 128),))
    norm_gain = jnp.clip(1.0 + 0.18 * jax.random.normal(seeds[6], (D,), jnp.float32), 0.1, 1.9)
    expert_ids_keys = jax.random.split(jax.random.fold_in(seeds[7], 1), REQUESTS // R_DEV)
    expert_ids_turns = jax.random.permutation(jax.random.fold_in(seeds[7], 3), REQUESTS // R_DEV)
    expert_ids = jax.vmap(lambda own, number: assign_block(jax.random.fold_in(seeds[7], 2), own, number, R_DEV, EXPERTS, TOP, CAP, 2))(expert_ids_keys, expert_ids_turns).reshape((REQUESTS, TOP))
    gate_weights = jnp.clip(0.099609375 + 0.9003906 * jax.random.uniform(seeds[8], (REQUESTS, TOP), jnp.float32) ** shard_levels(seeds[8], (REQUESTS, TOP), ((0, 128),), -0.2, 0.2), 0.099609375, 1.0).astype(jnp.bfloat16)
    replica_slot = draw_replica_slot(jax.random.fold_in(seeds[13], 71), 0)
    w_gate = draw_w_gate(jax.random.fold_in(seeds[13], 71), 0)
    w_up = draw_w_up(jax.random.fold_in(seeds[13], 71), 0)
    w_down = draw_w_down(jax.random.fold_in(seeds[13], 71), 0)
    return dict(queries=queries, cache=cache, lengths=lengths, w_uv=w_uv, w_out=w_out, resid=resid, norm_gain=norm_gain, expert_ids=expert_ids, gate_weights=gate_weights, replica_slot=replica_slot, w_gate=w_gate, w_up=w_up, w_down=w_down)


def attend_request(packed):
    query_rows, cache_rows, length = packed
    score_scale = 1.0 / math.sqrt(VD + ROPE)
    scores = jnp.dot(query_rows, cache_rows.T, preferred_element_type=jnp.float32) * score_scale
    valid_key = jnp.arange(LEN, dtype=jnp.int32) < length
    scores = jnp.where(valid_key[None, :], scores, -1e+30)
    highest = lax.optimization_barrier(jnp.max(scores, axis=1, keepdims=True))
    exponent = jnp.exp(scores - highest)
    weights = (exponent / lax.optimization_barrier(jnp.sum(exponent, axis=1, keepdims=True))).astype(jnp.bfloat16)
    return jnp.dot(weights, cache_rows[:, :LAT], preferred_element_type=jnp.float32).astype(jnp.bfloat16)

def reference(queries, cache, lengths, w_uv, w_out, resid, norm_gain, expert_ids, gate_weights, replica_slot, w_gate, w_up, w_down):
    latent = lax.map(attend_request, (queries, cache, lengths))
    values = jnp.einsum('rhc,hce->rhe', latent.astype(jnp.float32), w_uv.astype(jnp.float32)).astype(jnp.bfloat16)
    attention = jnp.dot(values.reshape(REQUESTS, H * VD), w_out, preferred_element_type=jnp.float32)
    attended = (resid.astype(jnp.float32) + attention).astype(jnp.bfloat16)
    stream = attended.astype(jnp.float32)
    normed = (stream * lax.rsqrt(lax.optimization_barrier(jnp.mean(stream * stream, axis=1, keepdims=True)) + 1e-06) * norm_gain).astype(jnp.bfloat16)
    parity = (jnp.arange(REQUESTS, dtype=jnp.int32)[:, None] + jnp.arange(TOP, dtype=jnp.int32)[None, :]) % 2
    pair_slot = replica_slot[expert_ids, parity].reshape(-1)
    pair_gate = gate_weights.astype(jnp.float32).reshape(-1)
    pair_count = REQUESTS * TOP
    most_rows = DEVICES * CAP

    def per_slot(carry, slot_id):
        chosen = pair_slot == slot_id
        position = jnp.nonzero(chosen, size=most_rows, fill_value=pair_count)[0].astype(jnp.int32)
        clamped = jnp.minimum(position, pair_count - 1)
        live = (position < pair_count).astype(jnp.float32)
        rows_in = normed[clamped // TOP]
        gate_in = pair_gate[clamped] * live
        total = carry
        for quarter in range(GROUP):
            holder = slot_id * GROUP + quarter
            gate_one = lax.dynamic_index_in_dim(w_gate, holder, 0, keepdims=False)
            up_one = lax.dynamic_index_in_dim(w_up, holder, 0, keepdims=False)
            down_one = lax.dynamic_index_in_dim(w_down, holder, 0, keepdims=False)
            gate_proj = jnp.dot(rows_in, gate_one, preferred_element_type=jnp.float32)
            up_proj = jnp.dot(rows_in, up_one, preferred_element_type=jnp.float32)
            hidden = (jax.nn.silu(gate_proj) * up_proj).astype(jnp.bfloat16)
            piece = (jnp.dot(hidden, down_one, preferred_element_type=jnp.float32) * gate_in[:, None]).astype(jnp.bfloat16)
            total = total.at[position].add(piece.astype(jnp.float32), mode='drop')
        return (total, None)
    moe_pairs, unused = lax.scan(per_slot, jnp.zeros((pair_count, D), jnp.float32), jnp.arange(SLOTS, dtype=jnp.int32))
    moe = lax.optimization_barrier(jnp.sum(moe_pairs.reshape(REQUESTS, TOP, D), axis=1))
    layer_out = (stream + moe).astype(jnp.bfloat16)
    return (attended, layer_out)
```

```python
import functools
import math

import jax
import jax.numpy as jnp
from jax import lax
from jax.experimental import pallas as pl
from jax.experimental.pallas import tpu as pltpu
from jax.sharding import PartitionSpec as P

GROUP = 4
BF = jnp.bfloat16
F32 = jnp.float32
MB = 1 << 20


def place():
    s = lax.axis_index("side")
    dev = lax.axis_index("dev")
    return s, dev // 4, dev % 4


def dot(a, b, dims=((1,), (0,))):
    return lax.dot_general(a, b, (dims, ((), ())), preferred_element_type=F32)


def send(src, dst, ssem, rsem, s, yx, z):
    pltpu.make_async_remote_copy(
        src_ref=src,
        dst_ref=dst,
        send_sem=ssem,
        recv_sem=rsem,
        device_id=(s, yx * 4 + z),
        device_id_type=pl.DeviceIdType.MESH,
    ).start()


def keep(src, dst, sem):
    pltpu.make_async_copy(src, dst, sem).start()


def wait(ref, sem):
    pltpu.make_async_copy(ref, ref, sem).wait()


def around(yx, k):
    return ((yx // 4 + k // 4) % 4) * 4 + (yx % 4 + k % 4) % 4


def iota(shape, dim):
    return lax.broadcasted_iota(jnp.int32, shape, dim)


def attention_phase(
    lengths, queries, cache, w_uv, w_out, resid,
    cbuf, late, lrecv, wuv, wo, vals, osend, orecv, rsend, rrecv, gathered,
    csem, ssem, rsem, vsem, osem,
):
    s, yx, z = place()
    for r in range(8):
        pltpu.make_async_copy(cache.at[r], cbuf.at[r], csem.at[r]).start()
    own_col = pl.multiple_of((s * 4 + z) * 128, 128)
    keep(w_uv, wuv.at[:, pl.ds(own_col, 128)], rsem.at[0])
    keep(w_out.at[:, pl.ds(pl.multiple_of(z * 1792, 256), 1792)], wo.at[pl.ds(own_col, 128)], rsem.at[1])
    for q in range(4):
        rsend[q] = resid[:, q * 1792 : (q + 1) * 1792].astype(F32)
    for k in (1, 3, 2):
        send(w_uv, wuv.at[:, pl.ds(own_col, 128)], ssem.at[0], rsem.at[0], s, yx, (z + k) % 4)
    for k in (1, 3, 2):
        t = (z + k) % 4
        send(
            w_out.at[:, pl.ds(pl.multiple_of(t * 1792, 256), 1792)],
            wo.at[pl.ds(own_col, 128)],
            ssem.at[1], rsem.at[1], s, yx, t,
        )
    keep(rsend.at[z], rrecv.at[z], rsem.at[2])
    for k in (1, 3, 2):
        t = (z + k) % 4
        send(rsend.at[t], rrecv.at[z], ssem.at[2], rsem.at[2], s, yx, t)

    row, col = iota((128, 128), 0), iota((128, 128), 1)
    head = ((row % 8) // 4) * 64 + (row // 8) * 4 + row % 4
    order = jnp.where(col == head, 1.0, 0.0).astype(BF)
    scale = 1.0 / math.sqrt(192)
    column = iota((128, 512), 1)

    def one(r):
        wait(cbuf.at[r], csem.at[r])
        q = dot(order, queries[r], ((1,), (1,))).astype(BF)
        scores = dot(q, cbuf[r]) * scale
        scores = jnp.where(column < lengths[r], scores, -1e30)
        weight = jnp.exp(scores - jnp.max(scores, axis=1, keepdims=True))
        total = jnp.sum(weight, axis=1, keepdims=True)
        latent = dot(weight.astype(BF), cbuf[r, 0:512], ((1,), (1,)))
        return (latent / total).reshape(16, 8, 512)

    def step(i, carry):
        late[i] = jnp.concatenate([one(2 * i), one(2 * i + 1)], axis=1).astype(BF)
        keep(late.at[i, yx], lrecv.at[yx, i], rsem.at[5])

        def out(k, carry):
            to = around(yx, k)
            send(late.at[i, to], lrecv.at[yx, i], ssem.at[5], rsem.at[5], s, to, z)
            return carry

        return lax.fori_loop(1, 16, out, carry)

    lax.fori_loop(0, 4, step, 0)

    half = pl.ds(pl.multiple_of(s * 512, 512), 512)
    wait(wuv.at[:, half], rsem.at[0])
    send(wuv.at[:, half], wuv.at[:, half], ssem.at[3], rsem.at[3], 1 - s, yx, z)
    wait(wuv.at[:, half], rsem.at[3])
    wait(lrecv, rsem.at[5])

    mine = iota((256, 1024), 0) % 8 == iota((256, 1024), 1) // 128
    pick = jnp.where(iota((32, 256), 1) // 8 == iota((32, 256), 0), 1.0, 0.0).astype(BF)

    def value(j, carry):
        rows = lrecv[pl.ds(j * 4, 4)].reshape(256, 512)
        full = dot(rows, wuv[...])
        own = jnp.where(mine, full, 0.0).astype(BF)
        vals[z, j] = dot(pick, own).astype(BF)
        for k in (1, 3, 2):
            send(vals.at[z, j], vals.at[z, j], ssem.at[6], vsem.at[z], s, yx, (z + k) % 4)
        return carry

    lax.fori_loop(0, 4, value, 0)

    wait(wo.at[half], rsem.at[1])
    send(wo.at[half], wo.at[half], ssem.at[4], rsem.at[4], 1 - s, yx, z)
    wait(wo.at[half], rsem.at[4])

    for pp in range(2):
        p = (z // 2 + pp) % 2
        for e in range(2):
            @pl.when(2 * p + e != z)
            def _():
                wait(vals.at[2 * p + e], vsem.at[2 * p + e])

        def project(c, carry):
            at = pl.ds(pl.multiple_of(c * 256, 256), 256)
            got = dot(vals[pl.ds(2 * p, 2)].reshape(256, 1024), wo[:, at]).reshape(2, 16, 8, 256)
            osend[p, :, :, at] = jnp.concatenate([got[0], got[1]], axis=1).astype(BF)
            return carry

        lax.fori_loop(0, 7, project, 0)
        keep(osend.at[p, yx], orecv.at[p, yx], osem.at[p])

        def out(k, carry):
            to = around(yx, k)
            send(osend.at[p, to], orecv.at[p, yx], ssem.at[7], osem.at[p], s, to, z)
            return carry

        lax.fori_loop(1, 16, out, 0)

    here = pl.ds(pl.multiple_of(z * 1792, 256), 1792)
    for pp in range(2):
        p = (z // 2 + pp) % 2
        wait(orecv.at[p], osem.at[p])
        if pp == 0:
            wait(rrecv, rsem.at[2])
        total = jnp.concatenate([rrecv[2 * p], rrecv[2 * p + 1]], axis=0)
        summed = lax.fori_loop(0, 16, lambda i, a: a + orecv[p, i].astype(F32), jnp.zeros((16, 1792), F32))
        gathered[s, pl.ds(pl.multiple_of(p * 16, 16), 16), here] = (total + summed).astype(BF)

    for k in (1, 3, 2):
        send(gathered.at[s, :, here], gathered.at[s, :, here], ssem.at[8], rsem.at[8], s, yx, (z + k) % 4)
    wait(gathered.at[s, :, pl.ds(0, 5376)], rsem.at[8])
    send(gathered.at[s], gathered.at[s], ssem.at[9], rsem.at[9], 1 - s, yx, z)
    wait(gathered.at[s], rsem.at[9])

    for ref, number in (
        (wuv.at[:, pl.ds(0, 384)], 0),
        (wo.at[pl.ds(0, 384)], 1),
        (rsend.at[pl.ds(0, 3)], 2),
        (wuv.at[:, half], 3),
        (wo.at[half], 4),
        (late.at[:, pl.ds(0, 15)], 5),
        (vals.at[pl.ds(0, 3)], 6),
        (osend.at[:, pl.ds(0, 15)], 7),
        (gathered.at[s, :, pl.ds(0, 5376)], 8),
        (gathered.at[s], 9),
    ):
        wait(ref, ssem.at[number])


def attention_kernel(lengths, queries, cache, w_uv, w_out, resid, gathered, *scratch):
    attention_phase(lengths, queries, cache, w_uv, w_out, resid, *scratch[:10], gathered, *scratch[10:])


VMEM = pl.BlockSpec(memory_space=pltpu.VMEM)
SMEM = pl.BlockSpec(memory_space=pltpu.SMEM)
ANY = pl.BlockSpec(memory_space=pl.ANY)


def attention_scratch():
    return [
        pltpu.VMEM((8, 576, 512), BF),
        pltpu.VMEM((4, 16, 16, 512), BF),
        pltpu.VMEM((16, 4, 16, 512), BF),
        pltpu.VMEM((512, 1024), BF),
        pltpu.VMEM((1024, 1792), BF),
        pltpu.VMEM((4, 4, 32, 1024), BF),
        pltpu.VMEM((2, 16, 16, 1792), BF),
        pltpu.VMEM((2, 16, 16, 1792), BF),
        pltpu.VMEM((4, 8, 1792), F32),
        pltpu.VMEM((4, 8, 1792), F32),
    ]


def attention_call(lengths, queries, cache, w_uv, w_out, resid):
    return pl.pallas_call(
        attention_kernel,
        out_shape=jax.ShapeDtypeStruct((2, 32, 7168), BF),
        in_specs=[SMEM, VMEM, ANY, ANY, ANY, VMEM],
        out_specs=VMEM,
        scratch_shapes=attention_scratch()
        + [pltpu.SemaphoreType.DMA((n,)) for n in (8, 10, 10, 4, 2)],
        compiler_params=pltpu.CompilerParams(has_side_effects=True, vmem_limit_bytes=56 * MB),
        name="attention",
    )(lengths, jnp.swapaxes(queries, 1, 2), jnp.swapaxes(cache, 1, 2), w_uv[0], w_out, resid)


def expert_phase(
    expert_ids, gates, replicas, gain, w_gate, w_up, w_down, gathered, attended, layer_out,
    wg, wu, wd, route, normed, select, picked, rows, acc, hidden, ysend, yrecv, bsend, asend, back, part, fsend, frecv,
    wsem, ssem, rsem, xsem, ysem, bsem,
):
    s, yx, z = place()
    keep(w_gate, wg, wsem.at[0])
    keep(w_up, wu, wsem.at[1])
    keep(w_down, wd, wsem.at[2])
    slot_me = s * 16 + yx
    line_me = s * 4 + z

    row, lane = iota((64, 128), 0), iota((64, 128), 1)

    def choice(p, carry):
        table, used = carry
        t, k = p // 4, p % 4
        slot = replicas[expert_ids[t, k], (t + k) % 2]
        same = row // 2 == slot
        hit = same & (row % 2 == used)
        table = jnp.where(hit & (lane == line_me * 8 + t), 1.0, table)
        table = jnp.where(hit & (lane == 64 + line_me * 8 + t), gates[t, k], table)
        return table, used + jnp.where(same, 1, 0)

    table, _ = lax.fori_loop(0, 32, choice, (jnp.zeros((64, 128), F32), jnp.zeros((64, 128), jnp.int32)))
    route[line_me] = table.astype(BF)

    def announce(k, carry):
        send(route.at[line_me], route.at[line_me], ssem.at[0], rsem.at[0], (s + k // 4) % 2, yx, (z + k % 4) % 4)
        return carry

    lax.fori_loop(1, 8, announce, 0)

    def norm(b, carry):
        at = pl.ds(pl.multiple_of((b % 2) * 16, 16), 16)
        stream = gathered[b // 2, at].astype(F32)
        mean = jnp.mean(stream * stream, axis=1, keepdims=True)
        normed[pl.ds(pl.multiple_of(b * 16, 16), 16)] = (stream * lax.rsqrt(mean + 1e-06) * gain[...]).astype(BF)
        return carry

    lax.fori_loop(0, 4, norm, 0)

    wait(route.at[pl.ds(0, 7)], rsem.at[0])
    a, b = iota((512, 512), 0), iota((512, 512), 1)
    deal = jnp.where(b == ((a % 16) // 2) * 64 + (a // 16) * 2 + a % 2, 1.0, 0.0).astype(BF)
    select[...] = dot(deal, route[...].reshape(512, 128)).astype(BF)

    for c in range(4):
        first = (z * 2 + s) * 512 if c == 0 else 4096 + s * 1536 + (c - 1) * 512
        cols = pl.ds(pl.multiple_of(first, 512), 512)
        picked[c] = dot(select[:, 0:64], normed[:, cols]).astype(BF).reshape(32, 16, 512)
        number = 1 if c == 0 else 2
        place_in = rows.at[pl.ds(pl.multiple_of(yx * 16, 16), 16), cols]
        keep(picked.at[c, slot_me], place_in, rsem.at[number])

        def out(k, carry):
            to, core = around(yx, k // 2), (s + k % 2) % 2
            send(picked.at[c, core * 16 + to], place_in, ssem.at[number], rsem.at[number], core, to, z)
            return carry

        lax.fori_loop(1, 32, out, 0)

    own = pl.ds(pl.multiple_of(z * 1024, 1024), 1024)
    wait(rows.at[:, own], rsem.at[1])
    for k in (1, 3, 2):
        send(rows.at[:, own], rows.at[:, own], ssem.at[3], xsem.at[z], s, yx, (z + k) % 4)

    wait(wg, wsem.at[0])
    wait(wu, wsem.at[1])
    acc[...] = jnp.zeros_like(acc)

    def project(c, carry):
        at = pl.ds(pl.multiple_of(c * 1024, 1024), 1024)
        acc[0] += dot(rows[:, at], wg[at])
        acc[1] += dot(rows[:, at], wu[at])
        return carry

    project(z, 0)
    for k in (1, 3, 2):
        t = (z + k) % 4
        wait(rows.at[:, pl.ds(pl.multiple_of(t * 1024, 1024), 1024)], xsem.at[t])
        project(t, 0)
    wait(rows.at[:, pl.ds(4096, 3072)], rsem.at[2])
    lax.fori_loop(4, 7, project, 0)
    gate = acc[0]
    hidden[...] = (gate * jax.nn.sigmoid(gate) * acc[1]).astype(BF)
    wait(wd, wsem.at[2])

    for k in (1, 3, 2, 0):
        t = (z + k) % 4
        at = pl.ds(pl.multiple_of(t * 1024, 1024), 1024)
        got = dot(hidden[...], wd[:, at]).astype(BF)
        if k == 0:
            yrecv[z] = got
        else:
            ysend[t] = got
            send(ysend.at[t], yrecv.at[z], ssem.at[4], ysem.at[z], s, yx, t)

    def give_back(source, core, c):
        keep_here = core == s

        @pl.when(keep_here)
        def _():
            keep(source.at[pl.ds(pl.multiple_of(yx * 16, 16), 16)], back.at[c, slot_me], bsem.at[c])

        @pl.when(jnp.logical_not(keep_here))
        def _():
            send(source.at[pl.ds(pl.multiple_of(yx * 16, 16), 16)], back.at[c, slot_me], ssem.at[5], bsem.at[c], core, yx, z)

        def out(k, carry):
            to = around(yx, k)
            send(source.at[pl.ds(pl.multiple_of(to * 16, 16), 16)], back.at[c, slot_me], ssem.at[5], bsem.at[c], core, to, z)
            return carry

        lax.fori_loop(1, 16, out, 0)

    for c in range(3):
        for core in range(2):
            j = core * 3 + c
            bsend[j] = dot(hidden[...], wd[:, 4096 + j * 512 : 4608 + j * 512]).astype(BF)
            give_back(bsend.at[j], core, c)

    for k in (1, 3, 2):
        wait(yrecv.at[(z + k) % 4], ysem.at[(z + k) % 4])
    for core in range(2):
        at = pl.ds(core * 512, 512)
        total = (yrecv[0, :, at].astype(F32) + yrecv[1, :, at].astype(F32)) + (
            yrecv[2, :, at].astype(F32) + yrecv[3, :, at].astype(F32)
        )
        asend[core] = total.astype(BF)
        give_back(asend.at[core], core, 3)

    for c in range(4):
        wait(back.at[c], bsem.at[c])
        part[c] = dot(select[...], back[c].reshape(512, 512), ((0,), (0,)))[64:128]

    def pair(c, d):
        return jnp.concatenate([part[c].reshape(8, 8, 512), part[d].reshape(8, 8, 512)], axis=1).astype(BF)

    fsend[:, :, 0:512] = pair(3, 1)
    fsend[:, :, 512:1024] = pair(0, 2)
    keep(fsend.at[line_me], frecv.at[line_me], rsem.at[6])

    def finish(k, carry):
        core, to = (s + k // 4) % 2, (z + k % 4) % 4
        send(fsend.at[core * 4 + to], frecv.at[line_me], ssem.at[6], rsem.at[6], core, yx, to)
        return carry

    lax.fori_loop(1, 8, finish, 0)
    wait(frecv, rsem.at[6])

    for j in range(14):
        at = slice(j * 512, (j + 1) * 512)
        stream = gathered[s, :, at].astype(F32)
        mine = jnp.zeros((8, 512), F32)
        for t in range(4):
            mine = jnp.where(z == t, stream[t * 8 : t * 8 + 8], mine)
        if j < 8:
            moe = frecv[(j % 2) * 4 + j // 2, :, 0:512].astype(F32)[0:8]
        else:
            core, c = (j - 8) // 3, (j - 8) % 3
            moe = jnp.zeros((8, 512), F32)
            for t in range(4):
                piece = frecv[core * 4 + t, :, (0 if c == 1 else 512) : (512 if c == 1 else 1024)].astype(F32)
                moe = moe + (piece[0:8] if c == 0 else piece[8:16])
        attended[:, at] = mine.astype(BF)
        layer_out[:, at] = (mine + moe).astype(BF)

    for ref, number in (
        (route.at[pl.ds(0, 7)], 0),
        (picked.at[0, pl.ds(0, 31)], 1),
        (picked.at[pl.ds(1, 3), pl.ds(0, 31)], 2),
        (rows.at[:, pl.ds(0, 3072)], 3),
        (ysend.at[pl.ds(0, 3)], 4),
        (back.at[:, pl.ds(0, 31)], 5),
        (fsend.at[pl.ds(0, 7)], 6),
    ):
        wait(ref, ssem.at[number])


def expert_scratch():
    return [
        pltpu.VMEM((7168, 256), BF),
        pltpu.VMEM((7168, 256), BF),
        pltpu.VMEM((256, 7168), BF),
        pltpu.VMEM((8, 64, 128), BF),
        pltpu.VMEM((64, 7168), BF),
        pltpu.VMEM((512, 128), BF),
        pltpu.VMEM((4, 32, 16, 512), BF),
        pltpu.VMEM((256, 7168), BF),
        pltpu.VMEM((2, 256, 256), F32),
        pltpu.VMEM((256, 256), BF),
        pltpu.VMEM((4, 256, 1024), BF),
        pltpu.VMEM((4, 256, 1024), BF),
        pltpu.VMEM((6, 256, 512), BF),
        pltpu.VMEM((2, 256, 512), BF),
        pltpu.VMEM((4, 32, 16, 512), BF),
        pltpu.VMEM((4, 64, 512), F32),
        pltpu.VMEM((8, 16, 1024), BF),
        pltpu.VMEM((8, 16, 1024), BF),
    ]


def expert_call(expert_ids, gates, replicas, gain, w_gate, w_up, w_down, gathered):
    return pl.pallas_call(
        expert_phase,
        out_shape=[jax.ShapeDtypeStruct((8, 7168), BF)] * 2,
        in_specs=[SMEM, SMEM, SMEM, VMEM, ANY, ANY, ANY, VMEM],
        out_specs=[VMEM, VMEM],
        scratch_shapes=expert_scratch() + [pltpu.SemaphoreType.DMA((n,)) for n in (3, 7, 7, 4, 4, 4)],
        compiler_params=pltpu.CompilerParams(has_side_effects=True, vmem_limit_bytes=56 * MB),
        name="experts",
    )(expert_ids, gates.astype(F32), replicas, gain[None], w_gate[0], w_up[0], w_down[0], gathered)


def local(
    queries, cache, lengths, w_uv, w_out, resid, norm_gain, expert_ids, gate_weights, replica_slot, w_gate, w_up, w_down
):
    gathered = attention_call(lengths, queries, cache, w_uv, w_out, resid)
    return tuple(
        expert_call(expert_ids, gate_weights, replica_slot, norm_gain, w_gate, w_up, w_down, gathered)
    )


def solution(mesh):
    return jax.shard_map(
        local,
        mesh=mesh,
        in_specs=(
            P(("side", "dev"), None, None),
            P(("side", "dev"), None, None),
            P(("side", "dev")),
            P(("side", "dev"), None, None),
            P(("side", "dev"), None),
            P(("side", "dev"), None),
            P(),
            P(("side", "dev"), None),
            P(("side", "dev"), None),
            P(),
            P(("side", "dev"), None, None),
            P(("side", "dev"), None, None),
            P(("side", "dev"), None, None),
        ),
        out_specs=(P(("side", "dev"), None), P(("side", "dev"), None)),
        check_vma=False,
    )
```

```python
import functools
import math

import jax
import jax.numpy as jnp
from jax import lax
from jax.experimental import pallas as pl
from jax.experimental.pallas import tpu as pltpu
from jax.sharding import PartitionSpec as P

GROUP = 4
BF = jnp.bfloat16
F32 = jnp.float32
MB = 1 << 20


def place():
    s = lax.axis_index("side")
    dev = lax.axis_index("dev")
    return s, dev // 4, dev % 4


def dot(a, b, dims=((1,), (0,))):
    return lax.dot_general(a, b, (dims, ((), ())), preferred_element_type=F32)


def around(yx, k):
    return ((yx // 4 + k // 4) % 4) * 4 + (yx % 4 + k % 4) % 4


def iota(shape, dim):
    return lax.broadcasted_iota(jnp.int32, shape, dim)


W_UV, W_OUT, RESID, UV_OVER, OUT_OVER, LATENT, VALUE, SUM, SLICE, ROWS_OVER, ROUTE, PICK, PICK_REST, GATHER, PIECE, BACK, RESULT, SUM_ON = range(18)
PARTS = (1, 4, 1, 1, 1, 1, 4, 4, 2, 2, 1, 2, 1, 8, 4, 4, 1, 4)
FIRST = tuple(sum(PARTS[:i]) for i in range(len(PARTS)))


def kernel(
    lengths, expert_ids, gates, replicas,
    queries, cache, w_uv, w_out, resid, gain, w_gate, w_up, w_down,
    both,
    cbuf, late, lrecv, wuv, wo, vals, osend, orecv, tsend, trecv, rsend, rrecv, gathered,
    wg, wu, wd, route, normed, select, picked, rest, rows, acc, hidden, ysend, yrecv, bsend, asend, back, part, fsend, frecv,
    csem, ssem, rsem,
):
    def send(src, dst, kind, number, s, yx, z):
        pltpu.make_async_remote_copy(
            src_ref=src,
            dst_ref=dst,
            send_sem=ssem.at[kind],
            recv_sem=rsem.at[FIRST[kind] + number],
            device_id=(s, yx * 4 + z),
            device_id_type=pl.DeviceIdType.MESH,
        ).start()

    def keep(src, dst, kind, number):
        pltpu.make_async_copy(src, dst, rsem.at[FIRST[kind] + number]).start()

    def wait(ref, kind, number):
        pltpu.make_async_copy(ref, ref, rsem.at[FIRST[kind] + number]).wait()

    def sent(ref, kind):
        pltpu.make_async_copy(ref, ref, ssem.at[kind]).wait()

    s, yx, z = place()
    y, x = yx // 4, yx % 4

    barrier = pltpu.get_barrier_semaphore()

    def greet(core, chip, level):
        pl.semaphore_signal(
            barrier, inc=1, device_id=(core, chip * 4 + level), device_id_type=pl.DeviceIdType.MESH
        )

    def greet_plane(k, carry):
        greet((s + k % 2) % 2, around(yx, k // 2), z)
        return carry

    def greet_line(k, carry):
        greet((s + k // 4) % 2, yx, (z + k % 4) % 4)
        return carry

    lax.fori_loop(1, 4, greet_line, 0)
    lax.fori_loop(5, 8, greet_line, 0)
    lax.fori_loop(1, 32, greet_plane, 0)

    for r in range(8):
        pltpu.make_async_copy(cache.at[r], cbuf.at[r], csem.at[r]).start()
    own_col = pl.multiple_of((s * 4 + z) * 128, 128)
    here = pl.ds(pl.multiple_of(z * 1792, 256), 1792)
    for q in range(4):
        rsend[q] = resid[:, q * 1792 : (q + 1) * 1792].astype(F32)
    pl.semaphore_wait(barrier, 37)

    keep(w_uv, wuv.at[:, pl.ds(own_col, 128)], W_UV, 0)
    keep(w_out.at[:, here], wo.at[pl.ds(own_col, 128)], W_OUT, z)
    for k in (1, 3, 2):
        send(w_uv, wuv.at[:, pl.ds(own_col, 128)], W_UV, 0, s, yx, (z + k) % 4)
    for k in (1, 3, 2):
        t = (z + k) % 4
        there = pl.ds(pl.multiple_of(t * 1792, 256), 1792)
        send(w_out.at[:, there], wo.at[pl.ds(own_col, 128)], W_OUT, z, s, yx, t)
    send(w_uv, wuv.at[:, pl.ds(own_col, 128)], UV_OVER, 0, 1 - s, yx, z)
    send(w_out.at[:, here], wo.at[pl.ds(own_col, 128)], OUT_OVER, 0, 1 - s, yx, z)
    keep(rsend.at[z], rrecv.at[z], RESID, 0)
    for k in (1, 3, 2):
        t = (z + k) % 4
        send(rsend.at[t], rrecv.at[z], RESID, 0, s, yx, t)

    row, col = iota((128, 128), 0), iota((128, 128), 1)
    head = ((row % 8) // 4) * 64 + (row // 8) * 4 + row % 4
    order = jnp.where(col == head, 1.0, 0.0).astype(BF)
    scale = 1.0 / math.sqrt(192)
    column = iota((128, 512), 1)

    def one(r):
        pltpu.make_async_copy(cache.at[r], cbuf.at[r], csem.at[r]).wait()
        q = dot(order, queries[r], ((1,), (1,))).astype(BF)
        scores = dot(q, cbuf[r]) * scale
        scores = jnp.where(column < lengths[r], scores, -1e30)
        weight = jnp.exp(scores - jnp.max(scores, axis=1, keepdims=True))
        total = jnp.sum(weight, axis=1, keepdims=True)
        latent = dot(weight.astype(BF), cbuf[r, 0:512], ((1,), (1,)))
        return (latent / total).reshape(16, 8, 512)

    def step(i, carry):
        late[i] = jnp.concatenate([one(2 * i), one(2 * i + 1)], axis=1).astype(BF)
        keep(late.at[i, yx], lrecv.at[yx, i], LATENT, 0)

        def out(k, carry):
            to = around(yx, k)
            send(late.at[i, to], lrecv.at[yx, i], LATENT, 0, s, to, z)
            return carry

        return lax.fori_loop(1, 16, out, carry)

    lax.fori_loop(0, 4, step, 0)

    pltpu.make_async_copy(w_gate, wg, csem.at[8]).start()
    pltpu.make_async_copy(w_up, wu, csem.at[9]).start()
    pltpu.make_async_copy(w_down, wd, csem.at[10]).start()
    slot_me = s * 16 + yx
    line_me = s * 4 + z

    half = pl.ds(pl.multiple_of(s * 512, 512), 512)
    wait(wuv.at[:, half], W_UV, 0)
    for k in (1, 3, 2):
        at = pl.ds(pl.multiple_of((s * 4 + (z + k) % 4) * 128, 128), 128)
        send(wuv.at[:, at], wuv.at[:, at], UV_OVER, 0, 1 - s, yx, z)

    row, lane = iota((64, 128), 0), iota((64, 128), 1)

    def choice(p, carry):
        table, used = carry
        t, k = p // 4, p % 4
        slot = replicas[(t + k) % 2, expert_ids[k, t]]
        same = row // 2 == slot
        hit = same & (row % 2 == used)
        table = jnp.where(hit & (lane == line_me * 8 + t), 1.0, table)
        table = jnp.where(hit & (lane == 64 + line_me * 8 + t), gates[k, t], table)
        return table, used + jnp.where(same, 1, 0)

    table, _ = lax.fori_loop(0, 32, choice, (jnp.zeros((64, 128), F32), jnp.zeros((64, 128), jnp.int32)))
    route[line_me] = table.astype(BF)

    def announce(k, carry):
        send(route.at[line_me], route.at[line_me], ROUTE, 0, (s + k // 4) % 2, yx, (z + k % 4) % 4)
        return carry

    lax.fori_loop(1, 8, announce, 0)
    wait(wuv.at[:, half], UV_OVER, 0)
    wait(lrecv, LATENT, 0)

    mine = iota((256, 1024), 0) % 8 == iota((256, 1024), 1) // 128
    pick = jnp.where(iota((32, 256), 1) // 8 == iota((32, 256), 0), 1.0, 0.0).astype(BF)

    def value(j, carry):
        some = lrecv[pl.ds(j * 4, 4)].reshape(256, 512)
        full = dot(some, wuv[...])
        own = jnp.where(mine, full, 0.0).astype(BF)
        vals[z, j] = dot(pick, own).astype(BF)
        for k in (1, 3, 2):
            send(vals.at[z, j], vals.at[z, j], VALUE, z, s, yx, (z + k) % 4)
        return carry

    lax.fori_loop(0, 4, value, 0)

    for k in (1, 3, 2, 0):
        t = (z + k) % 4
        at = pl.ds(pl.multiple_of((s * 4 + t) * 128, 128), 128)
        wait(wo.at[at], W_OUT, t)
        if k:
            send(wo.at[at], wo.at[at], OUT_OVER, 0, 1 - s, yx, z)

    wait(route.at[pl.ds(0, 7)], ROUTE, 0)
    a, b = iota((512, 512), 0), iota((512, 512), 1)
    deal = jnp.where(b == ((a % 16) // 2) * 64 + (a // 16) * 2 + a % 2, 1.0, 0.0).astype(BF)
    select[...] = dot(deal, route[...].reshape(512, 128)).astype(BF)
    wait(wo.at[half], OUT_OVER, 0)

    def of(ref, t, along):
        return ref.at[:, t, :, 0:896] if along == 0 else ref.at[t, :, :, 896:1792]

    def chip(t, along):
        return y * 4 + t if along == 0 else t * 4 + x

    place_on = (x, y)
    for pp in range(2):
        p = (z // 2 + pp) % 2
        for e in range(2):
            @pl.when(2 * p + e != z)
            def _():
                wait(vals.at[2 * p + e], VALUE, 2 * p + e)

        def project(c, carry):
            at = pl.ds(pl.multiple_of(c * 256, 256), 256)
            got = dot(vals[pl.ds(2 * p, 2)].reshape(256, 1024), wo[:, at]).reshape(2, 16, 8, 256)
            osend[p, :, :, :, at] = jnp.concatenate([got[0], got[1]], axis=1).astype(BF).reshape(4, 4, 16, 256)
            return carry

        lax.fori_loop(0, 7, project, 0)
        for along in range(2):
            at = place_on[along]
            keep(of(osend.at[p], at, along), orecv.at[p, along, at], SUM, 2 * p + along)
            for k in (1, 3, 2):
                t = (at + k) % 4
                send(of(osend.at[p], t, along), orecv.at[p, along, at], SUM, 2 * p + along, s, chip(t, along), z)

    for pp in range(2):
        p = (z // 2 + pp) % 2
        for along in range(2):
            wait(orecv.at[p, along], SUM, 2 * p + along)
            got = [orecv[p, along, i].astype(F32) for i in range(4)]
            tsend[p, along] = ((got[0] + got[1]) + (got[2] + got[3])).astype(BF)
            at = place_on[1 - along]
            keep(tsend.at[p, along, at], trecv.at[p, along, at], SUM_ON, 2 * p + along)
            for k in (1, 3, 2):
                t = (at + k) % 4
                send(
                    tsend.at[p, along, t], trecv.at[p, along, at],
                    SUM_ON, 2 * p + along, s, chip(t, 1 - along), z,
                )

    wait(rrecv, RESID, 0)
    for pp in range(2):
        p = (z // 2 + pp) % 2
        line = pl.ds(pl.multiple_of(p * 16, 16), 16)
        for along in range(2):
            wait(trecv.at[p, along], SUM_ON, 2 * p + along)
            got = [trecv[p, along, i].astype(F32) for i in range(4)]
            cols = slice(along * 896, along * 896 + 896)
            base = jnp.concatenate([rrecv[2 * p, :, cols], rrecv[2 * p + 1, :, cols]], axis=0)
            total = base + ((got[0] + got[1]) + (got[2] + got[3]))
            gathered[s, line, pl.ds(pl.multiple_of(z * 1792 + along * 896, 128), 896)] = total.astype(BF)
        for k in (1, 3, 2):
            send(gathered.at[s, line, here], gathered.at[s, line, here], SLICE, p, s, yx, (z + k) % 4)

    def norm(core, p):
        stream = gathered[core, pl.ds(pl.multiple_of(p * 16, 16), 16)].astype(F32)
        mean = jnp.mean(stream * stream, axis=1, keepdims=True)
        at = pl.ds(pl.multiple_of(core * 32 + p * 16, 16), 16)
        normed[at] = (stream * lax.rsqrt(mean + 1e-06) * gain[...]).astype(BF)

    for pp in range(2):
        p = (z // 2 + pp) % 2
        line = pl.ds(pl.multiple_of(p * 16, 16), 16)
        wait(gathered.at[s, line, pl.ds(0, 5376)], SLICE, p)
        send(gathered.at[s, line], gathered.at[s, line], ROWS_OVER, p, 1 - s, yx, z)
        norm(s, p)
    for pp in range(2):
        p = (z // 2 + pp) % 2
        wait(gathered.at[s, pl.ds(0, 16)], ROWS_OVER, p)
        norm(1 - s, p)

    land = pl.ds(pl.multiple_of(yx * 16, 16), 16)

    def deliver(source, cols, kind, number):
        keep(source.at[slot_me], rows.at[land, cols], kind, number)

        def out(k, carry):
            to, core = around(yx, k // 2), (s + k % 2) % 2
            send(source.at[core * 16 + to], rows.at[land, cols], kind, number, core, to, z)
            return carry

        lax.fori_loop(1, 32, out, 0)

    def deliver_slice(c):
        cols = pl.ds(pl.multiple_of(z * 1024 + c * 512 + s * 256, 256), 256)
        picked[c] = dot(select[:, 0:64], normed[:, cols]).astype(BF).reshape(32, 16, 256)
        deliver(picked.at[c], cols, PICK, c)

    def deliver_rest(c):
        cols = pl.ds(pl.multiple_of(4096 + s * 1536 + c * 512, 512), 512)
        rest[c] = dot(select[:, 0:64], normed[:, cols]).astype(BF).reshape(32, 16, 512)
        deliver(rest.at[c], cols, PICK_REST, 0)

    def spread(c):
        cols = pl.ds(pl.multiple_of(z * 1024 + c * 512, 512), 512)
        wait(rows.at[:, cols], PICK, c)
        for k in (1, 3, 2):
            send(rows.at[:, cols], rows.at[:, cols], GATHER, c * 4 + z, s, yx, (z + k) % 4)

    deliver_slice(0)
    deliver_slice(1)
    deliver_rest(0)
    spread(0)
    deliver_rest(1)
    spread(1)
    deliver_rest(2)

    pltpu.make_async_copy(w_gate, wg, csem.at[8]).wait()
    pltpu.make_async_copy(w_up, wu, csem.at[9]).wait()
    acc[...] = jnp.zeros_like(acc)

    def enter(c, carry):
        at = pl.ds(pl.multiple_of(c * 512, 512), 512)
        acc[0] += dot(rows[:, at], wg[at])
        acc[1] += dot(rows[:, at], wu[at])
        return carry

    lax.fori_loop(2 * z, 2 * z + 2, enter, 0)
    for c in range(2):
        for k in (1, 3, 2):
            t = (z + k) % 4
            wait(rows.at[:, pl.ds(pl.multiple_of(t * 1024 + c * 512, 512), 512)], GATHER, c * 4 + t)
            enter(2 * t + c, 0)
    wait(rows.at[:, pl.ds(4096, 3072)], PICK_REST, 0)
    lax.fori_loop(8, 14, enter, 0)
    gate = acc[0]
    hidden[...] = (gate * jax.nn.sigmoid(gate) * acc[1]).astype(BF)
    pltpu.make_async_copy(w_down, wd, csem.at[10]).wait()

    for k in (1, 3, 2, 0):
        t = (z + k) % 4
        got = dot(hidden[...], wd[:, pl.ds(pl.multiple_of(t * 1024, 1024), 1024)]).astype(BF)
        if k == 0:
            yrecv[z] = got
        else:
            ysend[t] = got
    for j in range(4):
        some = pl.ds(pl.multiple_of(((y + j) % 4) * 64, 64), 64)
        for k in (1, 3, 2):
            t = (z + k) % 4
            send(ysend.at[t, some], yrecv.at[z, some], PIECE, (y + j) % 4, s, yx, t)

    def give(source, core, to, c):
        src = source.at[pl.ds(pl.multiple_of(to * 16, 16), 16)]
        send(src, back.at[c, slot_me], BACK, c, core, to, z)

    def give_own(source, core, c):
        @pl.when(core == s)
        def _():
            keep(source.at[land], back.at[c, slot_me], BACK, c)

        @pl.when(core != s)
        def _():
            give(source, core, yx, c)

    for c in range(3):
        for core in range(2):
            j = core * 3 + c
            bsend[j] = dot(hidden[...], wd[:, 4096 + j * 512 : 4608 + j * 512]).astype(BF)
            give_own(bsend.at[j], core, c)

            def out(k, carry):
                give(bsend.at[j], core, around(yx, k), c)
                return carry

            lax.fori_loop(1, 16, out, 0)

    for j in range(4):
        to_y = (y + j) % 4
        some = pl.ds(pl.multiple_of(to_y * 64, 64), 64)
        wait(yrecv.at[pl.ds(0, 3), some], PIECE, to_y)
        got = [yrecv[q, some].astype(F32) for q in range(4)]
        total = ((got[0] + got[1]) + (got[2] + got[3])).astype(BF)
        for core in range(2):
            asend[core, some] = total[:, core * 512 : core * 512 + 512]
            if j == 0:
                give_own(asend.at[core], core, 3)
            for k in range(1 if j == 0 else 0, 4):
                give(asend.at[core], core, to_y * 4 + (x + k) % 4, 3)

    for c in range(4):
        wait(back.at[c], BACK, c)
        part[c] = dot(select[...], back[c].reshape(512, 512), ((0,), (0,)))[64:128]

    def pair(c, d):
        return jnp.concatenate([part[c].reshape(8, 8, 512), part[d].reshape(8, 8, 512)], axis=1).astype(BF)

    fsend[:, :, 0:512] = pair(3, 1)
    fsend[:, :, 512:1024] = pair(0, 2)
    keep(fsend.at[line_me], frecv.at[line_me], RESULT, 0)

    def finish(k, carry):
        core, to = (s + k // 4) % 2, (z + k % 4) % 4
        send(fsend.at[core * 4 + to], frecv.at[line_me], RESULT, 0, core, yx, to)
        return carry

    lax.fori_loop(1, 8, finish, 0)
    wait(frecv, RESULT, 0)

    for j in range(14):
        at = slice(j * 512, (j + 1) * 512)
        stream = gathered[s, :, at].astype(F32)
        own = jnp.zeros((8, 512), F32)
        for t in range(4):
            own = jnp.where(z == t, stream[t * 8 : t * 8 + 8], own)
        if j < 8:
            moe = frecv[(j % 2) * 4 + j // 2, :, 0:512].astype(F32)[0:8]
        else:
            core, c = (j - 8) // 3, (j - 8) % 3
            moe = jnp.zeros((8, 512), F32)
            for t in range(4):
                piece = frecv[core * 4 + t, :, (0 if c == 1 else 512) : (512 if c == 1 else 1024)].astype(F32)
                moe = moe + (piece[0:8] if c == 0 else piece[8:16])
        both[0, :, at] = own.astype(BF)
        both[1, :, at] = (own + moe).astype(BF)

    for ref, kind in (
        (wuv.at[:, pl.ds(0, 384)], W_UV),
        (wo.at[pl.ds(0, 384)], W_OUT),
        (rsend.at[pl.ds(0, 3)], RESID),
        (wuv.at[:, half], UV_OVER),
        (wo.at[half], OUT_OVER),
        (late.at[:, pl.ds(0, 15)], LATENT),
        (vals.at[pl.ds(0, 3)], VALUE),
        (orecv.at[:, :, pl.ds(0, 3)], SUM),
        (tsend.at[:, :, pl.ds(0, 3)], SUM_ON),
        (gathered.at[s, :, pl.ds(0, 5376)], SLICE),
        (gathered.at[s], ROWS_OVER),
        (route.at[pl.ds(0, 7)], ROUTE),
        (picked.at[:, pl.ds(0, 31)], PICK),
        (rest.at[:, pl.ds(0, 31)], PICK_REST),
        (rows.at[:, pl.ds(0, 3072)], GATHER),
        (ysend.at[pl.ds(0, 3)], PIECE),
        (back.at[:, pl.ds(0, 31)], BACK),
        (fsend.at[pl.ds(0, 7)], RESULT),
    ):
        sent(ref, kind)


VMEM = pl.BlockSpec(memory_space=pltpu.VMEM)
SMEM = pl.BlockSpec(memory_space=pltpu.SMEM)
ANY = pl.BlockSpec(memory_space=pl.ANY)


def local(
    queries, cache, lengths, w_uv, w_out, resid, norm_gain, expert_ids, gate_weights, replica_slot, w_gate, w_up, w_down
):
    scratch = [
        pltpu.VMEM((8, 576, 512), BF),
        pltpu.VMEM((4, 16, 16, 512), BF),
        pltpu.VMEM((16, 4, 16, 512), BF),
        pltpu.VMEM((512, 1024), BF),
        pltpu.VMEM((1024, 1792), BF),
        pltpu.VMEM((4, 4, 32, 1024), BF),
        pltpu.VMEM((2, 4, 4, 16, 1792), BF),
        pltpu.VMEM((2, 2, 4, 4, 16, 896), BF),
        pltpu.VMEM((2, 2, 4, 16, 896), BF),
        pltpu.VMEM((2, 2, 4, 16, 896), BF),
        pltpu.VMEM((4, 8, 1792), F32),
        pltpu.VMEM((4, 8, 1792), F32),
        pltpu.VMEM((2, 32, 7168), BF),
        pltpu.VMEM((7168, 256), BF),
        pltpu.VMEM((7168, 256), BF),
        pltpu.VMEM((256, 7168), BF),
        pltpu.VMEM((8, 64, 128), BF),
        pltpu.VMEM((64, 7168), BF),
        pltpu.VMEM((512, 128), BF),
        pltpu.VMEM((2, 32, 16, 256), BF),
        pltpu.VMEM((3, 32, 16, 512), BF),
        pltpu.VMEM((256, 7168), BF),
        pltpu.VMEM((2, 256, 256), F32),
        pltpu.VMEM((256, 256), BF),
        pltpu.VMEM((4, 256, 1024), BF),
        pltpu.VMEM((4, 256, 1024), BF),
        pltpu.VMEM((6, 256, 512), BF),
        pltpu.VMEM((2, 256, 512), BF),
        pltpu.VMEM((4, 32, 16, 512), BF),
        pltpu.VMEM((4, 64, 512), F32),
        pltpu.VMEM((8, 16, 1024), BF),
        pltpu.VMEM((8, 16, 1024), BF),
    ] + [pltpu.SemaphoreType.DMA((n,)) for n in (11, len(PARTS), sum(PARTS))]
    both = pl.pallas_call(
        kernel,
        out_shape=jax.ShapeDtypeStruct((2, 8, 7168), BF),
        in_specs=[SMEM] * 4 + [VMEM, ANY, ANY, ANY, VMEM, VMEM, ANY, ANY, ANY],
        out_specs=VMEM,
        scratch_shapes=scratch,
        compiler_params=pltpu.CompilerParams(collective_id=0, has_side_effects=True, vmem_limit_bytes=60 * MB),
        name="layer",
    )(
        lengths,
        expert_ids.T,
        gate_weights.T.astype(F32),
        replica_slot.T,
        jnp.swapaxes(queries, 1, 2),
        jnp.swapaxes(cache, 1, 2),
        w_uv[0],
        w_out,
        resid,
        norm_gain[None],
        w_gate[0],
        w_up[0],
        w_down[0],
    )
    return both[0], both[1]


def solution(mesh):
    return jax.shard_map(
        local,
        mesh=mesh,
        in_specs=(
            P(("side", "dev"), None, None),
            P(("side", "dev"), None, None),
            P(("side", "dev")),
            P(("side", "dev"), None, None),
            P(("side", "dev"), None),
            P(("side", "dev"), None),
            P(),
            P(("side", "dev"), None),
            P(("side", "dev"), None),
            P(),
            P(("side", "dev"), None, None),
            P(("side", "dev"), None, None),
            P(("side", "dev"), None, None),
        ),
        out_specs=(P(("side", "dev"), None), P(("side", "dev"), None)),
        check_vma=False,
    )
```

```python
import functools
import math

import jax
import jax.numpy as jnp
from jax import lax
from jax.experimental import pallas as pl
from jax.experimental.pallas import tpu as pltpu
from jax.sharding import PartitionSpec as P

GROUP = 4
BF = jnp.bfloat16
F32 = jnp.float32
MB = 1 << 20


def place():
    s = lax.axis_index("side")
    dev = lax.axis_index("dev")
    return s, dev // 4, dev % 4


def dot(a, b, dims=((1,), (0,))):
    return lax.dot_general(a, b, (dims, ((), ())), preferred_element_type=F32)


def around(yx, k):
    return ((yx // 4 + k // 4) % 4) * 4 + (yx % 4 + k % 4) % 4


def iota(shape, dim):
    return lax.broadcasted_iota(jnp.int32, shape, dim)


W_UV, W_OUT, RESID, UV_OVER, OUT_OVER, LATENT, VALUE, SUM, SLICE, ROWS_OVER, ROUTE, PICK, PICK_REST, GATHER, PIECE, BACK, RESULT, SUM_ON, TABLE, LINES, HOME, HOME_ON = range(22)
PARTS = (1, 4, 1, 1, 1, 1, 4, 4, 2, 2, 1, 2, 4, 8, 4, 1, 1, 4, 2, 4, 4, 4)
FIRST = tuple(sum(PARTS[:i]) for i in range(len(PARTS)))


def kernel(
    lengths, expert_ids, gates, replicas,
    queries, cache, w_uv, w_out, resid, gain, w_gate, w_up, w_down,
    both,
    cbuf, late, lrecv, wuv, wo, vals, osend, orecv, tsend, trecv, rsend, rrecv, gathered,
    wg, wu, wd, route, normed, select, tables, picked, picked_on, lines, rest, rows, acc, hidden,
    ysend, yrecv, bsend, brecv, tsend_home, trecv_home, asend, back, fsend, frecv,
    csem, ssem, rsem,
):
    def send(src, dst, kind, number, s, yx, z):
        pltpu.make_async_remote_copy(
            src_ref=src,
            dst_ref=dst,
            send_sem=ssem.at[kind],
            recv_sem=rsem.at[FIRST[kind] + number],
            device_id=(s, yx * 4 + z),
            device_id_type=pl.DeviceIdType.MESH,
        ).start()

    def keep(src, dst, kind, number):
        pltpu.make_async_copy(src, dst, rsem.at[FIRST[kind] + number]).start()

    def wait(ref, kind, number):
        pltpu.make_async_copy(ref, ref, rsem.at[FIRST[kind] + number]).wait()

    def sent(ref, kind):
        pltpu.make_async_copy(ref, ref, ssem.at[kind]).wait()

    s, yx, z = place()
    y, x = yx // 4, yx % 4

    barrier = pltpu.get_barrier_semaphore()

    def greet(core, chip, level):
        pl.semaphore_signal(
            barrier, inc=1, device_id=(core, chip * 4 + level), device_id_type=pl.DeviceIdType.MESH
        )

    def greet_plane(k, carry):
        greet((s + k % 2) % 2, around(yx, k // 2), z)
        return carry

    def greet_line(k, carry):
        greet((s + k // 4) % 2, yx, (z + k % 4) % 4)
        return carry

    lax.fori_loop(1, 4, greet_line, 0)
    lax.fori_loop(5, 8, greet_line, 0)
    lax.fori_loop(1, 32, greet_plane, 0)

    for r in range(8):
        pltpu.make_async_copy(cache.at[r], cbuf.at[r], csem.at[r]).start()
    own_col = pl.multiple_of((s * 4 + z) * 128, 128)
    here = pl.ds(pl.multiple_of(z * 1792, 256), 1792)
    for q in range(4):
        rsend[q] = resid[:, q * 1792 : (q + 1) * 1792].astype(F32)
    pl.semaphore_wait(barrier, 37)

    keep(w_uv, wuv.at[:, pl.ds(own_col, 128)], W_UV, 0)
    keep(w_out.at[:, here], wo.at[pl.ds(own_col, 128)], W_OUT, z)
    for k in (1, 3, 2):
        send(w_uv, wuv.at[:, pl.ds(own_col, 128)], W_UV, 0, s, yx, (z + k) % 4)
    for k in (1, 3, 2):
        t = (z + k) % 4
        there = pl.ds(pl.multiple_of(t * 1792, 256), 1792)
        send(w_out.at[:, there], wo.at[pl.ds(own_col, 128)], W_OUT, z, s, yx, t)
    send(w_uv, wuv.at[:, pl.ds(own_col, 128)], UV_OVER, 0, 1 - s, yx, z)
    send(w_out.at[:, here], wo.at[pl.ds(own_col, 128)], OUT_OVER, 0, 1 - s, yx, z)
    keep(rsend.at[z], rrecv.at[z], RESID, 0)
    for k in (1, 3, 2):
        t = (z + k) % 4
        send(rsend.at[t], rrecv.at[z], RESID, 0, s, yx, t)

    row, col = iota((128, 128), 0), iota((128, 128), 1)
    head = ((row % 8) // 4) * 64 + (row // 8) * 4 + row % 4
    order = jnp.where(col == head, 1.0, 0.0).astype(BF)
    scale = 1.0 / math.sqrt(192)
    column = iota((128, 512), 1)

    def one(r):
        pltpu.make_async_copy(cache.at[r], cbuf.at[r], csem.at[r]).wait()
        q = dot(order, queries[r], ((1,), (1,))).astype(BF)
        scores = dot(q, cbuf[r]) * scale
        scores = jnp.where(column < lengths[r], scores, -1e30)
        weight = jnp.exp(scores - jnp.max(scores, axis=1, keepdims=True))
        total = jnp.sum(weight, axis=1, keepdims=True)
        latent = dot(weight.astype(BF), cbuf[r, 0:512], ((1,), (1,)))
        return (latent / total).reshape(16, 8, 512)

    def step(i, carry):
        late[i] = jnp.concatenate([one(2 * i), one(2 * i + 1)], axis=1).astype(BF)
        keep(late.at[i, yx], lrecv.at[yx, i], LATENT, 0)

        def out(k, carry):
            to = around(yx, k)
            send(late.at[i, to], lrecv.at[yx, i], LATENT, 0, s, to, z)
            return carry

        return lax.fori_loop(1, 16, out, carry)

    lax.fori_loop(0, 4, step, 0)

    pltpu.make_async_copy(w_gate, wg, csem.at[8]).start()
    pltpu.make_async_copy(w_up, wu, csem.at[9]).start()
    pltpu.make_async_copy(w_down, wd, csem.at[10]).start()
    slot_me = s * 16 + yx
    line_me = s * 4 + z

    half = pl.ds(pl.multiple_of(s * 512, 512), 512)
    wait(wuv.at[:, half], W_UV, 0)
    for k in (1, 3, 2):
        at = pl.ds(pl.multiple_of((s * 4 + (z + k) % 4) * 128, 128), 128)
        send(wuv.at[:, at], wuv.at[:, at], UV_OVER, 0, 1 - s, yx, z)

    row, lane = iota((64, 128), 0), iota((64, 128), 1)

    def choice(p, carry):
        table, used = carry
        t, k = p // 4, p % 4
        slot = replicas[(t + k) % 2, expert_ids[k, t]]
        same = row // 2 == slot
        hit = same & (row % 2 == used)
        table = jnp.where(hit & (lane == line_me * 8 + t), 1.0, table)
        table = jnp.where(hit & (lane == 64 + line_me * 8 + t), gates[k, t], table)
        return table, used + jnp.where(same, 1, 0)

    table, _ = lax.fori_loop(0, 32, choice, (jnp.zeros((64, 128), F32), jnp.zeros((64, 128), jnp.int32)))
    route[line_me] = table.astype(BF)

    def announce(k, carry):
        send(route.at[line_me], route.at[line_me], ROUTE, 0, (s + k // 4) % 2, yx, (z + k % 4) % 4)
        return carry

    lax.fori_loop(1, 8, announce, 0)
    wait(wuv.at[:, half], UV_OVER, 0)
    wait(lrecv, LATENT, 0)

    mine = iota((256, 1024), 0) % 8 == iota((256, 1024), 1) // 128
    pick = jnp.where(iota((32, 256), 1) // 8 == iota((32, 256), 0), 1.0, 0.0).astype(BF)

    def value(j, carry):
        some = lrecv[pl.ds(j * 4, 4)].reshape(256, 512)
        full = dot(some, wuv[...])
        own = jnp.where(mine, full, 0.0).astype(BF)
        vals[z, j] = dot(pick, own).astype(BF)
        for k in (1, 3, 2):
            send(vals.at[z, j], vals.at[z, j], VALUE, z, s, yx, (z + k) % 4)
        return carry

    lax.fori_loop(0, 4, value, 0)

    for k in (1, 3, 2, 0):
        t = (z + k) % 4
        at = pl.ds(pl.multiple_of((s * 4 + t) * 128, 128), 128)
        wait(wo.at[at], W_OUT, t)
        if k:
            send(wo.at[at], wo.at[at], OUT_OVER, 0, 1 - s, yx, z)

    wait(route.at[pl.ds(0, 7)], ROUTE, 0)
    a, b = iota((512, 512), 0), iota((512, 512), 1)
    deal = jnp.where(b == ((a % 16) // 2) * 64 + (a // 16) * 2 + a % 2, 1.0, 0.0).astype(BF)
    select[...] = dot(deal, route[...].reshape(512, 128)).astype(BF).reshape(2, 4, 4, 16, 128)
    for along in range(2):
        at = (x, y)[along]

        def column(t):
            return select.at[:, :, t] if along == 0 else select.at[:, t]

        keep(column(at), tables.at[along, at], TABLE, along)
        for k in (1, 3, 2):
            t = (at + k) % 4
            to = y * 4 + t if along == 0 else t * 4 + x
            send(column(t), tables.at[along, at], TABLE, along, s, to, z)
    wait(wo.at[half], OUT_OVER, 0)

    def of(ref, t, along):
        return ref.at[:, t, :, 0:896] if along == 0 else ref.at[t, :, :, 896:1792]

    def chip(t, along):
        return y * 4 + t if along == 0 else t * 4 + x

    place_on = (x, y)
    for pp in range(2):
        p = (z // 2 + pp) % 2
        for e in range(2):
            @pl.when(2 * p + e != z)
            def _():
                wait(vals.at[2 * p + e], VALUE, 2 * p + e)

        def project(c, carry):
            at = pl.ds(pl.multiple_of(c * 256, 256), 256)
            got = dot(vals[pl.ds(2 * p, 2)].reshape(256, 1024), wo[:, at]).reshape(2, 16, 8, 256)
            osend[p, :, :, :, at] = jnp.concatenate([got[0], got[1]], axis=1).astype(BF).reshape(4, 4, 16, 256)
            return carry

        lax.fori_loop(0, 7, project, 0)
        for along in range(2):
            at = place_on[along]
            keep(of(osend.at[p], at, along), orecv.at[p, along, at], SUM, 2 * p + along)
            for k in (1, 3, 2):
                t = (at + k) % 4
                send(of(osend.at[p], t, along), orecv.at[p, along, at], SUM, 2 * p + along, s, chip(t, along), z)

    for pp in range(2):
        p = (z // 2 + pp) % 2
        for along in range(2):
            wait(orecv.at[p, along], SUM, 2 * p + along)
            got = [orecv[p, along, i].astype(F32) for i in range(4)]
            tsend[p, along] = ((got[0] + got[1]) + (got[2] + got[3])).astype(BF)
            at = place_on[1 - along]
            keep(tsend.at[p, along, at], trecv.at[p, along, at], SUM_ON, 2 * p + along)
            for k in (1, 3, 2):
                t = (at + k) % 4
                send(
                    tsend.at[p, along, t], trecv.at[p, along, at],
                    SUM_ON, 2 * p + along, s, chip(t, 1 - along), z,
                )

    wait(rrecv, RESID, 0)
    for pp in range(2):
        p = (z // 2 + pp) % 2
        line = pl.ds(pl.multiple_of(p * 16, 16), 16)
        for along in range(2):
            wait(trecv.at[p, along], SUM_ON, 2 * p + along)
            got = [trecv[p, along, i].astype(F32) for i in range(4)]
            cols = slice(along * 896, along * 896 + 896)
            base = jnp.concatenate([rrecv[2 * p, :, cols], rrecv[2 * p + 1, :, cols]], axis=0)
            total = base + ((got[0] + got[1]) + (got[2] + got[3]))
            gathered[s, line, pl.ds(pl.multiple_of(z * 1792 + along * 896, 128), 896)] = total.astype(BF)
        for k in (1, 3, 2):
            send(gathered.at[s, line, here], gathered.at[s, line, here], SLICE, p, s, yx, (z + k) % 4)

    def norm(core, p):
        stream = gathered[core, pl.ds(pl.multiple_of(p * 16, 16), 16)].astype(F32)
        mean = jnp.mean(stream * stream, axis=1, keepdims=True)
        at = pl.ds(pl.multiple_of(core * 32 + p * 16, 16), 16)
        normed[at] = (stream * lax.rsqrt(mean + 1e-06) * gain[...]).astype(BF)

    for pp in range(2):
        p = (z // 2 + pp) % 2
        line = pl.ds(pl.multiple_of(p * 16, 16), 16)
        wait(gathered.at[s, line, pl.ds(0, 5376)], SLICE, p)
        send(gathered.at[s, line], gathered.at[s, line], ROWS_OVER, p, 1 - s, yx, z)
        norm(s, p)
    for pp in range(2):
        p = (z // 2 + pp) % 2
        wait(gathered.at[s, pl.ds(0, 16)], ROWS_OVER, p)
        norm(1 - s, p)

    land = pl.ds(pl.multiple_of(yx * 16, 16), 16)
    flat = select[...].reshape(512, 128)[:, 0:64]

    def slice_cols(t, c, core):
        start, width = ((0, 128), (256, 256))[c]
        return pl.ds(pl.multiple_of(t * 768 + start + core * width, 128), width)

    def whole_cols(t, c):
        start, width = ((0, 256), (256, 512))[c]
        return pl.ds(pl.multiple_of(t * 768 + start, 256), width)

    def rest_cols(core, along, c):
        return pl.ds(pl.multiple_of(3072 + core * 2048 + along * 1024 + c * 512, 512), 512)

    def deliver_slice(c, buffer):
        cols = slice_cols(z, c, s)
        width = (128, 256)[c]
        buffer[...] = dot(flat, normed[:, cols]).astype(BF).reshape(32, 16, width)
        place_in = rows.at[y, x, :, cols]
        keep(buffer.at[slot_me], place_in, PICK, c)

        def out(k, carry):
            to, core = around(yx, k // 2), (s + k % 2) % 2
            send(buffer.at[core * 16 + to], place_in, PICK, c, core, to, z)
            return carry

        lax.fori_loop(1, 32, out, 0)

    def share_lines(c):
        for along in range(2):
            at = place_on[along]
            source = normed.at[:, rest_cols(s, along, c)]
            keep(source, lines.at[along, c, at], LINES, 2 * along + c)
            for k in (1, 3, 2):
                send(source, lines.at[along, c, at], LINES, 2 * along + c, s, chip((at + k) % 4, along), z)

    def deliver_rest(c):
        for along in range(2):
            wait(lines.at[along, c], LINES, 2 * along + c)
            for t in range(4):
                table = tables[along, t].reshape(128, 128)[:, 0:64]
                rest[along, c, :, :, t] = dot(table, lines[along, c, t]).astype(BF).reshape(2, 4, 16, 512)
            cols = rest_cols(s, along, c)
            place_in = rows.at[y, :, :, cols] if along == 0 else rows.at[:, x, :, cols]
            at = place_on[1 - along]
            keep(rest.at[along, c, s, at], place_in, PICK_REST, 2 * along + c)
            for k in (1, 3, 2):
                t = (at + k) % 4
                for core in range(2):
                    send(rest.at[along, c, core, t], place_in, PICK_REST, 2 * along + c, core, chip(t, 1 - along), z)
            send(rest.at[along, c, 1 - s, at], place_in, PICK_REST, 2 * along + c, 1 - s, yx, z)

    def spread(c):
        cols = whole_cols(z, c)
        wait(rows.at[:, :, :, cols], PICK, c)
        for k in (1, 3, 2):
            send(rows.at[:, :, :, cols], rows.at[:, :, :, cols], GATHER, c * 4 + z, s, yx, (z + k) % 4)

    wait(tables.at[0], TABLE, 0)
    wait(tables.at[1], TABLE, 1)
    deliver_slice(0, picked)
    share_lines(0)
    deliver_slice(1, picked_on)
    share_lines(1)
    spread(0)
    deliver_rest(0)
    spread(1)
    deliver_rest(1)

    pltpu.make_async_copy(w_gate, wg, csem.at[8]).wait()
    pltpu.make_async_copy(w_up, wu, csem.at[9]).wait()
    acc[...] = jnp.zeros_like(acc)

    def enter(at):
        some = rows[:, :, :, at].reshape(256, at.size)
        acc[0] += dot(some, wg[at])
        acc[1] += dot(some, wu[at])

    enter(whole_cols(z, 0))
    enter(whole_cols(z, 1))
    for c in range(2):
        for k in (1, 3, 2):
            t = (z + k) % 4
            wait(rows.at[:, :, :, whole_cols(t, c)], GATHER, c * 4 + t)
            enter(whole_cols(t, c))
        for along in range(2):
            wait(rows.at[:, :, :, pl.ds(0, 1024)], PICK_REST, 2 * along + c)
            for core in range(2):
                enter(rest_cols(core, along, c))
    gate = acc[0]
    hidden[...] = (gate * jax.nn.sigmoid(gate) * acc[1]).astype(BF)
    pltpu.make_async_copy(w_down, wd, csem.at[10]).wait()

    for k in (1, 3, 2, 0):
        t = (z + k) % 4
        got = dot(hidden[...], wd[:, pl.ds(pl.multiple_of(t * 768, 256), 768)]).astype(BF)
        if k == 0:
            yrecv[z] = got
        else:
            ysend[t] = got
    for j in range(4):
        some = pl.ds(pl.multiple_of(((y + j) % 4) * 64, 64), 64)
        for k in (1, 3, 2):
            t = (z + k) % 4
            send(ysend.at[t, some], yrecv.at[z, some], PIECE, (y + j) % 4, s, yx, t)

    for c in range(2):
        for along in range(2):
            at = place_on[1 - along]

            def part_of(core, t):
                source = bsend.at[core, along, c]
                return source.at[t] if along == 0 else source.at[:, t]

            for core in range(2):
                got = dot(hidden[...], wd[:, 3072 + core * 2048 + along * 1024 + c * 512 :][:, 0:512])
                bsend[core, along, c] = got.astype(BF).reshape(4, 4, 16, 512)
            land_in = brecv.at[along, c, s, at]
            keep(part_of(s, at), land_in, HOME, 2 * along + c)
            for k in (1, 3, 2):
                t = (at + k) % 4
                for core in range(2):
                    send(part_of(core, t), land_in, HOME, 2 * along + c, core, chip(t, 1 - along), z)
            send(part_of(1 - s, at), land_in, HOME, 2 * along + c, 1 - s, yx, z)

    def give(core, to):
        src = asend.at[core, pl.ds(pl.multiple_of(to * 16, 16), 16)]
        send(src, back.at[slot_me], BACK, 0, core, to, z)

    def home(c):
        for along in range(2):
            wait(brecv.at[along, c], HOME, 2 * along + c)
            for t in range(4):
                got = brecv[along, c, :, :, t].reshape(128, 512)
                summed = dot(tables[along, t].reshape(128, 128), got, ((0,), (0,)))[64:128]
                tsend_home[along, c, t] = summed.astype(BF)
            at = place_on[along]
            keep(tsend_home.at[along, c, at], trecv_home.at[along, c, at], HOME_ON, 2 * along + c)
            for k in (1, 3, 2):
                t = (at + k) % 4
                send(
                    tsend_home.at[along, c, t], trecv_home.at[along, c, at],
                    HOME_ON, 2 * along + c, s, chip(t, along), z,
                )

    def slices(j):
        to_y = (y + j) % 4
        some = pl.ds(pl.multiple_of(to_y * 64, 64), 64)
        wait(yrecv.at[pl.ds(0, 3), some], PIECE, to_y)
        got = [yrecv[q, some].astype(F32) for q in range(4)]
        total = ((got[0] + got[1]) + (got[2] + got[3])).astype(BF)
        for core in range(2):
            asend[core, some] = total[:, core * 384 : core * 384 + 384]
        if j == 0:
            keep(asend.at[s, land], back.at[slot_me], BACK, 0)
            give(1 - s, yx)
        for core in range(2):
            for k in range(1 if j == 0 else 0, 4):
                give(core, to_y * 4 + (x + k) % 4)

    slices(0)
    home(0)
    slices(1)
    slices(2)
    home(1)
    slices(3)

    for c in range(2):
        for along in range(2):
            wait(trecv_home.at[along, c], HOME_ON, 2 * along + c)
            got = [trecv_home[along, c, i].astype(F32) for i in range(4)]
            total = (got[0] + got[1]) + (got[2] + got[3])
            if along == 0:
                first = total
            else:
                both_rows = jnp.concatenate([first.reshape(8, 8, 512), total.reshape(8, 8, 512)], axis=1)
                fsend[:, :, c * 512 : c * 512 + 512] = both_rows.astype(BF)
    wait(back, BACK, 0)
    total = dot(select[...].reshape(512, 128), back[...].reshape(512, 384), ((0,), (0,)))[64:128]
    low = total[:, 0:256].reshape(8, 8, 256)
    high = jnp.concatenate([total[:, 256:384], jnp.zeros((64, 128), F32)], axis=1).reshape(8, 8, 256)
    fsend[:, :, 1024:1280] = jnp.concatenate([low, high], axis=1).astype(BF)
    keep(fsend.at[line_me], frecv.at[line_me], RESULT, 0)

    def finish(k, carry):
        core, to = (s + k // 4) % 2, (z + k % 4) % 4
        send(fsend.at[core * 4 + to], frecv.at[line_me], RESULT, 0, core, yx, to)
        return carry

    lax.fori_loop(1, 8, finish, 0)
    wait(frecv, RESULT, 0)

    def write(first, width, moe):
        at = slice(first, first + width)
        stream = gathered[s, :, at].astype(F32)
        own = jnp.zeros((8, width), F32)
        for t in range(4):
            own = jnp.where(z == t, stream[t * 8 : t * 8 + 8], own)
        both[0, :, at] = own.astype(BF)
        both[1, :, at] = (own + moe).astype(BF)

    for j in range(8):
        got = frecv[(j % 2) * 4 + j // 2, :, 1024:1280].astype(F32)
        write(j * 384, 256, got[0:8])
        write(j * 384 + 256, 128, got[8:16, 0:128])
    for core in range(2):
        for c in range(2):
            got = [frecv[core * 4 + t, :, c * 512 : c * 512 + 512].astype(F32) for t in range(4)]
            total = (got[0] + got[1]) + (got[2] + got[3])
            write(3072 + core * 2048 + c * 512, 512, total[0:8])
            write(3072 + core * 2048 + 1024 + c * 512, 512, total[8:16])

    for ref, kind in (
        (wuv.at[:, pl.ds(0, 384)], W_UV),
        (wo.at[pl.ds(0, 384)], W_OUT),
        (rsend.at[pl.ds(0, 3)], RESID),
        (wuv.at[:, half], UV_OVER),
        (wo.at[half], OUT_OVER),
        (late.at[:, pl.ds(0, 15)], LATENT),
        (vals.at[pl.ds(0, 3)], VALUE),
        (orecv.at[:, :, pl.ds(0, 3)], SUM),
        (tsend.at[:, :, pl.ds(0, 3)], SUM_ON),
        (gathered.at[s, :, pl.ds(0, 5376)], SLICE),
        (gathered.at[s], ROWS_OVER),
        (route.at[pl.ds(0, 7)], ROUTE),
        (tables.at[:, pl.ds(0, 3)], TABLE),
        (picked.at[pl.ds(0, 31)], PICK),
        (picked_on.at[pl.ds(0, 31)], PICK),
        (lines.at[:, :, pl.ds(0, 3)], LINES),
        (rest.at[:, :, 0], PICK_REST),
        (rest.at[:, :, 1, pl.ds(0, 3)], PICK_REST),
        (rows.at[:, :, :, pl.ds(0, 2304)], GATHER),
        (ysend.at[pl.ds(0, 3)], PIECE),
        (back.at[pl.ds(0, 31)], BACK),
        (brecv.at[:, :, 0], HOME),
        (brecv.at[:, :, 1, pl.ds(0, 3)], HOME),
        (tsend_home.at[:, :, pl.ds(0, 3)], HOME_ON),
        (fsend.at[pl.ds(0, 7)], RESULT),
    ):
        sent(ref, kind)


VMEM = pl.BlockSpec(memory_space=pltpu.VMEM)
SMEM = pl.BlockSpec(memory_space=pltpu.SMEM)
ANY = pl.BlockSpec(memory_space=pl.ANY)


def local(
    queries, cache, lengths, w_uv, w_out, resid, norm_gain, expert_ids, gate_weights, replica_slot, w_gate, w_up, w_down
):
    scratch = [
        pltpu.VMEM((8, 576, 512), BF),
        pltpu.VMEM((4, 16, 16, 512), BF),
        pltpu.VMEM((16, 4, 16, 512), BF),
        pltpu.VMEM((512, 1024), BF),
        pltpu.VMEM((1024, 1792), BF),
        pltpu.VMEM((4, 4, 32, 1024), BF),
        pltpu.VMEM((2, 4, 4, 16, 1792), BF),
        pltpu.VMEM((2, 2, 4, 4, 16, 896), BF),
        pltpu.VMEM((2, 2, 4, 16, 896), BF),
        pltpu.VMEM((2, 2, 4, 16, 896), BF),
        pltpu.VMEM((4, 8, 1792), F32),
        pltpu.VMEM((4, 8, 1792), F32),
        pltpu.VMEM((2, 32, 7168), BF),
        pltpu.VMEM((7168, 256), BF),
        pltpu.VMEM((7168, 256), BF),
        pltpu.VMEM((256, 7168), BF),
        pltpu.VMEM((8, 64, 128), BF),
        pltpu.VMEM((64, 7168), BF),
        pltpu.VMEM((2, 4, 4, 16, 128), BF),
        pltpu.VMEM((2, 4, 2, 4, 16, 128), BF),
        pltpu.VMEM((32, 16, 128), BF),
        pltpu.VMEM((32, 16, 256), BF),
        pltpu.VMEM((2, 2, 4, 64, 512), BF),
        pltpu.VMEM((2, 2, 2, 4, 4, 16, 512), BF),
        pltpu.VMEM((4, 4, 16, 7168), BF),
        pltpu.VMEM((2, 256, 256), F32),
        pltpu.VMEM((256, 256), BF),
        pltpu.VMEM((4, 256, 768), BF),
        pltpu.VMEM((4, 256, 768), BF),
        pltpu.VMEM((2, 2, 2, 4, 4, 16, 512), BF),
        pltpu.VMEM((2, 2, 2, 4, 4, 16, 512), BF),
        pltpu.VMEM((2, 2, 4, 64, 512), BF),
        pltpu.VMEM((2, 2, 4, 64, 512), BF),
        pltpu.VMEM((2, 256, 384), BF),
        pltpu.VMEM((32, 16, 384), BF),
        pltpu.VMEM((8, 16, 1280), BF),
        pltpu.VMEM((8, 16, 1280), BF),
    ] + [pltpu.SemaphoreType.DMA((n,)) for n in (11, len(PARTS), sum(PARTS))]
    both = pl.pallas_call(
        kernel,
        out_shape=jax.ShapeDtypeStruct((2, 8, 7168), BF),
        in_specs=[SMEM] * 4 + [VMEM, ANY, ANY, ANY, VMEM, VMEM, ANY, ANY, ANY],
        out_specs=VMEM,
        scratch_shapes=scratch,
        compiler_params=pltpu.CompilerParams(collective_id=0, has_side_effects=True, vmem_limit_bytes=60 * MB),
        name="layer",
    )(
        lengths,
        expert_ids.T,
        gate_weights.T.astype(F32),
        replica_slot.T,
        jnp.swapaxes(queries, 1, 2),
        jnp.swapaxes(cache, 1, 2),
        w_uv[0],
        w_out,
        resid,
        norm_gain[None],
        w_gate[0],
        w_up[0],
        w_down[0],
    )
    return both[0], both[1]


def solution(mesh):
    return jax.shard_map(
        local,
        mesh=mesh,
        in_specs=(
            P(("side", "dev"), None, None),
            P(("side", "dev"), None, None),
            P(("side", "dev")),
            P(("side", "dev"), None, None),
            P(("side", "dev"), None),
            P(("side", "dev"), None),
            P(),
            P(("side", "dev"), None),
            P(("side", "dev"), None),
            P(),
            P(("side", "dev"), None, None),
            P(("side", "dev"), None, None),
            P(("side", "dev"), None, None),
        ),
        out_specs=(P(("side", "dev"), None), P(("side", "dev"), None)),
        check_vma=False,
    )
```

```python
import functools
import math

import jax
import jax.numpy as jnp
from jax import lax
from jax.experimental import pallas as pl
from jax.experimental.pallas import tpu as pltpu
from jax.sharding import PartitionSpec as P

GROUP = 4
BF = jnp.bfloat16
F32 = jnp.float32
MB = 1 << 20


def place():
    s = lax.axis_index("side")
    dev = lax.axis_index("dev")
    return s, dev // 4, dev % 4


def dot(a, b, dims=((1,), (0,))):
    return lax.dot_general(a, b, (dims, ((), ())), preferred_element_type=F32)


def around(yx, k):
    return ((yx // 4 + k // 4) % 4) * 4 + (yx % 4 + k % 4) % 4


def iota(shape, dim):
    return lax.broadcasted_iota(jnp.int32, shape, dim)


W_UV, W_OUT, RESID, UV_OVER, OUT_OVER, LATENT, VALUE, SUM, SLICE, ROWS_OVER, ROUTE, PICK, PICK_REST, GATHER, PIECE, BACK, RESULT, SUM_ON, TABLE, LINES, HOME, HOME_ON = range(22)
PARTS = (8, 8, 1, 1, 2, 1, 8, 8, 2, 2, 1, 2, 4, 8, 4, 1, 1, 8, 2, 4, 4, 4)
FIRST = tuple(sum(PARTS[:i]) for i in range(len(PARTS)))


def kernel(
    lengths, expert_ids, gates, replicas,
    queries, cache, w_uv, w_out, resid, gain, w_gate, w_up, w_down,
    both,
    cbuf, qbuf, late, lrecv, wuv, wo, vals, osend, orecv, orecv_on, tsend, tsend_on, trecv, trecv_on, rsend, rrecv, gathered,
    wg, wu, wd, route, normed, select, tables, picked, picked_on, lines, rest, rows, acc, hidden,
    ysend, yrecv, bsend, brecv, tsend_home, trecv_home, asend, back, fsend, frecv,
    csem, ssem, rsem,
):
    def send(src, dst, kind, number, s, yx, z):
        pltpu.make_async_remote_copy(
            src_ref=src,
            dst_ref=dst,
            send_sem=ssem.at[kind],
            recv_sem=rsem.at[FIRST[kind] + number],
            device_id=(s, yx * 4 + z),
            device_id_type=pl.DeviceIdType.MESH,
        ).start()

    def keep(src, dst, kind, number):
        pltpu.make_async_copy(src, dst, rsem.at[FIRST[kind] + number]).start()

    def wait(ref, kind, number):
        pltpu.make_async_copy(ref, ref, rsem.at[FIRST[kind] + number]).wait()

    def sent(ref, kind):
        pltpu.make_async_copy(ref, ref, ssem.at[kind]).wait()

    s, yx, z = place()
    y, x = yx // 4, yx % 4

    barrier = pltpu.get_barrier_semaphore()

    def greet(core, chip, level):
        pl.semaphore_signal(
            barrier, inc=1, device_id=(core, chip * 4 + level), device_id_type=pl.DeviceIdType.MESH
        )

    def greet_plane(k, carry):
        greet((s + k % 2) % 2, around(yx, k // 2), z)
        return carry

    def greet_line(k, carry):
        greet((s + k // 4) % 2, yx, (z + k % 4) % 4)
        return carry

    lax.fori_loop(1, 4, greet_line, 0)
    lax.fori_loop(5, 8, greet_line, 0)
    lax.fori_loop(1, 32, greet_plane, 0)

    for r in range(8):
        pltpu.make_async_copy(queries.at[r], qbuf.at[r], csem.at[11 + r]).start()
        pltpu.make_async_copy(cache.at[r], cbuf.at[r], csem.at[r]).start()
    own_col = pl.multiple_of((s * 4 + z) * 128, 128)
    here = pl.ds(pl.multiple_of(z * 1792, 256), 1792)
    for q in range(4):
        rsend[q] = resid[:, q * 1792 : (q + 1) * 1792].astype(F32)
    pl.semaphore_wait(barrier, 37)

    def uv_part(t, h):
        return wuv.at[pl.ds(h * 256, 256), pl.ds(pl.multiple_of((s * 4 + t) * 128, 128), 128)]

    for h in range(2):
        keep(w_uv.at[pl.ds(h * 256, 256)], uv_part(z, h), W_UV, 2 * z + h)
        for k in (1, 3):
            send(w_uv.at[pl.ds(h * 256, 256)], uv_part(z, h), W_UV, 2 * z + h, s, yx, (z + k) % 4)

    parts = ((0, 1280), (1280, 512))

    def out_part(t, c):
        start, width = parts[c]
        return w_out.at[:, pl.ds(pl.multiple_of(t * 1792 + start, 256), width)]

    def wo_part(t, c):
        start, width = parts[c]
        return wo.at[pl.ds(pl.multiple_of((s * 4 + t) * 128, 128), 128), start : start + width]

    def send_out(c):
        for k in (1, 3, 2):
            t = (z + k) % 4
            send(out_part(t, c), wo_part(z, c), W_OUT, 2 * z + c, s, yx, t)

    def pass_out(c):
        for k in (1, 3, 2, 0):
            t = (z + k) % 4
            wait(wo_part(t, c), W_OUT, 2 * t + c)
            if k:
                send(wo_part(t, c), wo_part(t, c), OUT_OVER, c, 1 - s, yx, z)

    send_out(0)
    send(w_uv, wuv.at[:, pl.ds(own_col, 128)], UV_OVER, 0, 1 - s, yx, z)
    for c in range(2):
        keep(out_part(z, c), wo_part(z, c), W_OUT, 2 * z + c)
        send(out_part(z, c), wo_part(z, c), OUT_OVER, c, 1 - s, yx, z)
    keep(rsend.at[z], rrecv.at[z], RESID, 0)
    for k in (1, 3, 2):
        t = (z + k) % 4
        send(rsend.at[t], rrecv.at[z], RESID, 0, s, yx, t)

    row, col = iota((128, 128), 0), iota((128, 128), 1)
    head = ((row % 8) // 4) * 64 + (row // 8) * 4 + row % 4
    order = jnp.where(col == head, 1.0, 0.0).astype(BF)
    scale = 1.0 / math.sqrt(192)
    column = iota((128, 512), 1)

    def one(r):
        pltpu.make_async_copy(queries.at[r], qbuf.at[r], csem.at[11 + r]).wait()
        q = dot(order, qbuf[r], ((1,), (1,))).astype(BF)
        pltpu.make_async_copy(cache.at[r], cbuf.at[r], csem.at[r]).wait()
        scores = dot(q, cbuf[r]) * scale
        scores = jnp.where(column < lengths[r], scores, -1e30)
        weight = jnp.exp(scores - jnp.max(scores, axis=1, keepdims=True))
        total = jnp.sum(weight, axis=1, keepdims=True)
        latent = dot(weight.astype(BF), cbuf[r, 0:512], ((1,), (1,)))
        return (latent / total).reshape(16, 8, 512)

    def step(i, carry):
        late[i] = jnp.concatenate([one(2 * i), one(2 * i + 1)], axis=1).astype(BF)
        keep(late.at[i, yx], lrecv.at[yx, i], LATENT, 0)

        def out(k, carry):
            to = around(yx, k)
            send(late.at[i, to], lrecv.at[yx, i], LATENT, 0, s, to, z)
            return carry

        return lax.fori_loop(1, 16, out, carry)

    step(0, 0)
    for k, h in ((3, 0), (1, 1)):
        t = (z + k) % 4
        wait(uv_part(t, h), W_UV, 2 * t + h)
        send(uv_part(t, h), uv_part(t, h), W_UV, 2 * t + h, s, yx, (z + 4 - k) % 4)
    lax.fori_loop(1, 4, step, 0)

    pltpu.make_async_copy(w_gate, wg, csem.at[8]).start()
    pltpu.make_async_copy(w_up, wu, csem.at[9]).start()
    pltpu.make_async_copy(w_down, wd, csem.at[10]).start()
    slot_me = s * 16 + yx
    line_me = s * 4 + z

    half = pl.ds(pl.multiple_of(s * 512, 512), 512)
    for k, h in ((0, 0), (0, 1), (3, 1), (1, 0), (2, 0), (2, 1)):
        t = (z + k) % 4
        wait(uv_part(t, h), W_UV, 2 * t + h)
    for k in (1, 3, 2):
        at = pl.ds(pl.multiple_of((s * 4 + (z + k) % 4) * 128, 128), 128)
        send(wuv.at[:, at], wuv.at[:, at], UV_OVER, 0, 1 - s, yx, z)

    row, lane = iota((64, 128), 0), iota((64, 128), 1)

    gate_values = gates[...].astype(F32)
    table, used = jnp.zeros((64, 128), F32), jnp.zeros((64, 128), jnp.int32)
    for t in range(8):
        for k in range(4):
            slot = replicas[(t + k) % 2, expert_ids[k, t]]
            same = row // 2 == slot
            hit = same & (row % 2 == used)
            table = jnp.where(hit & (lane == line_me * 8 + t), 1.0, table)
            table = jnp.where(hit & (lane == 64 + line_me * 8 + t), gate_values[k : k + 1, t : t + 1], table)
            used = used + jnp.where(same, 1, 0)
    route[line_me] = table.astype(BF)

    def announce(k, carry):
        send(route.at[line_me], route.at[line_me], ROUTE, 0, (s + k // 4) % 2, yx, (z + k % 4) % 4)
        return carry

    lax.fori_loop(1, 8, announce, 0)
    wait(wuv.at[:, half], UV_OVER, 0)
    wait(lrecv, LATENT, 0)

    mine = iota((256, 1024), 0) % 8 == iota((256, 1024), 1) // 128
    pick = jnp.where(iota((32, 256), 1) // 8 == iota((32, 256), 0), 1.0, 0.0).astype(BF)

    def value(j, carry):
        some = lrecv[pl.ds(j * 4, 4)].reshape(256, 512)
        full = dot(some, wuv[...])
        own = jnp.where(mine, full, 0.0).astype(BF)
        vals[z, j] = dot(pick, own).astype(BF)
        for k in (1, 3):
            send(vals.at[z, j], vals.at[z, j], VALUE, 2 * z + j // 2, s, yx, (z + k) % 4)
        return carry

    lax.fori_loop(0, 4, value, 0)

    def values_of(k, h):
        t = (z + k) % 4
        wait(vals.at[t, pl.ds(2 * h, 2)], VALUE, 2 * t + h)
        return vals.at[t, pl.ds(2 * h, 2)], 2 * t + h

    pass_out(0)
    for k, h in ((3, 0), (1, 1)):
        ref, number = values_of(k, h)
        send(ref, ref, VALUE, number, s, yx, (z + 4 - k) % 4)
    send_out(1)
    wait(route.at[pl.ds(0, 7)], ROUTE, 0)
    a, b = iota((512, 512), 0), iota((512, 512), 1)
    deal = jnp.where(b == ((a % 16) // 2) * 64 + (a // 16) * 2 + a % 2, 1.0, 0.0).astype(BF)
    select[...] = dot(deal, route[...].reshape(512, 128)).astype(BF).reshape(2, 4, 4, 16, 128)
    for along in range(2):
        at = (x, y)[along]

        def column(t):
            return select.at[:, :, t] if along == 0 else select.at[:, t]

        keep(column(at), tables.at[along, at], TABLE, along)
        for k in (1, 3, 2):
            t = (at + k) % 4
            to = y * 4 + t if along == 0 else t * 4 + x
            send(column(t), tables.at[along, at], TABLE, along, s, to, z)
    wait(wo.at[half, 0:1280], OUT_OVER, 0)

    place_on = (x, y)
    buffers = ((orecv, tsend, trecv), (orecv_on, tsend_on, trecv_on))

    def of(ref, t, along, c):
        start, width = parts[c]
        cols = slice(start + along * width // 2, start + (along + 1) * width // 2)
        return ref.at[:, t, :, cols] if along == 0 else ref.at[t, :, :, cols]

    def chip(t, along):
        return y * 4 + t if along == 0 else t * 4 + x

    def project(c, p):
        def block(b, carry):
            at = pl.ds(pl.multiple_of(b * 256, 256), 256)
            got = dot(vals[pl.ds(2 * p, 2)].reshape(256, 1024), wo[:, at]).reshape(2, 16, 8, 256)
            osend[p, :, :, :, at] = jnp.concatenate([got[0], got[1]], axis=1).astype(BF).reshape(4, 4, 16, 256)
            return carry

        lax.fori_loop(parts[c][0] // 256, sum(parts[c]) // 256, block, 0)
        for along in range(2):
            at = place_on[along]
            number = 4 * c + 2 * p + along
            there = buffers[c][0].at[p, along, at]
            keep(of(osend.at[p], at, along, c), there, SUM, number)
            for k in (1, 3, 2):
                t = (at + k) % 4
                send(of(osend.at[p], t, along, c), there, SUM, number, s, chip(t, along), z)

    def sum_on(c, p):
        first, middle, last = buffers[c]
        for along in range(2):
            number = 4 * c + 2 * p + along
            wait(first.at[p, along], SUM, number)
            got = [first[p, along, i].astype(F32) for i in range(4)]
            middle[p, along] = ((got[0] + got[1]) + (got[2] + got[3])).astype(BF)
            at = place_on[1 - along]
            there = last.at[p, along, at]
            keep(middle.at[p, along, at], there, SUM_ON, number)
            for k in (1, 3, 2):
                t = (at + k) % 4
                send(middle.at[p, along, t], there, SUM_ON, number, s, chip(t, 1 - along), z)

    def row_cols(t, c):
        start, width = parts[c]
        return pl.ds(pl.multiple_of(t * 1792 + start, 256), width)

    def finish_sum(c):
        start, width = parts[c]
        last = buffers[c][2]
        for pp in range(2):
            p = (z // 2 + pp) % 2
            line = pl.ds(pl.multiple_of(p * 16, 16), 16)
            for along in range(2):
                wait(last.at[p, along], SUM_ON, 4 * c + 2 * p + along)
                got = [last[p, along, i].astype(F32) for i in range(4)]
                cols = slice(start + along * width // 2, start + (along + 1) * width // 2)
                base = jnp.concatenate([rrecv[2 * p, :, cols], rrecv[2 * p + 1, :, cols]], axis=0)
                total = base + ((got[0] + got[1]) + (got[2] + got[3]))
                at = pl.ds(pl.multiple_of(z * 1792 + start + along * width // 2, 128), width // 2)
                gathered[s, line, at] = total.astype(BF)
        mine = gathered.at[s, :, row_cols(z, c)]
        for k in (1, 3, 2):
            send(mine, mine, SLICE, c, s, yx, (z + k) % 4)
        for k in (0, 1, 3, 2) if c == 1 else (0,):
            send(mine, mine, ROWS_OVER, c, 1 - s, yx, (z + k) % 4)

    def pass_rows(c):
        width = parts[c][1]
        wait(gathered.at[s, :, pl.ds(0, 3 * width)], SLICE, c)
        for k in (1, 3, 2) if c == 0 else ():
            ref = gathered.at[s, :, row_cols((z + k) % 4, c)]
            send(ref, ref, ROWS_OVER, c, 1 - s, yx, z)

    wait(rrecv, RESID, 0)
    own_p = z // 2
    values_of(1, 0)
    values_of(3, 1)
    project(0, own_p)
    values_of(2, 0)
    values_of(2, 1)
    project(0, 1 - own_p)
    sum_on(0, own_p)
    sum_on(0, 1 - own_p)
    pass_out(1)
    wait(wo.at[half, 1280:1792], OUT_OVER, 1)
    project(1, own_p)
    project(1, 1 - own_p)
    finish_sum(0)
    sum_on(1, own_p)
    sum_on(1, 1 - own_p)
    pass_rows(0)
    finish_sum(1)
    pass_rows(1)

    def norm(core, p):
        stream = gathered[core, pl.ds(pl.multiple_of(p * 16, 16), 16)].astype(F32)
        mean = jnp.mean(stream * stream, axis=1, keepdims=True)
        at = pl.ds(pl.multiple_of(core * 32 + p * 16, 16), 16)
        normed[at] = (stream * lax.rsqrt(mean + 1e-06) * gain[...]).astype(BF)

    norm(s, 0)
    norm(s, 1)
    wait(gathered.at[s, :, pl.ds(0, 5120)], ROWS_OVER, 0)
    wait(gathered.at[s, :, pl.ds(0, 2048)], ROWS_OVER, 1)
    norm(1 - s, 0)
    norm(1 - s, 1)

    land = pl.ds(pl.multiple_of(yx * 16, 16), 16)
    flat = select[...].reshape(512, 128)[:, 0:64]

    def slice_cols(t, c, core):
        start, width = ((0, 128), (256, 256))[c]
        return pl.ds(pl.multiple_of(t * 768 + start + core * width, 128), width)

    def whole_cols(t, c):
        start, width = ((0, 256), (256, 512))[c]
        return pl.ds(pl.multiple_of(t * 768 + start, 256), width)

    def rest_cols(core, along, c):
        return pl.ds(pl.multiple_of(3072 + core * 2048 + along * 1024 + c * 512, 512), 512)

    def deliver_slice(c, buffer):
        cols = slice_cols(z, c, s)
        width = (128, 256)[c]
        buffer[...] = dot(flat, normed[:, cols]).astype(BF).reshape(32, 16, width)
        place_in = rows.at[y, x, :, cols]
        keep(buffer.at[slot_me], place_in, PICK, c)

        def out(k, carry):
            to, core = around(yx, k // 2), (s + k % 2) % 2
            send(buffer.at[core * 16 + to], place_in, PICK, c, core, to, z)
            return carry

        lax.fori_loop(1, 32, out, 0)

    def share_lines(c):
        for along in range(2):
            at = place_on[along]
            source = normed.at[:, rest_cols(s, along, c)]
            keep(source, lines.at[along, c, at], LINES, 2 * along + c)
            for k in (1, 3, 2):
                send(source, lines.at[along, c, at], LINES, 2 * along + c, s, chip((at + k) % 4, along), z)

    def deliver_rest(c):
        for along in range(2):
            wait(lines.at[along, c], LINES, 2 * along + c)
            for t in range(4):
                table = tables[along, t].reshape(128, 128)[:, 0:64]
                rest[along, c, :, :, t] = dot(table, lines[along, c, t]).astype(BF).reshape(2, 4, 16, 512)
            cols = rest_cols(s, along, c)
            place_in = rows.at[y, :, :, cols] if along == 0 else rows.at[:, x, :, cols]
            at = place_on[1 - along]
            keep(rest.at[along, c, s, at], place_in, PICK_REST, 2 * along + c)
            for k in (1, 3, 2):
                t = (at + k) % 4
                for core in range(2):
                    send(rest.at[along, c, core, t], place_in, PICK_REST, 2 * along + c, core, chip(t, 1 - along), z)
            send(rest.at[along, c, 1 - s, at], place_in, PICK_REST, 2 * along + c, 1 - s, yx, z)

    def spread(c):
        cols = whole_cols(z, c)
        wait(rows.at[:, :, :, cols], PICK, c)
        for k in (1, 3, 2):
            send(rows.at[:, :, :, cols], rows.at[:, :, :, cols], GATHER, c * 4 + z, s, yx, (z + k) % 4)

    wait(tables.at[0], TABLE, 0)
    wait(tables.at[1], TABLE, 1)
    deliver_slice(0, picked)
    share_lines(0)
    deliver_slice(1, picked_on)
    share_lines(1)
    spread(0)
    deliver_rest(0)
    spread(1)
    deliver_rest(1)

    pltpu.make_async_copy(w_gate, wg, csem.at[8]).wait()
    pltpu.make_async_copy(w_up, wu, csem.at[9]).wait()
    acc[...] = jnp.zeros_like(acc)

    def enter(at):
        some = rows[:, :, :, at].reshape(256, at.size)
        acc[0] += dot(some, wg[at])
        acc[1] += dot(some, wu[at])

    enter(whole_cols(z, 0))
    enter(whole_cols(z, 1))
    for c in range(2):
        for k in (1, 3, 2):
            t = (z + k) % 4
            wait(rows.at[:, :, :, whole_cols(t, c)], GATHER, c * 4 + t)
            enter(whole_cols(t, c))
        for along in range(2):
            wait(rows.at[:, :, :, pl.ds(0, 1024)], PICK_REST, 2 * along + c)
            for core in range(2):
                enter(rest_cols(core, along, c))
    gate = acc[0]
    hidden[...] = (gate * jax.nn.sigmoid(gate) * acc[1]).astype(BF)
    pltpu.make_async_copy(w_down, wd, csem.at[10]).wait()

    for k in (1, 3, 2, 0):
        t = (z + k) % 4
        got = dot(hidden[...], wd[:, pl.ds(pl.multiple_of(t * 768, 256), 768)]).astype(BF)
        if k == 0:
            yrecv[z] = got
        else:
            ysend[t] = got
    for j in range(4):
        some = pl.ds(pl.multiple_of(((y + j) % 4) * 64, 64), 64)
        for k in (1, 3, 2):
            t = (z + k) % 4
            send(ysend.at[t, some], yrecv.at[z, some], PIECE, (y + j) % 4, s, yx, t)

    for c in range(2):
        for along in range(2):
            at = place_on[1 - along]

            def part_of(core, t):
                source = bsend.at[core, along, c]
                return source.at[t] if along == 0 else source.at[:, t]

            for core in range(2):
                got = dot(hidden[...], wd[:, 3072 + core * 2048 + along * 1024 + c * 512 :][:, 0:512])
                bsend[core, along, c] = got.astype(BF).reshape(4, 4, 16, 512)
            land_in = brecv.at[along, c, s, at]
            keep(part_of(s, at), land_in, HOME, 2 * along + c)
            for k in (1, 3, 2):
                t = (at + k) % 4
                for core in range(2):
                    send(part_of(core, t), land_in, HOME, 2 * along + c, core, chip(t, 1 - along), z)
            send(part_of(1 - s, at), land_in, HOME, 2 * along + c, 1 - s, yx, z)

    def give(core, to):
        src = asend.at[core, pl.ds(pl.multiple_of(to * 16, 16), 16)]
        send(src, back.at[slot_me], BACK, 0, core, to, z)

    def home(c):
        for along in range(2):
            wait(brecv.at[along, c], HOME, 2 * along + c)
            for t in range(4):
                got = brecv[along, c, :, :, t].reshape(128, 512)
                summed = dot(tables[along, t].reshape(128, 128), got, ((0,), (0,)))[64:128]
                tsend_home[along, c, t] = summed.astype(BF)
            at = place_on[along]
            keep(tsend_home.at[along, c, at], trecv_home.at[along, c, at], HOME_ON, 2 * along + c)
            for k in (1, 3, 2):
                t = (at + k) % 4
                send(
                    tsend_home.at[along, c, t], trecv_home.at[along, c, at],
                    HOME_ON, 2 * along + c, s, chip(t, along), z,
                )

    def slices(j):
        to_y = (y + j) % 4
        some = pl.ds(pl.multiple_of(to_y * 64, 64), 64)
        wait(yrecv.at[pl.ds(0, 3), some], PIECE, to_y)
        got = [yrecv[q, some].astype(F32) for q in range(4)]
        total = ((got[0] + got[1]) + (got[2] + got[3])).astype(BF)
        for core in range(2):
            asend[core, some] = total[:, core * 384 : core * 384 + 384]
        if j == 0:
            keep(asend.at[s, land], back.at[slot_me], BACK, 0)
            give(1 - s, yx)
        for core in range(2):
            for k in range(1 if j == 0 else 0, 4):
                give(core, to_y * 4 + (x + k) % 4)

    slices(0)
    home(0)
    slices(1)
    slices(2)
    home(1)
    slices(3)

    for c in range(2):
        for along in range(2):
            wait(trecv_home.at[along, c], HOME_ON, 2 * along + c)
            got = [trecv_home[along, c, i].astype(F32) for i in range(4)]
            total = (got[0] + got[1]) + (got[2] + got[3])
            if along == 0:
                first = total
            else:
                both_rows = jnp.concatenate([first.reshape(8, 8, 512), total.reshape(8, 8, 512)], axis=1)
                fsend[:, :, c * 512 : c * 512 + 512] = both_rows.astype(BF)
    wait(back, BACK, 0)
    total = dot(select[...].reshape(512, 128), back[...].reshape(512, 384), ((0,), (0,)))[64:128]
    low = total[:, 0:256].reshape(8, 8, 256)
    high = jnp.concatenate([total[:, 256:384], jnp.zeros((64, 128), F32)], axis=1).reshape(8, 8, 256)
    fsend[:, :, 1024:1280] = jnp.concatenate([low, high], axis=1).astype(BF)
    keep(fsend.at[line_me], frecv.at[line_me], RESULT, 0)

    def finish(k, carry):
        core, to = (s + k // 4) % 2, (z + k % 4) % 4
        send(fsend.at[core * 4 + to], frecv.at[line_me], RESULT, 0, core, yx, to)
        return carry

    lax.fori_loop(1, 8, finish, 0)
    wait(frecv, RESULT, 0)

    def write(first, width, moe):
        at = slice(first, first + width)
        stream = gathered[s, :, at].astype(F32)
        own = jnp.zeros((8, width), F32)
        for t in range(4):
            own = jnp.where(z == t, stream[t * 8 : t * 8 + 8], own)
        both[0, :, at] = own.astype(BF)
        both[1, :, at] = (own + moe).astype(BF)

    for j in range(8):
        got = frecv[(j % 2) * 4 + j // 2, :, 1024:1280].astype(F32)
        write(j * 384, 256, got[0:8])
        write(j * 384 + 256, 128, got[8:16, 0:128])
    for core in range(2):
        for c in range(2):
            got = [frecv[core * 4 + t, :, c * 512 : c * 512 + 512].astype(F32) for t in range(4)]
            total = (got[0] + got[1]) + (got[2] + got[3])
            write(3072 + core * 2048 + c * 512, 512, total[0:8])
            write(3072 + core * 2048 + 1024 + c * 512, 512, total[8:16])

    for ref, kind in (
        (wuv.at[:, pl.ds(0, 384)], W_UV),
        (wo.at[pl.ds(0, 384)], W_OUT),
        (rsend.at[pl.ds(0, 3)], RESID),
        (wuv.at[:, half], UV_OVER),
        (wo.at[half], OUT_OVER),
        (late.at[:, pl.ds(0, 15)], LATENT),
        (vals.at[pl.ds(0, 3)], VALUE),
        (orecv.at[:, :, pl.ds(0, 3)], SUM),
        (orecv_on.at[:, :, pl.ds(0, 3)], SUM),
        (tsend.at[:, :, pl.ds(0, 3)], SUM_ON),
        (tsend_on.at[:, :, pl.ds(0, 3)], SUM_ON),
        (gathered.at[s, :, pl.ds(0, 5376)], SLICE),
        (gathered.at[s], ROWS_OVER),
        (route.at[pl.ds(0, 7)], ROUTE),
        (tables.at[:, pl.ds(0, 3)], TABLE),
        (picked.at[pl.ds(0, 31)], PICK),
        (picked_on.at[pl.ds(0, 31)], PICK),
        (lines.at[:, :, pl.ds(0, 3)], LINES),
        (rest.at[:, :, 0], PICK_REST),
        (rest.at[:, :, 1, pl.ds(0, 3)], PICK_REST),
        (rows.at[:, :, :, pl.ds(0, 2304)], GATHER),
        (ysend.at[pl.ds(0, 3)], PIECE),
        (back.at[pl.ds(0, 31)], BACK),
        (brecv.at[:, :, 0], HOME),
        (brecv.at[:, :, 1, pl.ds(0, 3)], HOME),
        (tsend_home.at[:, :, pl.ds(0, 3)], HOME_ON),
        (fsend.at[pl.ds(0, 7)], RESULT),
    ):
        sent(ref, kind)


VMEM = pl.BlockSpec(memory_space=pltpu.VMEM)
SMEM = pl.BlockSpec(memory_space=pltpu.SMEM)
ANY = pl.BlockSpec(memory_space=pl.ANY)


def local(
    queries, cache, lengths, w_uv, w_out, resid, norm_gain, expert_ids, gate_weights, replica_slot, w_gate, w_up, w_down
):
    scratch = [
        pltpu.VMEM((8, 576, 512), BF),
        pltpu.VMEM((8, 576, 128), BF),
        pltpu.VMEM((4, 16, 16, 512), BF),
        pltpu.VMEM((16, 4, 16, 512), BF),
        pltpu.VMEM((512, 1024), BF),
        pltpu.VMEM((1024, 1792), BF),
        pltpu.VMEM((4, 4, 32, 1024), BF),
        pltpu.VMEM((2, 4, 4, 16, 1792), BF),
        pltpu.VMEM((2, 2, 4, 4, 16, 640), BF),
        pltpu.VMEM((2, 2, 4, 4, 16, 256), BF),
        pltpu.VMEM((2, 2, 4, 16, 640), BF),
        pltpu.VMEM((2, 2, 4, 16, 256), BF),
        pltpu.VMEM((2, 2, 4, 16, 640), BF),
        pltpu.VMEM((2, 2, 4, 16, 256), BF),
        pltpu.VMEM((4, 8, 1792), F32),
        pltpu.VMEM((4, 8, 1792), F32),
        pltpu.VMEM((2, 32, 7168), BF),
        pltpu.VMEM((7168, 256), BF),
        pltpu.VMEM((7168, 256), BF),
        pltpu.VMEM((256, 7168), BF),
        pltpu.VMEM((8, 64, 128), BF),
        pltpu.VMEM((64, 7168), BF),
        pltpu.VMEM((2, 4, 4, 16, 128), BF),
        pltpu.VMEM((2, 4, 2, 4, 16, 128), BF),
        pltpu.VMEM((32, 16, 128), BF),
        pltpu.VMEM((32, 16, 256), BF),
        pltpu.VMEM((2, 2, 4, 64, 512), BF),
        pltpu.VMEM((2, 2, 2, 4, 4, 16, 512), BF),
        pltpu.VMEM((4, 4, 16, 7168), BF),
        pltpu.VMEM((2, 256, 256), F32),
        pltpu.VMEM((256, 256), BF),
        pltpu.VMEM((4, 256, 768), BF),
        pltpu.VMEM((4, 256, 768), BF),
        pltpu.VMEM((2, 2, 2, 4, 4, 16, 512), BF),
        pltpu.VMEM((2, 2, 2, 4, 4, 16, 512), BF),
        pltpu.VMEM((2, 2, 4, 64, 512), BF),
        pltpu.VMEM((2, 2, 4, 64, 512), BF),
        pltpu.VMEM((2, 256, 384), BF),
        pltpu.VMEM((32, 16, 384), BF),
        pltpu.VMEM((8, 16, 1280), BF),
        pltpu.VMEM((8, 16, 1280), BF),
    ] + [pltpu.SemaphoreType.DMA((n,)) for n in (19, len(PARTS), sum(PARTS))]
    both = pl.pallas_call(
        kernel,
        out_shape=jax.ShapeDtypeStruct((2, 8, 7168), BF),
        in_specs=[SMEM, SMEM, VMEM, SMEM, ANY, ANY, ANY, ANY, VMEM, VMEM, ANY, ANY, ANY],
        out_specs=VMEM,
        scratch_shapes=scratch,
        compiler_params=pltpu.CompilerParams(collective_id=0, has_side_effects=True, vmem_limit_bytes=60 * MB),
        name="layer",
    )(
        lengths,
        expert_ids.T,
        gate_weights.T,
        replica_slot.T,
        jnp.swapaxes(queries, 1, 2),
        jnp.swapaxes(cache, 1, 2),
        w_uv[0],
        w_out,
        resid,
        norm_gain[None],
        w_gate[0],
        w_up[0],
        w_down[0],
    )
    return both[0], both[1]


def solution(mesh):
    return jax.shard_map(
        local,
        mesh=mesh,
        in_specs=(
            P(("side", "dev"), None, None),
            P(("side", "dev"), None, None),
            P(("side", "dev")),
            P(("side", "dev"), None, None),
            P(("side", "dev"), None),
            P(("side", "dev"), None),
            P(),
            P(("side", "dev"), None),
            P(("side", "dev"), None),
            P(),
            P(("side", "dev"), None, None),
            P(("side", "dev"), None, None),
            P(("side", "dev"), None, None),
        ),
        out_specs=(P(("side", "dev"), None), P(("side", "dev"), None)),
        check_vma=False,
    )
```

```python
import functools
import math

import jax
import jax.numpy as jnp
from jax import lax
from jax.experimental import pallas as pl
from jax.experimental.pallas import tpu as pltpu
from jax.sharding import PartitionSpec as P

GROUP = 4
BF = jnp.bfloat16
F32 = jnp.float32
MB = 1 << 20


def place():
    s = lax.axis_index("side")
    dev = lax.axis_index("dev")
    return s, dev // 4, dev % 4


def dot(a, b, dims=((1,), (0,))):
    return lax.dot_general(a, b, (dims, ((), ())), preferred_element_type=F32)


def around(yx, k):
    return ((yx // 4 + k // 4) % 4) * 4 + (yx % 4 + k % 4) % 4


def iota(shape, dim):
    return lax.broadcasted_iota(jnp.int32, shape, dim)


W_UV, W_OUT, RESID, UV_OVER, OUT_OVER, LATENT, VALUE, SUM, SLICE, ROWS_OVER, ROUTE, PICK, PICK_REST, GATHER, PIECE, BACK, RESULT, SUM_ON, TABLE, LINES, HOME, HOME_ON = range(22)
PARTS = (8, 8, 1, 1, 2, 1, 8, 8, 2, 2, 1, 2, 4, 8, 4, 1, 3, 8, 2, 4, 4, 4)
FIRST = tuple(sum(PARTS[:i]) for i in range(len(PARTS)))


def kernel(
    lengths, expert_ids, gates, replicas,
    queries, cache, w_uv, w_out, resid, gain, w_gate, w_up, w_down,
    both,
    cbuf, qbuf, late, lrecv, wuv, wo, vals, osend, orecv, orecv_on, tsend, tsend_on, trecv, trecv_on, rsend, rrecv, gathered,
    wg, wu, wd, route, normed, select, tables, picked, picked_on, lines, rest, rows, acc, hidden,
    ysend, yrecv, bsend, brecv, tsend_home, trecv_home, asend, back, fsend, frecv,
    csem, ssem, rsem,
):
    def send(src, dst, kind, number, s, yx, z):
        pltpu.make_async_remote_copy(
            src_ref=src,
            dst_ref=dst,
            send_sem=ssem.at[kind],
            recv_sem=rsem.at[FIRST[kind] + number],
            device_id=(s, yx * 4 + z),
            device_id_type=pl.DeviceIdType.MESH,
        ).start()

    def keep(src, dst, kind, number):
        pltpu.make_async_copy(src, dst, rsem.at[FIRST[kind] + number]).start()

    def wait(ref, kind, number):
        pltpu.make_async_copy(ref, ref, rsem.at[FIRST[kind] + number]).wait()

    def sent(ref, kind):
        pltpu.make_async_copy(ref, ref, ssem.at[kind]).wait()

    s, yx, z = place()
    y, x = yx // 4, yx % 4

    barrier = pltpu.get_barrier_semaphore()

    def greet(core, chip, level):
        pl.semaphore_signal(
            barrier, inc=1, device_id=(core, chip * 4 + level), device_id_type=pl.DeviceIdType.MESH
        )

    def greet_plane(k, carry):
        greet((s + k % 2) % 2, around(yx, k // 2), z)
        return carry

    def greet_line(k, carry):
        greet((s + k // 4) % 2, yx, (z + k % 4) % 4)
        return carry

    lax.fori_loop(1, 4, greet_line, 0)
    lax.fori_loop(5, 8, greet_line, 0)
    lax.fori_loop(1, 32, greet_plane, 0)

    for r in range(8):
        pltpu.make_async_copy(queries.at[r], qbuf.at[r], csem.at[11 + r]).start()
        pltpu.make_async_copy(cache.at[r], cbuf.at[r], csem.at[r]).start()
    own_col = pl.multiple_of((s * 4 + z) * 128, 128)
    here = pl.ds(pl.multiple_of(z * 1792, 256), 1792)
    for q in range(4):
        rsend[q] = resid[:, q * 1792 : (q + 1) * 1792].astype(F32)
    pl.semaphore_wait(barrier, 37)

    def uv_part(t, h):
        return wuv.at[pl.ds(h * 256, 256), pl.ds(pl.multiple_of((s * 4 + t) * 128, 128), 128)]

    for h in range(2):
        keep(w_uv.at[pl.ds(h * 256, 256)], uv_part(z, h), W_UV, 2 * z + h)
        for k in (1, 3):
            send(w_uv.at[pl.ds(h * 256, 256)], uv_part(z, h), W_UV, 2 * z + h, s, yx, (z + k) % 4)

    parts = ((0, 1280), (1280, 512))

    def out_part(t, c):
        start, width = parts[c]
        return w_out.at[:, pl.ds(pl.multiple_of(t * 1792 + start, 256), width)]

    def wo_part(t, c):
        start, width = parts[c]
        return wo.at[pl.ds(pl.multiple_of((s * 4 + t) * 128, 128), 128), start : start + width]

    def send_out(c):
        for k in (1, 3, 2):
            t = (z + k) % 4
            send(out_part(t, c), wo_part(z, c), W_OUT, 2 * z + c, s, yx, t)

    def pass_out(c):
        for k in (1, 3, 2, 0):
            t = (z + k) % 4
            wait(wo_part(t, c), W_OUT, 2 * t + c)
            if k:
                send(wo_part(t, c), wo_part(t, c), OUT_OVER, c, 1 - s, yx, z)

    send_out(0)
    send(w_uv, wuv.at[:, pl.ds(own_col, 128)], UV_OVER, 0, 1 - s, yx, z)
    for c in range(2):
        keep(out_part(z, c), wo_part(z, c), W_OUT, 2 * z + c)
        send(out_part(z, c), wo_part(z, c), OUT_OVER, c, 1 - s, yx, z)
    keep(rsend.at[z], rrecv.at[z], RESID, 0)
    for k in (1, 3, 2):
        t = (z + k) % 4
        send(rsend.at[t], rrecv.at[z], RESID, 0, s, yx, t)

    row, col = iota((128, 128), 0), iota((128, 128), 1)
    head = ((row % 8) // 4) * 64 + (row // 8) * 4 + row % 4
    order = jnp.where(col == head, 1.0, 0.0).astype(BF)
    scale = 1.0 / math.sqrt(192)
    column = iota((128, 512), 1)

    def one(r):
        pltpu.make_async_copy(queries.at[r], qbuf.at[r], csem.at[11 + r]).wait()
        q = dot(order, qbuf[r], ((1,), (1,))).astype(BF)
        pltpu.make_async_copy(cache.at[r], cbuf.at[r], csem.at[r]).wait()
        scores = dot(q, cbuf[r]) * scale
        scores = jnp.where(column < lengths[r], scores, -1e30)
        weight = jnp.exp(scores - jnp.max(scores, axis=1, keepdims=True))
        total = jnp.sum(weight, axis=1, keepdims=True)
        latent = dot(weight.astype(BF), cbuf[r, 0:512], ((1,), (1,)))
        return (latent / total).reshape(16, 8, 512)

    def step(i, carry):
        late[i] = jnp.concatenate([one(2 * i), one(2 * i + 1)], axis=1).astype(BF)
        keep(late.at[i, yx], lrecv.at[yx, i], LATENT, 0)

        def out(k, carry):
            to = around(yx, k)
            send(late.at[i, to], lrecv.at[yx, i], LATENT, 0, s, to, z)
            return carry

        return lax.fori_loop(1, 16, out, carry)

    step(0, 0)
    for k, h in ((3, 0), (1, 1)):
        t = (z + k) % 4
        wait(uv_part(t, h), W_UV, 2 * t + h)
        send(uv_part(t, h), uv_part(t, h), W_UV, 2 * t + h, s, yx, (z + 4 - k) % 4)
    lax.fori_loop(1, 4, step, 0)

    pltpu.make_async_copy(w_gate, wg, csem.at[8]).start()
    pltpu.make_async_copy(w_up, wu, csem.at[9]).start()
    pltpu.make_async_copy(w_down, wd, csem.at[10]).start()
    slot_me = s * 16 + yx
    line_me = s * 4 + z

    half = pl.ds(pl.multiple_of(s * 512, 512), 512)
    for k, h in ((0, 0), (0, 1), (3, 1), (1, 0), (2, 0), (2, 1)):
        t = (z + k) % 4
        wait(uv_part(t, h), W_UV, 2 * t + h)
    for k in (1, 3, 2):
        at = pl.ds(pl.multiple_of((s * 4 + (z + k) % 4) * 128, 128), 128)
        send(wuv.at[:, at], wuv.at[:, at], UV_OVER, 0, 1 - s, yx, z)

    row, lane = iota((64, 128), 0), iota((64, 128), 1)

    gate_values = gates[...].astype(F32)
    table, used = jnp.zeros((64, 128), F32), jnp.zeros((64, 128), jnp.int32)
    for t in range(8):
        for k in range(4):
            slot = replicas[(t + k) % 2, expert_ids[k, t]]
            same = row // 2 == slot
            hit = same & (row % 2 == used)
            table = jnp.where(hit & (lane == line_me * 8 + t), 1.0, table)
            table = jnp.where(hit & (lane == 64 + line_me * 8 + t), gate_values[k : k + 1, t : t + 1], table)
            used = used + jnp.where(same, 1, 0)
    route[line_me] = table.astype(BF)

    def announce(k, carry):
        send(route.at[line_me], route.at[line_me], ROUTE, 0, (s + k // 4) % 2, yx, (z + k % 4) % 4)
        return carry

    lax.fori_loop(1, 8, announce, 0)
    wait(wuv.at[:, half], UV_OVER, 0)
    wait(lrecv, LATENT, 0)

    mine = iota((256, 1024), 0) % 8 == iota((256, 1024), 1) // 128
    pick = jnp.where(iota((32, 256), 1) // 8 == iota((32, 256), 0), 1.0, 0.0).astype(BF)

    def value(j, carry):
        some = lrecv[pl.ds(j * 4, 4)].reshape(256, 512)
        full = dot(some, wuv[...])
        own = jnp.where(mine, full, 0.0).astype(BF)
        vals[z, j] = dot(pick, own).astype(BF)
        for k in (1, 3):
            send(vals.at[z, j], vals.at[z, j], VALUE, 2 * z + j // 2, s, yx, (z + k) % 4)
        return carry

    lax.fori_loop(0, 4, value, 0)

    def values_of(k, h):
        t = (z + k) % 4
        wait(vals.at[t, pl.ds(2 * h, 2)], VALUE, 2 * t + h)
        return vals.at[t, pl.ds(2 * h, 2)], 2 * t + h

    pass_out(0)
    for k, h in ((3, 0), (1, 1)):
        ref, number = values_of(k, h)
        send(ref, ref, VALUE, number, s, yx, (z + 4 - k) % 4)
    send_out(1)
    wait(route.at[pl.ds(0, 7)], ROUTE, 0)
    a, b = iota((512, 512), 0), iota((512, 512), 1)
    deal = jnp.where(b == ((a % 16) // 2) * 64 + (a // 16) * 2 + a % 2, 1.0, 0.0).astype(BF)
    select[...] = dot(deal, route[...].reshape(512, 128)).astype(BF).reshape(2, 4, 4, 16, 128)
    for along in range(2):
        at = (x, y)[along]

        def column(t):
            return select.at[:, :, t] if along == 0 else select.at[:, t]

        keep(column(at), tables.at[along, at], TABLE, along)
        for k in (1, 3, 2):
            t = (at + k) % 4
            to = y * 4 + t if along == 0 else t * 4 + x
            send(column(t), tables.at[along, at], TABLE, along, s, to, z)
    wait(wo.at[half, 0:1280], OUT_OVER, 0)

    place_on = (x, y)
    buffers = ((orecv, tsend, trecv), (orecv_on, tsend_on, trecv_on))

    def of(ref, t, along, c):
        start, width = parts[c]
        cols = slice(start + along * width // 2, start + (along + 1) * width // 2)
        return ref.at[:, t, :, cols] if along == 0 else ref.at[t, :, :, cols]

    def chip(t, along):
        return y * 4 + t if along == 0 else t * 4 + x

    def project(c, p):
        def block(b, carry):
            at = pl.ds(pl.multiple_of(b * 256, 256), 256)
            got = dot(vals[pl.ds(2 * p, 2)].reshape(256, 1024), wo[:, at]).reshape(2, 16, 8, 256)
            osend[p, :, :, :, at] = jnp.concatenate([got[0], got[1]], axis=1).astype(BF).reshape(4, 4, 16, 256)
            return carry

        lax.fori_loop(parts[c][0] // 256, sum(parts[c]) // 256, block, 0)
        for along in range(2):
            at = place_on[along]
            number = 4 * c + 2 * p + along
            there = buffers[c][0].at[p, along, at]
            keep(of(osend.at[p], at, along, c), there, SUM, number)
            for k in (1, 3, 2):
                t = (at + k) % 4
                send(of(osend.at[p], t, along, c), there, SUM, number, s, chip(t, along), z)

    def sum_on(c, p):
        first, middle, last = buffers[c]
        for along in range(2):
            number = 4 * c + 2 * p + along
            wait(first.at[p, along], SUM, number)
            got = [first[p, along, i].astype(F32) for i in range(4)]
            middle[p, along] = ((got[0] + got[1]) + (got[2] + got[3])).astype(BF)
            at = place_on[1 - along]
            there = last.at[p, along, at]
            keep(middle.at[p, along, at], there, SUM_ON, number)
            for k in (1, 3, 2):
                t = (at + k) % 4
                send(middle.at[p, along, t], there, SUM_ON, number, s, chip(t, 1 - along), z)

    def row_cols(t, c):
        start, width = parts[c]
        return pl.ds(pl.multiple_of(t * 1792 + start, 256), width)

    def finish_sum(c):
        start, width = parts[c]
        last = buffers[c][2]
        for pp in range(2):
            p = (z // 2 + pp) % 2
            line = pl.ds(pl.multiple_of(p * 16, 16), 16)
            for along in range(2):
                wait(last.at[p, along], SUM_ON, 4 * c + 2 * p + along)
                got = [last[p, along, i].astype(F32) for i in range(4)]
                cols = slice(start + along * width // 2, start + (along + 1) * width // 2)
                base = jnp.concatenate([rrecv[2 * p, :, cols], rrecv[2 * p + 1, :, cols]], axis=0)
                total = base + ((got[0] + got[1]) + (got[2] + got[3]))
                at = pl.ds(pl.multiple_of(z * 1792 + start + along * width // 2, 128), width // 2)
                gathered[s, line, at] = total.astype(BF)
        mine = gathered.at[s, :, row_cols(z, c)]
        for k in (1, 3, 2):
            send(mine, mine, SLICE, c, s, yx, (z + k) % 4)
        for k in (0, 1, 3, 2) if c == 1 else (0,):
            send(mine, mine, ROWS_OVER, c, 1 - s, yx, (z + k) % 4)

    def pass_rows(c):
        width = parts[c][1]
        wait(gathered.at[s, :, pl.ds(0, 3 * width)], SLICE, c)
        for k in (1, 3, 2) if c == 0 else ():
            ref = gathered.at[s, :, row_cols((z + k) % 4, c)]
            send(ref, ref, ROWS_OVER, c, 1 - s, yx, z)

    wait(rrecv, RESID, 0)
    own_p = z // 2
    values_of(1, 0)
    values_of(3, 1)
    project(0, own_p)
    values_of(2, 0)
    values_of(2, 1)
    project(0, 1 - own_p)
    sum_on(0, own_p)
    sum_on(0, 1 - own_p)
    pass_out(1)
    wait(wo.at[half, 1280:1792], OUT_OVER, 1)
    project(1, own_p)
    project(1, 1 - own_p)
    finish_sum(0)
    sum_on(1, own_p)
    sum_on(1, 1 - own_p)
    pass_rows(0)
    finish_sum(1)
    pass_rows(1)

    def norm(core, p):
        stream = gathered[core, pl.ds(pl.multiple_of(p * 16, 16), 16)].astype(F32)
        mean = jnp.mean(stream * stream, axis=1, keepdims=True)
        at = pl.ds(pl.multiple_of(core * 32 + p * 16, 16), 16)
        normed[at] = (stream * lax.rsqrt(mean + 1e-06) * gain[...]).astype(BF)

    norm(s, 0)
    norm(s, 1)
    wait(gathered.at[s, :, pl.ds(0, 5120)], ROWS_OVER, 0)
    wait(gathered.at[s, :, pl.ds(0, 2048)], ROWS_OVER, 1)
    norm(1 - s, 0)
    norm(1 - s, 1)

    land = pl.ds(pl.multiple_of(yx * 16, 16), 16)
    flat = select[...].reshape(512, 128)[:, 0:64]

    def slice_cols(t, c, core):
        start, width = ((0, 128), (256, 256))[c]
        return pl.ds(pl.multiple_of(t * 768 + start + core * width, 128), width)

    def whole_cols(t, c):
        start, width = ((0, 256), (256, 512))[c]
        return pl.ds(pl.multiple_of(t * 768 + start, 256), width)

    def rest_cols(core, along, c):
        return pl.ds(pl.multiple_of(3072 + core * 2048 + along * 1024 + c * 512, 512), 512)

    def deliver_slice(c, buffer):
        cols = slice_cols(z, c, s)
        width = (128, 256)[c]
        buffer[...] = dot(flat, normed[:, cols]).astype(BF).reshape(32, 16, width)
        place_in = rows.at[y, x, :, cols]
        keep(buffer.at[slot_me], place_in, PICK, c)

        def out(k, carry):
            to, core = around(yx, k // 2), (s + k % 2) % 2
            send(buffer.at[core * 16 + to], place_in, PICK, c, core, to, z)
            return carry

        lax.fori_loop(1, 32, out, 0)

    def share_lines(c):
        for along in range(2):
            at = place_on[along]
            source = normed.at[:, rest_cols(s, along, c)]
            keep(source, lines.at[along, c, at], LINES, 2 * along + c)
            for k in (1, 3, 2):
                send(source, lines.at[along, c, at], LINES, 2 * along + c, s, chip((at + k) % 4, along), z)

    def deliver_rest(c):
        for along in range(2):
            wait(lines.at[along, c], LINES, 2 * along + c)
            for t in range(4):
                table = tables[along, t].reshape(128, 128)[:, 0:64]
                rest[along, c, :, :, t] = dot(table, lines[along, c, t]).astype(BF).reshape(2, 4, 16, 512)
            cols = rest_cols(s, along, c)
            place_in = rows.at[y, :, :, cols] if along == 0 else rows.at[:, x, :, cols]
            at = place_on[1 - along]
            keep(rest.at[along, c, s, at], place_in, PICK_REST, 2 * along + c)
            for k in (1, 3, 2):
                t = (at + k) % 4
                for core in range(2):
                    send(rest.at[along, c, core, t], place_in, PICK_REST, 2 * along + c, core, chip(t, 1 - along), z)
            send(rest.at[along, c, 1 - s, at], place_in, PICK_REST, 2 * along + c, 1 - s, yx, z)

    def spread(c):
        cols = whole_cols(z, c)
        wait(rows.at[:, :, :, cols], PICK, c)
        for k in (1, 3, 2):
            send(rows.at[:, :, :, cols], rows.at[:, :, :, cols], GATHER, c * 4 + z, s, yx, (z + k) % 4)

    wait(tables.at[0], TABLE, 0)
    wait(tables.at[1], TABLE, 1)
    deliver_slice(0, picked)
    share_lines(0)
    deliver_slice(1, picked_on)
    share_lines(1)
    spread(0)
    deliver_rest(0)
    spread(1)
    deliver_rest(1)

    pltpu.make_async_copy(w_gate, wg, csem.at[8]).wait()
    pltpu.make_async_copy(w_up, wu, csem.at[9]).wait()
    acc[...] = jnp.zeros_like(acc)

    def enter(at):
        some = rows[:, :, :, at].reshape(256, at.size)
        acc[0] += dot(some, wg[at])
        acc[1] += dot(some, wu[at])

    enter(whole_cols(z, 0))
    enter(whole_cols(z, 1))
    for c in range(2):
        for k in (1, 3, 2):
            t = (z + k) % 4
            wait(rows.at[:, :, :, whole_cols(t, c)], GATHER, c * 4 + t)
            enter(whole_cols(t, c))
        for along in range(2):
            wait(rows.at[:, :, :, pl.ds(0, 1024)], PICK_REST, 2 * along + c)
            for core in range(2):
                enter(rest_cols(core, along, c))
    gate = acc[0]
    hidden[...] = (gate * jax.nn.sigmoid(gate) * acc[1]).astype(BF)
    pltpu.make_async_copy(w_down, wd, csem.at[10]).wait()

    for k in (1, 3, 2, 0):
        t = (z + k) % 4
        got = dot(hidden[...], wd[:, pl.ds(pl.multiple_of(t * 768, 256), 768)]).astype(BF)
        if k == 0:
            yrecv[z] = got
        else:
            ysend[t] = got
    for j in range(4):
        some = pl.ds(pl.multiple_of(((y + j) % 4) * 64, 64), 64)
        for k in (1, 3, 2):
            t = (z + k) % 4
            send(ysend.at[t, some], yrecv.at[z, some], PIECE, (y + j) % 4, s, yx, t)

    for c in range(2):
        for along in range(2):
            at = place_on[1 - along]

            def part_of(core, t):
                source = bsend.at[core, along, c]
                return source.at[t] if along == 0 else source.at[:, t]

            for core in range(2):
                got = dot(hidden[...], wd[:, 3072 + core * 2048 + along * 1024 + c * 512 :][:, 0:512])
                bsend[core, along, c] = got.astype(BF).reshape(4, 4, 16, 512)
            land_in = brecv.at[along, c, s, at]
            keep(part_of(s, at), land_in, HOME, 2 * along + c)
            for k in (1, 3, 2):
                t = (at + k) % 4
                for core in range(2):
                    send(part_of(core, t), land_in, HOME, 2 * along + c, core, chip(t, 1 - along), z)
            send(part_of(1 - s, at), land_in, HOME, 2 * along + c, 1 - s, yx, z)

    def give(core, to):
        src = asend.at[core, pl.ds(pl.multiple_of(to * 16, 16), 16)]
        send(src, back.at[slot_me], BACK, 0, core, to, z)

    def home(c):
        for along in range(2):
            wait(brecv.at[along, c], HOME, 2 * along + c)
            for t in range(4):
                got = brecv[along, c, :, :, t].reshape(128, 512)
                summed = dot(tables[along, t].reshape(128, 128), got, ((0,), (0,)))[64:128]
                tsend_home[along, c, t] = summed.astype(BF)
            at = place_on[along]
            keep(tsend_home.at[along, c, at], trecv_home.at[along, c, at], HOME_ON, 2 * along + c)
            for k in (1, 3, 2):
                t = (at + k) % 4
                send(
                    tsend_home.at[along, c, t], trecv_home.at[along, c, at],
                    HOME_ON, 2 * along + c, s, chip(t, along), z,
                )

    def slices(j):
        to_y = (y + j) % 4
        some = pl.ds(pl.multiple_of(to_y * 64, 64), 64)
        wait(yrecv.at[pl.ds(0, 3), some], PIECE, to_y)
        got = [yrecv[q, some].astype(F32) for q in range(4)]
        total = ((got[0] + got[1]) + (got[2] + got[3])).astype(BF)
        for core in range(2):
            asend[core, some] = total[:, core * 384 : core * 384 + 384]
        if j == 0:
            keep(asend.at[s, land], back.at[slot_me], BACK, 0)
            give(1 - s, yx)
        for core in range(2):
            for k in range(1 if j == 0 else 0, 4):
                give(core, to_y * 4 + (x + k) % 4)

    slices(0)
    home(0)
    slices(1)
    slices(2)
    home(1)
    slices(3)

    result_cols = (slice(0, 512), slice(512, 1024), slice(1024, 1280))

    def finish(n):
        cols = result_cols[n]
        keep(fsend.at[line_me, :, cols], frecv.at[line_me, :, cols], RESULT, n)

        def out(k, carry):
            core, to = (s + k // 4) % 2, (z + k % 4) % 4
            send(fsend.at[core * 4 + to, :, cols], frecv.at[line_me, :, cols], RESULT, n, core, yx, to)
            return carry

        lax.fori_loop(1, 8, out, 0)

    def finish_rest(c):
        total = []
        for along in range(2):
            wait(trecv_home.at[along, c], HOME_ON, 2 * along + c)
            got = [trecv_home[along, c, i].astype(F32) for i in range(4)]
            total.append(((got[0] + got[1]) + (got[2] + got[3])).reshape(8, 8, 512))
        fsend[:, :, result_cols[c]] = jnp.concatenate(total, axis=1).astype(BF)
        finish(c)

    def finish_slices():
        wait(back, BACK, 0)
        total = dot(select[...].reshape(512, 128), back[...].reshape(512, 384), ((0,), (0,)))[64:128]
        low = total[:, 0:256].reshape(8, 8, 256)
        high = jnp.concatenate([total[:, 256:384], jnp.zeros((64, 128), F32)], axis=1).reshape(8, 8, 256)
        fsend[:, :, 1024:1280] = jnp.concatenate([low, high], axis=1).astype(BF)
        finish(2)

    finish_rest(0)
    finish_rest(1)
    finish_slices()

    def write(first, width, moe):
        at = slice(first, first + width)
        stream = gathered[s, :, at].astype(F32)
        own = jnp.zeros((8, width), F32)
        for t in range(4):
            own = jnp.where(z == t, stream[t * 8 : t * 8 + 8], own)
        both[0, :, at] = own.astype(BF)
        both[1, :, at] = (own + moe).astype(BF)

    for c in range(2):
        wait(frecv.at[:, :, result_cols[c]], RESULT, c)
        for core in range(2):
            got = [frecv[core * 4 + t, :, result_cols[c]].astype(F32) for t in range(4)]
            total = (got[0] + got[1]) + (got[2] + got[3])
            write(3072 + core * 2048 + c * 512, 512, total[0:8])
            write(3072 + core * 2048 + 1024 + c * 512, 512, total[8:16])
    wait(frecv.at[:, :, result_cols[2]], RESULT, 2)
    for j in range(8):
        got = frecv[(j % 2) * 4 + j // 2, :, 1024:1280].astype(F32)
        write(j * 384, 256, got[0:8])
        write(j * 384 + 256, 128, got[8:16, 0:128])

    for ref, kind in (
        (wuv.at[:, pl.ds(0, 384)], W_UV),
        (wo.at[pl.ds(0, 384)], W_OUT),
        (rsend.at[pl.ds(0, 3)], RESID),
        (wuv.at[:, half], UV_OVER),
        (wo.at[half], OUT_OVER),
        (late.at[:, pl.ds(0, 15)], LATENT),
        (vals.at[pl.ds(0, 3)], VALUE),
        (orecv.at[:, :, pl.ds(0, 3)], SUM),
        (orecv_on.at[:, :, pl.ds(0, 3)], SUM),
        (tsend.at[:, :, pl.ds(0, 3)], SUM_ON),
        (tsend_on.at[:, :, pl.ds(0, 3)], SUM_ON),
        (gathered.at[s, :, pl.ds(0, 5376)], SLICE),
        (gathered.at[s], ROWS_OVER),
        (route.at[pl.ds(0, 7)], ROUTE),
        (tables.at[:, pl.ds(0, 3)], TABLE),
        (picked.at[pl.ds(0, 31)], PICK),
        (picked_on.at[pl.ds(0, 31)], PICK),
        (lines.at[:, :, pl.ds(0, 3)], LINES),
        (rest.at[:, :, 0], PICK_REST),
        (rest.at[:, :, 1, pl.ds(0, 3)], PICK_REST),
        (rows.at[:, :, :, pl.ds(0, 2304)], GATHER),
        (ysend.at[pl.ds(0, 3)], PIECE),
        (back.at[pl.ds(0, 31)], BACK),
        (brecv.at[:, :, 0], HOME),
        (brecv.at[:, :, 1, pl.ds(0, 3)], HOME),
        (tsend_home.at[:, :, pl.ds(0, 3)], HOME_ON),
        (fsend.at[pl.ds(0, 7)], RESULT),
    ):
        sent(ref, kind)


VMEM = pl.BlockSpec(memory_space=pltpu.VMEM)
SMEM = pl.BlockSpec(memory_space=pltpu.SMEM)
ANY = pl.BlockSpec(memory_space=pl.ANY)


def local(
    queries, cache, lengths, w_uv, w_out, resid, norm_gain, expert_ids, gate_weights, replica_slot, w_gate, w_up, w_down
):
    scratch = [
        pltpu.VMEM((8, 576, 512), BF),
        pltpu.VMEM((8, 576, 128), BF),
        pltpu.VMEM((4, 16, 16, 512), BF),
        pltpu.VMEM((16, 4, 16, 512), BF),
        pltpu.VMEM((512, 1024), BF),
        pltpu.VMEM((1024, 1792), BF),
        pltpu.VMEM((4, 4, 32, 1024), BF),
        pltpu.VMEM((2, 4, 4, 16, 1792), BF),
        pltpu.VMEM((2, 2, 4, 4, 16, 640), BF),
        pltpu.VMEM((2, 2, 4, 4, 16, 256), BF),
        pltpu.VMEM((2, 2, 4, 16, 640), BF),
        pltpu.VMEM((2, 2, 4, 16, 256), BF),
        pltpu.VMEM((2, 2, 4, 16, 640), BF),
        pltpu.VMEM((2, 2, 4, 16, 256), BF),
        pltpu.VMEM((4, 8, 1792), F32),
        pltpu.VMEM((4, 8, 1792), F32),
        pltpu.VMEM((2, 32, 7168), BF),
        pltpu.VMEM((7168, 256), BF),
        pltpu.VMEM((7168, 256), BF),
        pltpu.VMEM((256, 7168), BF),
        pltpu.VMEM((8, 64, 128), BF),
        pltpu.VMEM((64, 7168), BF),
        pltpu.VMEM((2, 4, 4, 16, 128), BF),
        pltpu.VMEM((2, 4, 2, 4, 16, 128), BF),
        pltpu.VMEM((32, 16, 128), BF),
        pltpu.VMEM((32, 16, 256), BF),
        pltpu.VMEM((2, 2, 4, 64, 512), BF),
        pltpu.VMEM((2, 2, 2, 4, 4, 16, 512), BF),
        pltpu.VMEM((4, 4, 16, 7168), BF),
        pltpu.VMEM((2, 256, 256), F32),
        pltpu.VMEM((256, 256), BF),
        pltpu.VMEM((4, 256, 768), BF),
        pltpu.VMEM((4, 256, 768), BF),
        pltpu.VMEM((2, 2, 2, 4, 4, 16, 512), BF),
        pltpu.VMEM((2, 2, 2, 4, 4, 16, 512), BF),
        pltpu.VMEM((2, 2, 4, 64, 512), BF),
        pltpu.VMEM((2, 2, 4, 64, 512), BF),
        pltpu.VMEM((2, 256, 384), BF),
        pltpu.VMEM((32, 16, 384), BF),
        pltpu.VMEM((8, 16, 1280), BF),
        pltpu.VMEM((8, 16, 1280), BF),
    ] + [pltpu.SemaphoreType.DMA((n,)) for n in (19, len(PARTS), sum(PARTS))]
    both = pl.pallas_call(
        kernel,
        out_shape=jax.ShapeDtypeStruct((2, 8, 7168), BF),
        in_specs=[SMEM, SMEM, VMEM, SMEM, ANY, ANY, ANY, ANY, VMEM, VMEM, ANY, ANY, ANY],
        out_specs=VMEM,
        scratch_shapes=scratch,
        compiler_params=pltpu.CompilerParams(collective_id=0, has_side_effects=True, vmem_limit_bytes=60 * MB),
        name="layer",
    )(
        lengths,
        expert_ids.T,
        gate_weights.T,
        replica_slot.T,
        jnp.swapaxes(queries, 1, 2),
        jnp.swapaxes(cache, 1, 2),
        w_uv[0],
        w_out,
        resid,
        norm_gain[None],
        w_gate[0],
        w_up[0],
        w_down[0],
    )
    return both[0], both[1]


def solution(mesh):
    return jax.shard_map(
        local,
        mesh=mesh,
        in_specs=(
            P(("side", "dev"), None, None),
            P(("side", "dev"), None, None),
            P(("side", "dev")),
            P(("side", "dev"), None, None),
            P(("side", "dev"), None),
            P(("side", "dev"), None),
            P(),
            P(("side", "dev"), None),
            P(("side", "dev"), None),
            P(),
            P(("side", "dev"), None, None),
            P(("side", "dev"), None, None),
            P(("side", "dev"), None, None),
        ),
        out_specs=(P(("side", "dev"), None), P(("side", "dev"), None)),
        check_vma=False,
    )
```

```python
import functools
import math

import jax
import jax.numpy as jnp
from jax import lax
from jax.experimental import pallas as pl
from jax.experimental.pallas import tpu as pltpu
from jax.sharding import PartitionSpec as P

GROUP = 4
BF = jnp.bfloat16
F32 = jnp.float32
MB = 1 << 20


def place():
    s = lax.axis_index("side")
    dev = lax.axis_index("dev")
    return s, dev // 4, dev % 4


def dot(a, b, dims=((1,), (0,))):
    return lax.dot_general(a, b, (dims, ((), ())), preferred_element_type=F32)


def around(yx, k):
    return ((yx // 4 + k // 4) % 4) * 4 + (yx % 4 + k % 4) % 4


def iota(shape, dim):
    return lax.broadcasted_iota(jnp.int32, shape, dim)


W_UV, W_OUT, RESID, UV_OVER, OUT_OVER, LATENT, VALUE, SUM, SLICE, ROWS_OVER, ROUTE, PICK, PICK_REST, GATHER, PIECE, BACK, RESULT, SUM_ON, TABLE, LINES, HOME, HOME_ON = range(22)
PARTS = (8, 8, 1, 1, 2, 1, 8, 8, 2, 2, 1, 2, 4, 16, 4, 1, 3, 8, 2, 4, 4, 4)
FIRST = tuple(sum(PARTS[:i]) for i in range(len(PARTS)))


def kernel(
    lengths, expert_ids, gates, replicas,
    queries, cache, w_uv, w_out, resid, gain, w_gate, w_up, w_down,
    both,
    cbuf, qbuf, late, lrecv, wuv, wo, vals, osend, orecv, orecv_on, tsend, tsend_on, trecv, trecv_on, rsend, rrecv, gathered,
    wg, wu, wd, route, normed, select, tables, picked, picked_on, lines, rest, rows, acc, hidden,
    ysend, yrecv, bsend, brecv, tsend_home, trecv_home, asend, back, fsend, frecv,
    csem, ssem, rsem,
):
    def send(src, dst, kind, number, s, yx, z):
        pltpu.make_async_remote_copy(
            src_ref=src,
            dst_ref=dst,
            send_sem=ssem.at[kind],
            recv_sem=rsem.at[FIRST[kind] + number],
            device_id=(s, yx * 4 + z),
            device_id_type=pl.DeviceIdType.MESH,
        ).start()

    def keep(src, dst, kind, number):
        pltpu.make_async_copy(src, dst, rsem.at[FIRST[kind] + number]).start()

    def wait(ref, kind, number):
        pltpu.make_async_copy(ref, ref, rsem.at[FIRST[kind] + number]).wait()

    def sent(ref, kind):
        pltpu.make_async_copy(ref, ref, ssem.at[kind]).wait()

    s, yx, z = place()
    y, x = yx // 4, yx % 4

    barrier = pltpu.get_barrier_semaphore()

    def greet(core, chip, level):
        pl.semaphore_signal(
            barrier, inc=1, device_id=(core, chip * 4 + level), device_id_type=pl.DeviceIdType.MESH
        )

    def greet_plane(k, carry):
        greet((s + k % 2) % 2, around(yx, k // 2), z)
        return carry

    def greet_line(k, carry):
        greet((s + k // 4) % 2, yx, (z + k % 4) % 4)
        return carry

    lax.fori_loop(1, 4, greet_line, 0)
    lax.fori_loop(5, 8, greet_line, 0)
    lax.fori_loop(1, 32, greet_plane, 0)

    for r in range(8):
        pltpu.make_async_copy(queries.at[r], qbuf.at[r], csem.at[11 + r]).start()
        pltpu.make_async_copy(cache.at[r], cbuf.at[r], csem.at[r]).start()
    own_col = pl.multiple_of((s * 4 + z) * 128, 128)
    here = pl.ds(pl.multiple_of(z * 1792, 256), 1792)
    for q in range(4):
        rsend[q] = resid[:, q * 1792 : (q + 1) * 1792].astype(F32)
    pl.semaphore_wait(barrier, 37)

    def uv_part(t, h):
        return wuv.at[pl.ds(h * 256, 256), pl.ds(pl.multiple_of((s * 4 + t) * 128, 128), 128)]

    for h in range(2):
        keep(w_uv.at[pl.ds(h * 256, 256)], uv_part(z, h), W_UV, 2 * z + h)
        for k in (1, 3):
            send(w_uv.at[pl.ds(h * 256, 256)], uv_part(z, h), W_UV, 2 * z + h, s, yx, (z + k) % 4)

    parts = ((0, 1280), (1280, 512))

    def out_part(t, c):
        start, width = parts[c]
        return w_out.at[:, pl.ds(pl.multiple_of(t * 1792 + start, 256), width)]

    def wo_part(t, c):
        start, width = parts[c]
        return wo.at[pl.ds(pl.multiple_of((s * 4 + t) * 128, 128), 128), start : start + width]

    def send_out(c):
        for k in (1, 3, 2):
            t = (z + k) % 4
            send(out_part(t, c), wo_part(z, c), W_OUT, 2 * z + c, s, yx, t)

    def pass_out(c):
        for k in (1, 3, 2, 0):
            t = (z + k) % 4
            wait(wo_part(t, c), W_OUT, 2 * t + c)
            if k:
                send(wo_part(t, c), wo_part(t, c), OUT_OVER, c, 1 - s, yx, z)

    send_out(0)
    send(w_uv, wuv.at[:, pl.ds(own_col, 128)], UV_OVER, 0, 1 - s, yx, z)
    for c in range(2):
        keep(out_part(z, c), wo_part(z, c), W_OUT, 2 * z + c)
        send(out_part(z, c), wo_part(z, c), OUT_OVER, c, 1 - s, yx, z)
    keep(rsend.at[z], rrecv.at[z], RESID, 0)
    for k in (1, 3, 2):
        t = (z + k) % 4
        send(rsend.at[t], rrecv.at[z], RESID, 0, s, yx, t)

    row, col = iota((128, 128), 0), iota((128, 128), 1)
    head = ((row % 8) // 4) * 64 + (row // 8) * 4 + row % 4
    order = jnp.where(col == head, 1.0, 0.0).astype(BF)
    scale = 1.0 / math.sqrt(192)
    column = iota((128, 512), 1)

    def one(r):
        pltpu.make_async_copy(queries.at[r], qbuf.at[r], csem.at[11 + r]).wait()
        q = dot(order, qbuf[r], ((1,), (1,))).astype(BF)
        pltpu.make_async_copy(cache.at[r], cbuf.at[r], csem.at[r]).wait()
        scores = dot(q, cbuf[r]) * scale
        scores = jnp.where(column < lengths[r], scores, -1e30)
        weight = jnp.exp(scores - jnp.max(scores, axis=1, keepdims=True))
        total = jnp.sum(weight, axis=1, keepdims=True)
        latent = dot(weight.astype(BF), cbuf[r, 0:512], ((1,), (1,)))
        return (latent / total).reshape(16, 8, 512)

    def step(i, carry):
        late[i] = jnp.concatenate([one(2 * i), one(2 * i + 1)], axis=1).astype(BF)
        keep(late.at[i, yx], lrecv.at[yx, i], LATENT, 0)

        def out(k, carry):
            to = around(yx, k)
            send(late.at[i, to], lrecv.at[yx, i], LATENT, 0, s, to, z)
            return carry

        return lax.fori_loop(1, 16, out, carry)

    step(0, 0)
    for k, h in ((3, 0), (1, 1)):
        t = (z + k) % 4
        wait(uv_part(t, h), W_UV, 2 * t + h)
        send(uv_part(t, h), uv_part(t, h), W_UV, 2 * t + h, s, yx, (z + 4 - k) % 4)
    lax.fori_loop(1, 4, step, 0)

    pltpu.make_async_copy(w_gate, wg, csem.at[8]).start()
    pltpu.make_async_copy(w_up, wu, csem.at[9]).start()
    pltpu.make_async_copy(w_down, wd, csem.at[10]).start()
    slot_me = s * 16 + yx
    line_me = s * 4 + z

    half = pl.ds(pl.multiple_of(s * 512, 512), 512)
    for k, h in ((0, 0), (0, 1), (3, 1), (1, 0), (2, 0), (2, 1)):
        t = (z + k) % 4
        wait(uv_part(t, h), W_UV, 2 * t + h)
    for k in (1, 3, 2):
        at = pl.ds(pl.multiple_of((s * 4 + (z + k) % 4) * 128, 128), 128)
        send(wuv.at[:, at], wuv.at[:, at], UV_OVER, 0, 1 - s, yx, z)

    row, lane = iota((64, 128), 0), iota((64, 128), 1)

    gate_values = gates[...].astype(F32)
    table, used = jnp.zeros((64, 128), F32), jnp.zeros((64, 128), jnp.int32)
    for t in range(8):
        for k in range(4):
            slot = replicas[(t + k) % 2, expert_ids[k, t]]
            same = row // 2 == slot
            hit = same & (row % 2 == used)
            table = jnp.where(hit & (lane == line_me * 8 + t), 1.0, table)
            table = jnp.where(hit & (lane == 64 + line_me * 8 + t), gate_values[k : k + 1, t : t + 1], table)
            used = used + jnp.where(same, 1, 0)
    route[line_me] = table.astype(BF)

    def announce(k, carry):
        send(route.at[line_me], route.at[line_me], ROUTE, 0, (s + k // 4) % 2, yx, (z + k % 4) % 4)
        return carry

    lax.fori_loop(1, 8, announce, 0)
    wait(wuv.at[:, half], UV_OVER, 0)
    wait(lrecv, LATENT, 0)

    mine = iota((256, 1024), 0) % 8 == iota((256, 1024), 1) // 128
    pick = jnp.where(iota((32, 256), 1) // 8 == iota((32, 256), 0), 1.0, 0.0).astype(BF)

    def value(j, carry):
        some = lrecv[pl.ds(j * 4, 4)].reshape(256, 512)
        full = dot(some, wuv[...])
        own = jnp.where(mine, full, 0.0).astype(BF)
        vals[z, j] = dot(pick, own).astype(BF)
        for k in (1, 3):
            send(vals.at[z, j], vals.at[z, j], VALUE, 2 * z + j // 2, s, yx, (z + k) % 4)
        return carry

    lax.fori_loop(0, 4, value, 0)

    def values_of(k, h):
        t = (z + k) % 4
        wait(vals.at[t, pl.ds(2 * h, 2)], VALUE, 2 * t + h)
        return vals.at[t, pl.ds(2 * h, 2)], 2 * t + h

    pass_out(0)
    for k, h in ((3, 0), (1, 1)):
        ref, number = values_of(k, h)
        send(ref, ref, VALUE, number, s, yx, (z + 4 - k) % 4)
    send_out(1)
    wait(route.at[pl.ds(0, 7)], ROUTE, 0)
    a, b = iota((512, 512), 0), iota((512, 512), 1)
    deal = jnp.where(b == ((a % 16) // 2) * 64 + (a // 16) * 2 + a % 2, 1.0, 0.0).astype(BF)
    select[...] = dot(deal, route[...].reshape(512, 128)).astype(BF).reshape(2, 4, 4, 16, 128)
    for along in range(2):
        at = (x, y)[along]

        def column(t):
            return select.at[:, :, t] if along == 0 else select.at[:, t]

        keep(column(at), tables.at[along, at], TABLE, along)
        for k in (1, 3, 2):
            t = (at + k) % 4
            to = y * 4 + t if along == 0 else t * 4 + x
            send(column(t), tables.at[along, at], TABLE, along, s, to, z)
    wait(wo.at[half, 0:1280], OUT_OVER, 0)

    place_on = (x, y)
    buffers = ((orecv, tsend, trecv), (orecv_on, tsend_on, trecv_on))

    def of(ref, t, along, c):
        start, width = parts[c]
        cols = slice(start + along * width // 2, start + (along + 1) * width // 2)
        return ref.at[:, t, :, cols] if along == 0 else ref.at[t, :, :, cols]

    def chip(t, along):
        return y * 4 + t if along == 0 else t * 4 + x

    def project(c, p):
        def block(b, carry):
            at = pl.ds(pl.multiple_of(b * 256, 256), 256)
            got = dot(vals[pl.ds(2 * p, 2)].reshape(256, 1024), wo[:, at]).reshape(2, 16, 8, 256)
            osend[p, :, :, :, at] = jnp.concatenate([got[0], got[1]], axis=1).astype(BF).reshape(4, 4, 16, 256)
            return carry

        lax.fori_loop(parts[c][0] // 256, sum(parts[c]) // 256, block, 0)
        for along in range(2):
            at = place_on[along]
            number = 4 * c + 2 * p + along
            there = buffers[c][0].at[p, along, at]
            keep(of(osend.at[p], at, along, c), there, SUM, number)
            for k in (1, 3, 2):
                t = (at + k) % 4
                send(of(osend.at[p], t, along, c), there, SUM, number, s, chip(t, along), z)

    def sum_on(c, p):
        first, middle, last = buffers[c]
        for along in range(2):
            number = 4 * c + 2 * p + along
            wait(first.at[p, along], SUM, number)
            got = [first[p, along, i].astype(F32) for i in range(4)]
            middle[p, along] = ((got[0] + got[1]) + (got[2] + got[3])).astype(BF)
            at = place_on[1 - along]
            there = last.at[p, along, at]
            keep(middle.at[p, along, at], there, SUM_ON, number)
            for k in (1, 3, 2):
                t = (at + k) % 4
                send(middle.at[p, along, t], there, SUM_ON, number, s, chip(t, 1 - along), z)

    def row_cols(t, c):
        start, width = parts[c]
        return pl.ds(pl.multiple_of(t * 1792 + start, 256), width)

    def finish_sum(c):
        start, width = parts[c]
        last = buffers[c][2]
        for pp in range(2):
            p = (z // 2 + pp) % 2
            line = pl.ds(pl.multiple_of(p * 16, 16), 16)
            for along in range(2):
                wait(last.at[p, along], SUM_ON, 4 * c + 2 * p + along)
                got = [last[p, along, i].astype(F32) for i in range(4)]
                cols = slice(start + along * width // 2, start + (along + 1) * width // 2)
                base = jnp.concatenate([rrecv[2 * p, :, cols], rrecv[2 * p + 1, :, cols]], axis=0)
                total = base + ((got[0] + got[1]) + (got[2] + got[3]))
                at = pl.ds(pl.multiple_of(z * 1792 + start + along * width // 2, 128), width // 2)
                gathered[s, line, at] = total.astype(BF)
        mine = gathered.at[s, :, row_cols(z, c)]
        for k in (1, 3, 2):
            send(mine, mine, SLICE, c, s, yx, (z + k) % 4)
        for k in (0, 1, 3, 2) if c == 1 else (0,):
            send(mine, mine, ROWS_OVER, c, 1 - s, yx, (z + k) % 4)

    def pass_rows(c):
        width = parts[c][1]
        wait(gathered.at[s, :, pl.ds(0, 3 * width)], SLICE, c)
        for k in (1, 3, 2) if c == 0 else ():
            ref = gathered.at[s, :, row_cols((z + k) % 4, c)]
            send(ref, ref, ROWS_OVER, c, 1 - s, yx, z)

    wait(rrecv, RESID, 0)
    own_p = z // 2
    values_of(1, 0)
    values_of(3, 1)
    project(0, own_p)
    values_of(2, 0)
    values_of(2, 1)
    project(0, 1 - own_p)
    sum_on(0, own_p)
    sum_on(0, 1 - own_p)
    pass_out(1)
    wait(wo.at[half, 1280:1792], OUT_OVER, 1)
    project(1, own_p)
    project(1, 1 - own_p)
    finish_sum(0)
    sum_on(1, own_p)
    sum_on(1, 1 - own_p)
    pass_rows(0)
    finish_sum(1)
    pass_rows(1)

    def norm(core, p):
        stream = gathered[core, pl.ds(pl.multiple_of(p * 16, 16), 16)].astype(F32)
        mean = jnp.mean(stream * stream, axis=1, keepdims=True)
        at = pl.ds(pl.multiple_of(core * 32 + p * 16, 16), 16)
        normed[at] = (stream * lax.rsqrt(mean + 1e-06) * gain[...]).astype(BF)

    norm(s, 0)
    norm(s, 1)
    wait(gathered.at[s, :, pl.ds(0, 5120)], ROWS_OVER, 0)
    wait(gathered.at[s, :, pl.ds(0, 2048)], ROWS_OVER, 1)
    norm(1 - s, 0)
    norm(1 - s, 1)

    land = pl.ds(pl.multiple_of(yx * 16, 16), 16)
    flat = select[...].reshape(512, 128)[:, 0:64]

    def slice_cols(t, c, core):
        start, width = ((0, 128), (256, 256))[c]
        return pl.ds(pl.multiple_of(t * 768 + start + core * width, 128), width)

    def whole_cols(t, c):
        start, width = ((0, 256), (256, 512))[c]
        return pl.ds(pl.multiple_of(t * 768 + start, 256), width)

    def rest_cols(core, along, c):
        return pl.ds(pl.multiple_of(3072 + core * 2048 + along * 1024 + c * 512, 512), 512)

    def deliver_slice(c, buffer):
        cols = slice_cols(z, c, s)
        width = (128, 256)[c]
        buffer[...] = dot(flat, normed[:, cols]).astype(BF).reshape(32, 16, width)
        place_in = rows.at[y, x, :, cols]
        keep(buffer.at[slot_me], place_in, PICK, c)

        def out(k, carry):
            to, core = around(yx, k // 2), (s + k % 2) % 2
            send(buffer.at[core * 16 + to], place_in, PICK, c, core, to, z)
            return carry

        lax.fori_loop(1, 32, out, 0)

    def share_lines(c):
        for along in range(2):
            at = place_on[along]
            source = normed.at[:, rest_cols(s, along, c)]
            keep(source, lines.at[along, c, at], LINES, 2 * along + c)
            for k in (1, 3, 2):
                send(source, lines.at[along, c, at], LINES, 2 * along + c, s, chip((at + k) % 4, along), z)

    def deliver_rest(c):
        for along in range(2):
            wait(lines.at[along, c], LINES, 2 * along + c)
            for t in range(4):
                table = tables[along, t].reshape(128, 128)[:, 0:64]
                rest[along, c, :, :, t] = dot(table, lines[along, c, t]).astype(BF).reshape(2, 4, 16, 512)
            cols = rest_cols(s, along, c)
            place_in = rows.at[y, :, :, cols] if along == 0 else rows.at[:, x, :, cols]
            at = place_on[1 - along]
            keep(rest.at[along, c, s, at], place_in, PICK_REST, 2 * along + c)
            for k in (1, 3, 2):
                t = (at + k) % 4
                for core in range(2):
                    send(rest.at[along, c, core, t], place_in, PICK_REST, 2 * along + c, core, chip(t, 1 - along), z)
            send(rest.at[along, c, 1 - s, at], place_in, PICK_REST, 2 * along + c, 1 - s, yx, z)

    def spread_part(t, c, h):
        return rows.at[2 * h : 2 * h + 2, :, :, whole_cols(t, c)], 8 * c + 2 * t + h

    def spread(c):
        wait(rows.at[:, :, :, whole_cols(z, c)], PICK, c)
        for h in range(2):
            ref, number = spread_part(z, c, h)
            for k in (1, 3):
                send(ref, ref, GATHER, number, s, yx, (z + k) % 4)

    def spread_on(c):
        for k, h in ((3, 0), (1, 1)):
            ref, number = spread_part((z + k) % 4, c, h)
            wait(ref, GATHER, number)
            send(ref, ref, GATHER, number, s, yx, (z + 4 - k) % 4)

    wait(tables.at[0], TABLE, 0)
    wait(tables.at[1], TABLE, 1)
    deliver_slice(0, picked)
    share_lines(0)
    deliver_slice(1, picked_on)
    share_lines(1)
    spread(0)
    deliver_rest(0)
    spread(1)
    spread_on(0)
    deliver_rest(1)
    spread_on(1)

    pltpu.make_async_copy(w_gate, wg, csem.at[8]).wait()
    pltpu.make_async_copy(w_up, wu, csem.at[9]).wait()
    acc[...] = jnp.zeros_like(acc)

    def enter(at):
        some = rows[:, :, :, at].reshape(256, at.size)
        acc[0] += dot(some, wg[at])
        acc[1] += dot(some, wu[at])

    enter(whole_cols(z, 0))
    enter(whole_cols(z, 1))
    for c in range(2):
        for k in (1, 3, 2):
            t = (z + k) % 4
            for h in range(2):
                if (k, h) not in ((3, 0), (1, 1)):
                    ref, number = spread_part(t, c, h)
                    wait(ref, GATHER, number)
            enter(whole_cols(t, c))
        for along in range(2):
            wait(rows.at[:, :, :, pl.ds(0, 1024)], PICK_REST, 2 * along + c)
            for core in range(2):
                enter(rest_cols(core, along, c))
    gate = acc[0]
    hidden[...] = (gate * jax.nn.sigmoid(gate) * acc[1]).astype(BF)
    pltpu.make_async_copy(w_down, wd, csem.at[10]).wait()

    for k in (1, 3, 2, 0):
        t = (z + k) % 4
        got = dot(hidden[...], wd[:, pl.ds(pl.multiple_of(t * 768, 256), 768)]).astype(BF)
        if k == 0:
            yrecv[z] = got
        else:
            ysend[t] = got
    for j in range(4):
        some = pl.ds(pl.multiple_of(((y + j) % 4) * 64, 64), 64)
        for k in (1, 3, 2):
            t = (z + k) % 4
            send(ysend.at[t, some], yrecv.at[z, some], PIECE, (y + j) % 4, s, yx, t)

    for c in range(2):
        for along in range(2):
            at = place_on[1 - along]

            def part_of(core, t):
                source = bsend.at[core, along, c]
                return source.at[t] if along == 0 else source.at[:, t]

            for core in range(2):
                got = dot(hidden[...], wd[:, 3072 + core * 2048 + along * 1024 + c * 512 :][:, 0:512])
                bsend[core, along, c] = got.astype(BF).reshape(4, 4, 16, 512)
            land_in = brecv.at[along, c, s, at]
            keep(part_of(s, at), land_in, HOME, 2 * along + c)
            for k in (1, 3, 2):
                t = (at + k) % 4
                for core in range(2):
                    send(part_of(core, t), land_in, HOME, 2 * along + c, core, chip(t, 1 - along), z)
            send(part_of(1 - s, at), land_in, HOME, 2 * along + c, 1 - s, yx, z)

    def give(core, to):
        src = asend.at[core, pl.ds(pl.multiple_of(to * 16, 16), 16)]
        send(src, back.at[slot_me], BACK, 0, core, to, z)

    def home(c):
        for along in range(2):
            wait(brecv.at[along, c], HOME, 2 * along + c)
            for t in range(4):
                got = brecv[along, c, :, :, t].reshape(128, 512)
                summed = dot(tables[along, t].reshape(128, 128), got, ((0,), (0,)))[64:128]
                tsend_home[along, c, t] = summed.astype(BF)
            at = place_on[along]
            keep(tsend_home.at[along, c, at], trecv_home.at[along, c, at], HOME_ON, 2 * along + c)
            for k in (1, 3, 2):
                t = (at + k) % 4
                send(
                    tsend_home.at[along, c, t], trecv_home.at[along, c, at],
                    HOME_ON, 2 * along + c, s, chip(t, along), z,
                )

    def slices(j):
        to_y = (y + j) % 4
        some = pl.ds(pl.multiple_of(to_y * 64, 64), 64)
        wait(yrecv.at[pl.ds(0, 3), some], PIECE, to_y)
        got = [yrecv[q, some].astype(F32) for q in range(4)]
        total = ((got[0] + got[1]) + (got[2] + got[3])).astype(BF)
        for core in range(2):
            asend[core, some] = total[:, core * 384 : core * 384 + 384]
        if j == 0:
            keep(asend.at[s, land], back.at[slot_me], BACK, 0)
            give(1 - s, yx)
        for core in range(2):
            for k in range(1 if j == 0 else 0, 4):
                give(core, to_y * 4 + (x + k) % 4)

    slices(0)
    home(0)
    slices(1)
    slices(2)
    home(1)
    slices(3)

    result_cols = (slice(0, 512), slice(512, 1024), slice(1024, 1280))

    def finish(n):
        cols = result_cols[n]
        keep(fsend.at[line_me, :, cols], frecv.at[line_me, :, cols], RESULT, n)

        def out(k, carry):
            core, to = (s + k // 4) % 2, (z + k % 4) % 4
            send(fsend.at[core * 4 + to, :, cols], frecv.at[line_me, :, cols], RESULT, n, core, yx, to)
            return carry

        lax.fori_loop(1, 8, out, 0)

    def finish_rest(c):
        total = []
        for along in range(2):
            wait(trecv_home.at[along, c], HOME_ON, 2 * along + c)
            got = [trecv_home[along, c, i].astype(F32) for i in range(4)]
            total.append(((got[0] + got[1]) + (got[2] + got[3])).reshape(8, 8, 512))
        fsend[:, :, result_cols[c]] = jnp.concatenate(total, axis=1).astype(BF)
        finish(c)

    def finish_slices():
        wait(back, BACK, 0)
        total = dot(select[...].reshape(512, 128), back[...].reshape(512, 384), ((0,), (0,)))[64:128]
        low = total[:, 0:256].reshape(8, 8, 256)
        high = jnp.concatenate([total[:, 256:384], jnp.zeros((64, 128), F32)], axis=1).reshape(8, 8, 256)
        fsend[:, :, 1024:1280] = jnp.concatenate([low, high], axis=1).astype(BF)
        finish(2)

    finish_rest(0)
    finish_rest(1)
    finish_slices()

    def write(first, width, moe):
        at = slice(first, first + width)
        stream = gathered[s, :, at].astype(F32)
        own = jnp.zeros((8, width), F32)
        for t in range(4):
            own = jnp.where(z == t, stream[t * 8 : t * 8 + 8], own)
        both[0, :, at] = own.astype(BF)
        both[1, :, at] = (own + moe).astype(BF)

    for c in range(2):
        wait(frecv.at[:, :, result_cols[c]], RESULT, c)
        for core in range(2):
            got = [frecv[core * 4 + t, :, result_cols[c]].astype(F32) for t in range(4)]
            total = (got[0] + got[1]) + (got[2] + got[3])
            write(3072 + core * 2048 + c * 512, 512, total[0:8])
            write(3072 + core * 2048 + 1024 + c * 512, 512, total[8:16])
    wait(frecv.at[:, :, result_cols[2]], RESULT, 2)
    for j in range(8):
        got = frecv[(j % 2) * 4 + j // 2, :, 1024:1280].astype(F32)
        write(j * 384, 256, got[0:8])
        write(j * 384 + 256, 128, got[8:16, 0:128])

    for ref, kind in (
        (wuv.at[:, pl.ds(0, 384)], W_UV),
        (wo.at[pl.ds(0, 384)], W_OUT),
        (rsend.at[pl.ds(0, 3)], RESID),
        (wuv.at[:, half], UV_OVER),
        (wo.at[half], OUT_OVER),
        (late.at[:, pl.ds(0, 15)], LATENT),
        (vals.at[pl.ds(0, 3)], VALUE),
        (orecv.at[:, :, pl.ds(0, 3)], SUM),
        (orecv_on.at[:, :, pl.ds(0, 3)], SUM),
        (tsend.at[:, :, pl.ds(0, 3)], SUM_ON),
        (tsend_on.at[:, :, pl.ds(0, 3)], SUM_ON),
        (gathered.at[s, :, pl.ds(0, 5376)], SLICE),
        (gathered.at[s], ROWS_OVER),
        (route.at[pl.ds(0, 7)], ROUTE),
        (tables.at[:, pl.ds(0, 3)], TABLE),
        (picked.at[pl.ds(0, 31)], PICK),
        (picked_on.at[pl.ds(0, 31)], PICK),
        (lines.at[:, :, pl.ds(0, 3)], LINES),
        (rest.at[:, :, 0], PICK_REST),
        (rest.at[:, :, 1, pl.ds(0, 3)], PICK_REST),
        (rows.at[:, :, :, pl.ds(0, 2304)], GATHER),
        (ysend.at[pl.ds(0, 3)], PIECE),
        (back.at[pl.ds(0, 31)], BACK),
        (brecv.at[:, :, 0], HOME),
        (brecv.at[:, :, 1, pl.ds(0, 3)], HOME),
        (tsend_home.at[:, :, pl.ds(0, 3)], HOME_ON),
        (fsend.at[pl.ds(0, 7)], RESULT),
    ):
        sent(ref, kind)


VMEM = pl.BlockSpec(memory_space=pltpu.VMEM)
SMEM = pl.BlockSpec(memory_space=pltpu.SMEM)
ANY = pl.BlockSpec(memory_space=pl.ANY)


def local(
    queries, cache, lengths, w_uv, w_out, resid, norm_gain, expert_ids, gate_weights, replica_slot, w_gate, w_up, w_down
):
    scratch = [
        pltpu.VMEM((8, 576, 512), BF),
        pltpu.VMEM((8, 576, 128), BF),
        pltpu.VMEM((4, 16, 16, 512), BF),
        pltpu.VMEM((16, 4, 16, 512), BF),
        pltpu.VMEM((512, 1024), BF),
        pltpu.VMEM((1024, 1792), BF),
        pltpu.VMEM((4, 4, 32, 1024), BF),
        pltpu.VMEM((2, 4, 4, 16, 1792), BF),
        pltpu.VMEM((2, 2, 4, 4, 16, 640), BF),
        pltpu.VMEM((2, 2, 4, 4, 16, 256), BF),
        pltpu.VMEM((2, 2, 4, 16, 640), BF),
        pltpu.VMEM((2, 2, 4, 16, 256), BF),
        pltpu.VMEM((2, 2, 4, 16, 640), BF),
        pltpu.VMEM((2, 2, 4, 16, 256), BF),
        pltpu.VMEM((4, 8, 1792), F32),
        pltpu.VMEM((4, 8, 1792), F32),
        pltpu.VMEM((2, 32, 7168), BF),
        pltpu.VMEM((7168, 256), BF),
        pltpu.VMEM((7168, 256), BF),
        pltpu.VMEM((256, 7168), BF),
        pltpu.VMEM((8, 64, 128), BF),
        pltpu.VMEM((64, 7168), BF),
        pltpu.VMEM((2, 4, 4, 16, 128), BF),
        pltpu.VMEM((2, 4, 2, 4, 16, 128), BF),
        pltpu.VMEM((32, 16, 128), BF),
        pltpu.VMEM((32, 16, 256), BF),
        pltpu.VMEM((2, 2, 4, 64, 512), BF),
        pltpu.VMEM((2, 2, 2, 4, 4, 16, 512), BF),
        pltpu.VMEM((4, 4, 16, 7168), BF),
        pltpu.VMEM((2, 256, 256), F32),
        pltpu.VMEM((256, 256), BF),
        pltpu.VMEM((4, 256, 768), BF),
        pltpu.VMEM((4, 256, 768), BF),
        pltpu.VMEM((2, 2, 2, 4, 4, 16, 512), BF),
        pltpu.VMEM((2, 2, 2, 4, 4, 16, 512), BF),
        pltpu.VMEM((2, 2, 4, 64, 512), BF),
        pltpu.VMEM((2, 2, 4, 64, 512), BF),
        pltpu.VMEM((2, 256, 384), BF),
        pltpu.VMEM((32, 16, 384), BF),
        pltpu.VMEM((8, 16, 1280), BF),
        pltpu.VMEM((8, 16, 1280), BF),
    ] + [pltpu.SemaphoreType.DMA((n,)) for n in (19, len(PARTS), sum(PARTS))]
    both = pl.pallas_call(
        kernel,
        out_shape=jax.ShapeDtypeStruct((2, 8, 7168), BF),
        in_specs=[SMEM, SMEM, VMEM, SMEM, ANY, ANY, ANY, ANY, VMEM, VMEM, ANY, ANY, ANY],
        out_specs=VMEM,
        scratch_shapes=scratch,
        compiler_params=pltpu.CompilerParams(collective_id=0, has_side_effects=True, vmem_limit_bytes=60 * MB),
        name="layer",
    )(
        lengths,
        expert_ids.T,
        gate_weights.T,
        replica_slot.T,
        jnp.swapaxes(queries, 1, 2),
        jnp.swapaxes(cache, 1, 2),
        w_uv[0],
        w_out,
        resid,
        norm_gain[None],
        w_gate[0],
        w_up[0],
        w_down[0],
    )
    return both[0], both[1]


def solution(mesh):
    return jax.shard_map(
        local,
        mesh=mesh,
        in_specs=(
            P(("side", "dev"), None, None),
            P(("side", "dev"), None, None),
            P(("side", "dev")),
            P(("side", "dev"), None, None),
            P(("side", "dev"), None),
            P(("side", "dev"), None),
            P(),
            P(("side", "dev"), None),
            P(("side", "dev"), None),
            P(),
            P(("side", "dev"), None, None),
            P(("side", "dev"), None, None),
            P(("side", "dev"), None, None),
        ),
        out_specs=(P(("side", "dev"), None), P(("side", "dev"), None)),
        check_vma=False,
    )
```

```python
import functools
import math

import jax
import jax.numpy as jnp
from jax import lax
from jax.experimental import pallas as pl
from jax.experimental.pallas import tpu as pltpu
from jax.sharding import PartitionSpec as P

GROUP = 4
BF = jnp.bfloat16
F32 = jnp.float32
MB = 1 << 20


def place():
    s = lax.axis_index("side")
    dev = lax.axis_index("dev")
    return s, dev // 4, dev % 4


def dot(a, b, dims=((1,), (0,))):
    return lax.dot_general(a, b, (dims, ((), ())), preferred_element_type=F32)


def around(yx, k):
    return ((yx // 4 + k // 4) % 4) * 4 + (yx % 4 + k % 4) % 4


def iota(shape, dim):
    return lax.broadcasted_iota(jnp.int32, shape, dim)


W_UV, W_OUT, RESID, UV_OVER, OUT_OVER, LATENT, VALUE, SUM, SLICE, ROWS_OVER, ROUTE, PICK, PICK_REST, GATHER, PIECE, BACK, RESULT, SUM_ON, TABLE, LINES, HOME, HOME_ON = range(22)
PARTS = (8, 8, 1, 1, 2, 1, 8, 8, 2, 2, 1, 2, 4, 16, 4, 1, 3, 8, 2, 4, 4, 4)
FIRST = tuple(sum(PARTS[:i]) for i in range(len(PARTS)))


def kernel(
    lengths, expert_ids, gates, replicas,
    queries, cache, w_uv, w_out, resid, gain, w_gate, w_up, w_down,
    both,
    cbuf, qbuf, late, lrecv, wuv, wo, vals, osend, orecv, orecv_on, tsend, tsend_on, trecv, trecv_on, rsend, rrecv, gathered,
    wg, wu, wd, route, normed, select, tables, picked, picked_on, lines, rest, rows, acc, hidden,
    ysend, yrecv, bsend, brecv, tsend_home, trecv_home, asend, back, fsend, frecv,
    csem, ssem, rsem,
):
    def send(src, dst, kind, number, s, yx, z):
        pltpu.make_async_remote_copy(
            src_ref=src,
            dst_ref=dst,
            send_sem=ssem.at[kind],
            recv_sem=rsem.at[FIRST[kind] + number],
            device_id=(s, yx * 4 + z),
            device_id_type=pl.DeviceIdType.MESH,
        ).start()

    def keep(src, dst, kind, number):
        pltpu.make_async_copy(src, dst, rsem.at[FIRST[kind] + number]).start()

    def wait(ref, kind, number):
        pltpu.make_async_copy(ref, ref, rsem.at[FIRST[kind] + number]).wait()

    def sent(ref, kind):
        pltpu.make_async_copy(ref, ref, ssem.at[kind]).wait()

    s, yx, z = place()
    y, x = yx // 4, yx % 4

    barrier = pltpu.get_barrier_semaphore()

    def greet(core, chip, level):
        pl.semaphore_signal(
            barrier, inc=1, device_id=(core, chip * 4 + level), device_id_type=pl.DeviceIdType.MESH
        )

    def greet_plane(k, carry):
        greet((s + k % 2) % 2, around(yx, k // 2), z)
        return carry

    def greet_line(k, carry):
        greet((s + k // 4) % 2, yx, (z + k % 4) % 4)
        return carry

    lax.fori_loop(1, 4, greet_line, 0)
    lax.fori_loop(5, 8, greet_line, 0)
    lax.fori_loop(1, 32, greet_plane, 0)

    for r in range(8):
        pltpu.make_async_copy(queries.at[r], qbuf.at[r], csem.at[11 + r]).start()
        pltpu.make_async_copy(cache.at[r], cbuf.at[r], csem.at[r]).start()
    own_col = pl.multiple_of((s * 4 + z) * 128, 128)
    here = pl.ds(pl.multiple_of(z * 1792, 256), 1792)
    for q in range(4):
        rsend[q] = resid[:, q * 1792 : (q + 1) * 1792].astype(F32)
    pl.semaphore_wait(barrier, 37)

    def uv_part(t, h):
        return wuv.at[pl.ds(h * 256, 256), pl.ds(pl.multiple_of((s * 4 + t) * 128, 128), 128)]

    for h in range(2):
        keep(w_uv.at[pl.ds(h * 256, 256)], uv_part(z, h), W_UV, 2 * z + h)
        for k in (1, 3):
            send(w_uv.at[pl.ds(h * 256, 256)], uv_part(z, h), W_UV, 2 * z + h, s, yx, (z + k) % 4)

    parts = ((0, 1280), (1280, 512))

    def out_part(t, c):
        start, width = parts[c]
        return w_out.at[:, pl.ds(pl.multiple_of(t * 1792 + start, 256), width)]

    def wo_part(t, c):
        start, width = parts[c]
        return wo.at[pl.ds(pl.multiple_of((s * 4 + t) * 128, 128), 128), start : start + width]

    def send_out(c):
        for k in (1, 3, 2):
            t = (z + k) % 4
            send(out_part(t, c), wo_part(z, c), W_OUT, 2 * z + c, s, yx, t)

    def pass_out(c):
        for k in (1, 3, 2, 0):
            t = (z + k) % 4
            wait(wo_part(t, c), W_OUT, 2 * t + c)
            if k:
                send(wo_part(t, c), wo_part(t, c), OUT_OVER, c, 1 - s, yx, z)

    send_out(0)
    send(w_uv, wuv.at[:, pl.ds(own_col, 128)], UV_OVER, 0, 1 - s, yx, z)
    for c in range(2):
        keep(out_part(z, c), wo_part(z, c), W_OUT, 2 * z + c)
        send(out_part(z, c), wo_part(z, c), OUT_OVER, c, 1 - s, yx, z)
    keep(rsend.at[z], rrecv.at[z], RESID, 0)
    for k in (1, 3, 2):
        t = (z + k) % 4
        send(rsend.at[t], rrecv.at[z], RESID, 0, s, yx, t)

    row, col = iota((128, 128), 0), iota((128, 128), 1)
    head = ((row % 8) // 4) * 64 + (row // 8) * 4 + row % 4
    order = jnp.where(col == head, 1.0, 0.0).astype(BF)
    scale = 1.0 / math.sqrt(192)
    column = iota((128, 512), 1)

    def one(r):
        pltpu.make_async_copy(queries.at[r], qbuf.at[r], csem.at[11 + r]).wait()
        q = dot(order, qbuf[r], ((1,), (1,))).astype(BF)
        pltpu.make_async_copy(cache.at[r], cbuf.at[r], csem.at[r]).wait()
        scores = dot(q, cbuf[r]) * scale
        scores = jnp.where(column < lengths[r], scores, -1e30)
        weight = jnp.exp(scores - jnp.max(scores, axis=1, keepdims=True))
        total = jnp.sum(weight, axis=1, keepdims=True)
        latent = dot(weight.astype(BF), cbuf[r, 0:512], ((1,), (1,)))
        return (latent / total).reshape(16, 8, 512)

    def step(i, carry):
        late[i] = jnp.concatenate([one(2 * i), one(2 * i + 1)], axis=1).astype(BF)
        keep(late.at[i, yx], lrecv.at[yx, i], LATENT, 0)

        def out(k, carry):
            to = around(yx, k)
            send(late.at[i, to], lrecv.at[yx, i], LATENT, 0, s, to, z)
            return carry

        return lax.fori_loop(1, 16, out, carry)

    step(0, 0)
    for k, h in ((3, 0), (1, 1)):
        t = (z + k) % 4
        wait(uv_part(t, h), W_UV, 2 * t + h)
        send(uv_part(t, h), uv_part(t, h), W_UV, 2 * t + h, s, yx, (z + 4 - k) % 4)
    lax.fori_loop(1, 4, step, 0)

    pltpu.make_async_copy(w_gate, wg, csem.at[8]).start()
    pltpu.make_async_copy(w_up, wu, csem.at[9]).start()
    pltpu.make_async_copy(w_down, wd, csem.at[10]).start()
    slot_me = s * 16 + yx
    line_me = s * 4 + z

    half = pl.ds(pl.multiple_of(s * 512, 512), 512)
    for k, h in ((0, 0), (0, 1), (3, 1), (1, 0), (2, 0), (2, 1)):
        t = (z + k) % 4
        wait(uv_part(t, h), W_UV, 2 * t + h)
    for k in (1, 3, 2):
        at = pl.ds(pl.multiple_of((s * 4 + (z + k) % 4) * 128, 128), 128)
        send(wuv.at[:, at], wuv.at[:, at], UV_OVER, 0, 1 - s, yx, z)

    row, lane = iota((64, 128), 0), iota((64, 128), 1)

    gate_values = gates[...].astype(F32)
    table, used = jnp.zeros((64, 128), F32), jnp.zeros((64, 128), jnp.int32)
    for t in range(8):
        for k in range(4):
            slot = replicas[(t + k) % 2, expert_ids[k, t]]
            same = row // 2 == slot
            hit = same & (row % 2 == used)
            table = jnp.where(hit & (lane == line_me * 8 + t), 1.0, table)
            table = jnp.where(hit & (lane == 64 + line_me * 8 + t), gate_values[k : k + 1, t : t + 1], table)
            used = used + jnp.where(same, 1, 0)
    route[line_me] = table.astype(BF)

    def announce(k, carry):
        send(route.at[line_me], route.at[line_me], ROUTE, 0, (s + k // 4) % 2, yx, (z + k % 4) % 4)
        return carry

    lax.fori_loop(1, 8, announce, 0)
    wait(wuv.at[:, half], UV_OVER, 0)
    wait(lrecv, LATENT, 0)

    mine = iota((256, 1024), 0) % 8 == iota((256, 1024), 1) // 128
    pick = jnp.where(iota((32, 256), 1) // 8 == iota((32, 256), 0), 1.0, 0.0).astype(BF)

    def value(j, carry):
        some = lrecv[pl.ds(j * 4, 4)].reshape(256, 512)
        full = dot(some, wuv[...])
        own = jnp.where(mine, full, 0.0).astype(BF)
        vals[z, j] = dot(pick, own).astype(BF)
        for k in (1, 3):
            send(vals.at[z, j], vals.at[z, j], VALUE, 2 * z + j // 2, s, yx, (z + k) % 4)
        return carry

    lax.fori_loop(0, 4, value, 0)

    def values_of(k, h):
        t = (z + k) % 4
        wait(vals.at[t, pl.ds(2 * h, 2)], VALUE, 2 * t + h)
        return vals.at[t, pl.ds(2 * h, 2)], 2 * t + h

    pass_out(0)
    for k, h in ((3, 0), (1, 1)):
        ref, number = values_of(k, h)
        send(ref, ref, VALUE, number, s, yx, (z + 4 - k) % 4)
    send_out(1)
    wait(route.at[pl.ds(0, 7)], ROUTE, 0)
    a, b = iota((512, 512), 0), iota((512, 512), 1)
    deal = jnp.where(b == ((a % 16) // 2) * 64 + (a // 16) * 2 + a % 2, 1.0, 0.0).astype(BF)
    select[...] = dot(deal, route[...].reshape(512, 128)).astype(BF).reshape(2, 4, 4, 16, 128)
    for along in range(2):
        at = (x, y)[along]

        def column(t):
            return select.at[:, :, t] if along == 0 else select.at[:, t]

        keep(column(at), tables.at[along, at], TABLE, along)
        for k in (1, 3, 2):
            t = (at + k) % 4
            to = y * 4 + t if along == 0 else t * 4 + x
            send(column(t), tables.at[along, at], TABLE, along, s, to, z)
    wait(wo.at[half, 0:1280], OUT_OVER, 0)

    place_on = (x, y)
    buffers = ((orecv, tsend, trecv), (orecv_on, tsend_on, trecv_on))

    def of(ref, t, along, c):
        start, width = parts[c]
        cols = slice(start + along * width // 2, start + (along + 1) * width // 2)
        return ref.at[:, t, :, cols] if along == 0 else ref.at[t, :, :, cols]

    def chip(t, along):
        return y * 4 + t if along == 0 else t * 4 + x

    def project(c, p):
        def block(b, carry):
            at = pl.ds(pl.multiple_of(b * 256, 256), 256)
            got = dot(vals[pl.ds(2 * p, 2)].reshape(256, 1024), wo[:, at]).reshape(2, 16, 8, 256)
            osend[p, :, :, :, at] = jnp.concatenate([got[0], got[1]], axis=1).astype(BF).reshape(4, 4, 16, 256)
            return carry

        lax.fori_loop(parts[c][0] // 256, sum(parts[c]) // 256, block, 0)
        for along in range(2):
            at = place_on[along]
            number = 4 * c + 2 * p + along
            there = buffers[c][0].at[p, along, at]
            keep(of(osend.at[p], at, along, c), there, SUM, number)
            for k in (1, 3, 2):
                t = (at + k) % 4
                send(of(osend.at[p], t, along, c), there, SUM, number, s, chip(t, along), z)

    def sum_on(c, p):
        first, middle, last = buffers[c]
        for along in range(2):
            number = 4 * c + 2 * p + along
            wait(first.at[p, along], SUM, number)
            got = [first[p, along, i].astype(F32) for i in range(4)]
            middle[p, along] = ((got[0] + got[1]) + (got[2] + got[3])).astype(BF)
            at = place_on[1 - along]
            there = last.at[p, along, at]
            keep(middle.at[p, along, at], there, SUM_ON, number)
            for k in (1, 3, 2):
                t = (at + k) % 4
                send(middle.at[p, along, t], there, SUM_ON, number, s, chip(t, 1 - along), z)

    def row_cols(t, c):
        start, width = parts[c]
        return pl.ds(pl.multiple_of(t * 1792 + start, 256), width)

    def finish_sum(c):
        start, width = parts[c]
        last = buffers[c][2]
        for pp in range(2):
            p = (z // 2 + pp) % 2
            line = pl.ds(pl.multiple_of(p * 16, 16), 16)
            for along in range(2):
                wait(last.at[p, along], SUM_ON, 4 * c + 2 * p + along)
                got = [last[p, along, i].astype(F32) for i in range(4)]
                cols = slice(start + along * width // 2, start + (along + 1) * width // 2)
                base = jnp.concatenate([rrecv[2 * p, :, cols], rrecv[2 * p + 1, :, cols]], axis=0)
                total = base + ((got[0] + got[1]) + (got[2] + got[3]))
                at = pl.ds(pl.multiple_of(z * 1792 + start + along * width // 2, 128), width // 2)
                gathered[s, line, at] = total.astype(BF)
        mine = gathered.at[s, :, row_cols(z, c)]
        for k in (1, 3, 2):
            send(mine, mine, SLICE, c, s, yx, (z + k) % 4)
        for k in (0, 1, 3, 2) if c == 1 else (0,):
            send(mine, mine, ROWS_OVER, c, 1 - s, yx, (z + k) % 4)

    def pass_rows(c):
        width = parts[c][1]
        wait(gathered.at[s, :, pl.ds(0, 3 * width)], SLICE, c)
        for k in (1, 3, 2) if c == 0 else ():
            ref = gathered.at[s, :, row_cols((z + k) % 4, c)]
            send(ref, ref, ROWS_OVER, c, 1 - s, yx, z)

    wait(rrecv, RESID, 0)
    own_p = z // 2
    values_of(1, 0)
    values_of(3, 1)
    project(0, own_p)
    values_of(2, 0)
    values_of(2, 1)
    project(0, 1 - own_p)
    sum_on(0, own_p)
    sum_on(0, 1 - own_p)
    pass_out(1)
    wait(wo.at[half, 1280:1792], OUT_OVER, 1)
    project(1, own_p)
    project(1, 1 - own_p)
    finish_sum(0)
    sum_on(1, own_p)
    sum_on(1, 1 - own_p)
    pass_rows(0)
    finish_sum(1)
    pass_rows(1)

    def norm(core, p):
        stream = gathered[core, pl.ds(pl.multiple_of(p * 16, 16), 16)].astype(F32)
        mean = jnp.mean(stream * stream, axis=1, keepdims=True)
        at = pl.ds(pl.multiple_of(core * 32 + p * 16, 16), 16)
        normed[at] = (stream * lax.rsqrt(mean + 1e-06) * gain[...]).astype(BF)

    norm(s, 0)
    norm(s, 1)
    wait(gathered.at[s, :, pl.ds(0, 5120)], ROWS_OVER, 0)
    wait(gathered.at[s, :, pl.ds(0, 2048)], ROWS_OVER, 1)
    norm(1 - s, 0)
    norm(1 - s, 1)

    land = pl.ds(pl.multiple_of(yx * 16, 16), 16)
    flat = select[...].reshape(512, 128)[:, 0:64]

    def slice_cols(t, c, core):
        start, width = ((0, 128), (256, 256))[c]
        return pl.ds(pl.multiple_of(t * 768 + start + core * width, 128), width)

    def whole_cols(t, c):
        start, width = ((0, 256), (256, 512))[c]
        return pl.ds(pl.multiple_of(t * 768 + start, 256), width)

    def rest_cols(core, along, c):
        return pl.ds(pl.multiple_of(3072 + core * 2048 + along * 1024 + c * 512, 512), 512)

    def deliver_slice(c, buffer):
        cols = slice_cols(z, c, s)
        width = (128, 256)[c]
        buffer[...] = dot(flat, normed[:, cols]).astype(BF).reshape(32, 16, width)
        place_in = rows.at[y, x, :, cols]
        keep(buffer.at[slot_me], place_in, PICK, c)

        def out(k, carry):
            to, core = around(yx, k // 2), (s + k % 2) % 2
            send(buffer.at[core * 16 + to], place_in, PICK, c, core, to, z)
            return carry

        lax.fori_loop(1, 32, out, 0)

    def share_lines(c):
        for along in range(2):
            at = place_on[along]
            source = normed.at[:, rest_cols(s, along, c)]
            keep(source, lines.at[along, c, at], LINES, 2 * along + c)
            for k in (1, 3, 2):
                send(source, lines.at[along, c, at], LINES, 2 * along + c, s, chip((at + k) % 4, along), z)

    def deliver_rest(c):
        for along in range(2):
            wait(lines.at[along, c], LINES, 2 * along + c)
            for t in range(4):
                table = tables[along, t].reshape(128, 128)[:, 0:64]
                rest[along, c, :, :, t] = dot(table, lines[along, c, t]).astype(BF).reshape(2, 4, 16, 512)
            cols = rest_cols(s, along, c)
            place_in = rows.at[y, :, :, cols] if along == 0 else rows.at[:, x, :, cols]
            at = place_on[1 - along]
            keep(rest.at[along, c, s, at], place_in, PICK_REST, 2 * along + c)
            for k in (1, 3, 2):
                t = (at + k) % 4
                for core in range(2):
                    send(rest.at[along, c, core, t], place_in, PICK_REST, 2 * along + c, core, chip(t, 1 - along), z)
            send(rest.at[along, c, 1 - s, at], place_in, PICK_REST, 2 * along + c, 1 - s, yx, z)

    def spread_part(t, c, h):
        return rows.at[2 * h : 2 * h + 2, :, :, whole_cols(t, c)], 8 * c + 2 * t + h

    def spread(c):
        wait(rows.at[:, :, :, whole_cols(z, c)], PICK, c)
        for h in range(2):
            ref, number = spread_part(z, c, h)
            for k in (1, 3):
                send(ref, ref, GATHER, number, s, yx, (z + k) % 4)

    def spread_on(c):
        for k, h in ((3, 0), (1, 1)):
            ref, number = spread_part((z + k) % 4, c, h)
            wait(ref, GATHER, number)
            send(ref, ref, GATHER, number, s, yx, (z + 4 - k) % 4)

    wait(tables.at[0], TABLE, 0)
    wait(tables.at[1], TABLE, 1)
    deliver_slice(0, picked)
    share_lines(0)
    deliver_slice(1, picked_on)
    share_lines(1)
    spread(0)
    deliver_rest(0)
    spread(1)
    spread_on(0)
    deliver_rest(1)
    spread_on(1)

    pltpu.make_async_copy(w_gate, wg, csem.at[8]).wait()
    pltpu.make_async_copy(w_up, wu, csem.at[9]).wait()
    acc[...] = jnp.zeros_like(acc)

    def enter(at):
        some = rows[:, :, :, at].reshape(256, at.size)
        acc[0] += dot(some, wg[at])
        acc[1] += dot(some, wu[at])

    enter(whole_cols(z, 0))
    enter(whole_cols(z, 1))
    for c in range(2):
        for k in (1, 3, 2):
            t = (z + k) % 4
            for h in range(2):
                if (k, h) not in ((3, 0), (1, 1)):
                    ref, number = spread_part(t, c, h)
                    wait(ref, GATHER, number)
            enter(whole_cols(t, c))
        for along in range(2):
            wait(rows.at[:, :, :, pl.ds(0, 1024)], PICK_REST, 2 * along + c)
            for core in range(2):
                enter(rest_cols(core, along, c))
    gate = acc[0]
    hidden[...] = (gate * jax.nn.sigmoid(gate) * acc[1]).astype(BF)
    pltpu.make_async_copy(w_down, wd, csem.at[10]).wait()

    for k in (1, 3, 2, 0):
        t = (z + k) % 4
        got = dot(hidden[...], wd[:, pl.ds(pl.multiple_of(t * 768, 256), 768)]).astype(BF)
        if k == 0:
            yrecv[z] = got
        else:
            ysend[t] = got
    for j in range(4):
        some = pl.ds(pl.multiple_of(((y + j) % 4) * 64, 64), 64)
        for k in (1, 3, 2):
            t = (z + k) % 4
            send(ysend.at[t, some], yrecv.at[z, some], PIECE, (y + j) % 4, s, yx, t)

    for c in range(2):
        for along in range(2):
            at = place_on[1 - along]

            def part_of(core, t):
                source = bsend.at[core, along, c]
                return source.at[t] if along == 0 else source.at[:, t]

            for core in range(2):
                got = dot(hidden[...], wd[:, 3072 + core * 2048 + along * 1024 + c * 512 :][:, 0:512])
                bsend[core, along, c] = got.astype(BF).reshape(4, 4, 16, 512)
            land_in = brecv.at[along, c, s, at]
            keep(part_of(s, at), land_in, HOME, 2 * along + c)
            for k in (1, 3, 2):
                t = (at + k) % 4
                for core in range(2):
                    send(part_of(core, t), land_in, HOME, 2 * along + c, core, chip(t, 1 - along), z)
            send(part_of(1 - s, at), land_in, HOME, 2 * along + c, 1 - s, yx, z)

    def give(core, to):
        src = asend.at[core, pl.ds(pl.multiple_of(to * 16, 16), 16)]
        send(src, back.at[slot_me], BACK, 0, core, to, z)

    def home(c):
        for along in range(2):
            wait(brecv.at[along, c], HOME, 2 * along + c)
            for t in range(4):
                got = brecv[along, c, :, :, t].reshape(128, 512)
                summed = dot(tables[along, t].reshape(128, 128), got, ((0,), (0,)))[64:128]
                tsend_home[along, c, t] = summed.astype(BF)
            at = place_on[along]
            keep(tsend_home.at[along, c, at], trecv_home.at[along, c, at], HOME_ON, 2 * along + c)
            for k in (1, 3, 2):
                t = (at + k) % 4
                send(
                    tsend_home.at[along, c, t], trecv_home.at[along, c, at],
                    HOME_ON, 2 * along + c, s, chip(t, along), z,
                )

    def slices(j):
        to_y = (y + j) % 4
        some = pl.ds(pl.multiple_of(to_y * 64, 64), 64)
        wait(yrecv.at[pl.ds(0, 3), some], PIECE, to_y)
        got = [yrecv[q, some].astype(F32) for q in range(4)]
        total = ((got[0] + got[1]) + (got[2] + got[3])).astype(BF)
        for core in range(2):
            asend[core, some] = total[:, core * 384 : core * 384 + 384]
        if j == 0:
            keep(asend.at[s, land], back.at[slot_me], BACK, 0)
            give(1 - s, yx)
        for core in range(2):
            for k in range(1 if j == 0 else 0, 4):
                give(core, to_y * 4 + (x + k) % 4)

    slices(0)
    home(0)
    slices(1)
    slices(2)
    home(1)
    slices(3)

    result_cols = (slice(0, 512), slice(512, 1024), slice(1024, 1280))

    def finish(n):
        cols = result_cols[n]
        keep(fsend.at[line_me, :, cols], frecv.at[line_me, :, cols], RESULT, n)

        def out(k, carry):
            core, to = (s + k // 4) % 2, (z + k % 4) % 4
            send(fsend.at[core * 4 + to, :, cols], frecv.at[line_me, :, cols], RESULT, n, core, yx, to)
            return carry

        lax.fori_loop(1, 8, out, 0)

    def finish_rest(c):
        total = []
        for along in range(2):
            wait(trecv_home.at[along, c], HOME_ON, 2 * along + c)
            got = [trecv_home[along, c, i].astype(F32) for i in range(4)]
            total.append(((got[0] + got[1]) + (got[2] + got[3])).reshape(8, 8, 512))
        fsend[:, :, result_cols[c]] = jnp.concatenate(total, axis=1).astype(BF)
        finish(c)

    def finish_slices():
        wait(back, BACK, 0)
        total = dot(select[...].reshape(512, 128), back[...].reshape(512, 384), ((0,), (0,)))[64:128]
        low = total[:, 0:256].reshape(8, 8, 256)
        high = jnp.concatenate([total[:, 256:384], jnp.zeros((64, 128), F32)], axis=1).reshape(8, 8, 256)
        fsend[:, :, 1024:1280] = jnp.concatenate([low, high], axis=1).astype(BF)
        finish(2)

    finish_rest(0)
    finish_slices()
    finish_rest(1)

    def write(first, width, moe):
        at = slice(first, first + width)
        stream = gathered[s, :, at].astype(F32)
        own = jnp.zeros((8, width), F32)
        for t in range(4):
            own = jnp.where(z == t, stream[t * 8 : t * 8 + 8], own)
        both[0, :, at] = own.astype(BF)
        both[1, :, at] = (own + moe).astype(BF)

    for c in range(2):
        wait(frecv.at[:, :, result_cols[c]], RESULT, c)
        for core in range(2):
            got = [frecv[core * 4 + t, :, result_cols[c]].astype(F32) for t in range(4)]
            total = (got[0] + got[1]) + (got[2] + got[3])
            write(3072 + core * 2048 + c * 512, 512, total[0:8])
            write(3072 + core * 2048 + 1024 + c * 512, 512, total[8:16])
    wait(frecv.at[:, :, result_cols[2]], RESULT, 2)
    for j in range(8):
        got = frecv[(j % 2) * 4 + j // 2, :, 1024:1280].astype(F32)
        write(j * 384, 256, got[0:8])
        write(j * 384 + 256, 128, got[8:16, 0:128])

    for ref, kind in (
        (wuv.at[:, pl.ds(0, 384)], W_UV),
        (wo.at[pl.ds(0, 384)], W_OUT),
        (rsend.at[pl.ds(0, 3)], RESID),
        (wuv.at[:, half], UV_OVER),
        (wo.at[half], OUT_OVER),
        (late.at[:, pl.ds(0, 15)], LATENT),
        (vals.at[pl.ds(0, 3)], VALUE),
        (orecv.at[:, :, pl.ds(0, 3)], SUM),
        (orecv_on.at[:, :, pl.ds(0, 3)], SUM),
        (tsend.at[:, :, pl.ds(0, 3)], SUM_ON),
        (tsend_on.at[:, :, pl.ds(0, 3)], SUM_ON),
        (gathered.at[s, :, pl.ds(0, 5376)], SLICE),
        (gathered.at[s], ROWS_OVER),
        (route.at[pl.ds(0, 7)], ROUTE),
        (tables.at[:, pl.ds(0, 3)], TABLE),
        (picked.at[pl.ds(0, 31)], PICK),
        (picked_on.at[pl.ds(0, 31)], PICK),
        (lines.at[:, :, pl.ds(0, 3)], LINES),
        (rest.at[:, :, 0], PICK_REST),
        (rest.at[:, :, 1, pl.ds(0, 3)], PICK_REST),
        (rows.at[:, :, :, pl.ds(0, 2304)], GATHER),
        (ysend.at[pl.ds(0, 3)], PIECE),
        (back.at[pl.ds(0, 31)], BACK),
        (brecv.at[:, :, 0], HOME),
        (brecv.at[:, :, 1, pl.ds(0, 3)], HOME),
        (tsend_home.at[:, :, pl.ds(0, 3)], HOME_ON),
        (fsend.at[pl.ds(0, 7)], RESULT),
    ):
        sent(ref, kind)


VMEM = pl.BlockSpec(memory_space=pltpu.VMEM)
SMEM = pl.BlockSpec(memory_space=pltpu.SMEM)
ANY = pl.BlockSpec(memory_space=pl.ANY)


def local(
    queries, cache, lengths, w_uv, w_out, resid, norm_gain, expert_ids, gate_weights, replica_slot, w_gate, w_up, w_down
):
    scratch = [
        pltpu.VMEM((8, 576, 512), BF),
        pltpu.VMEM((8, 576, 128), BF),
        pltpu.VMEM((4, 16, 16, 512), BF),
        pltpu.VMEM((16, 4, 16, 512), BF),
        pltpu.VMEM((512, 1024), BF),
        pltpu.VMEM((1024, 1792), BF),
        pltpu.VMEM((4, 4, 32, 1024), BF),
        pltpu.VMEM((2, 4, 4, 16, 1792), BF),
        pltpu.VMEM((2, 2, 4, 4, 16, 640), BF),
        pltpu.VMEM((2, 2, 4, 4, 16, 256), BF),
        pltpu.VMEM((2, 2, 4, 16, 640), BF),
        pltpu.VMEM((2, 2, 4, 16, 256), BF),
        pltpu.VMEM((2, 2, 4, 16, 640), BF),
        pltpu.VMEM((2, 2, 4, 16, 256), BF),
        pltpu.VMEM((4, 8, 1792), F32),
        pltpu.VMEM((4, 8, 1792), F32),
        pltpu.VMEM((2, 32, 7168), BF),
        pltpu.VMEM((7168, 256), BF),
        pltpu.VMEM((7168, 256), BF),
        pltpu.VMEM((256, 7168), BF),
        pltpu.VMEM((8, 64, 128), BF),
        pltpu.VMEM((64, 7168), BF),
        pltpu.VMEM((2, 4, 4, 16, 128), BF),
        pltpu.VMEM((2, 4, 2, 4, 16, 128), BF),
        pltpu.VMEM((32, 16, 128), BF),
        pltpu.VMEM((32, 16, 256), BF),
        pltpu.VMEM((2, 2, 4, 64, 512), BF),
        pltpu.VMEM((2, 2, 2, 4, 4, 16, 512), BF),
        pltpu.VMEM((4, 4, 16, 7168), BF),
        pltpu.VMEM((2, 256, 256), F32),
        pltpu.VMEM((256, 256), BF),
        pltpu.VMEM((4, 256, 768), BF),
        pltpu.VMEM((4, 256, 768), BF),
        pltpu.VMEM((2, 2, 2, 4, 4, 16, 512), BF),
        pltpu.VMEM((2, 2, 2, 4, 4, 16, 512), BF),
        pltpu.VMEM((2, 2, 4, 64, 512), BF),
        pltpu.VMEM((2, 2, 4, 64, 512), BF),
        pltpu.VMEM((2, 256, 384), BF),
        pltpu.VMEM((32, 16, 384), BF),
        pltpu.VMEM((8, 16, 1280), BF),
        pltpu.VMEM((8, 16, 1280), BF),
    ] + [pltpu.SemaphoreType.DMA((n,)) for n in (19, len(PARTS), sum(PARTS))]
    both = pl.pallas_call(
        kernel,
        out_shape=jax.ShapeDtypeStruct((2, 8, 7168), BF),
        in_specs=[SMEM, SMEM, VMEM, SMEM, ANY, ANY, ANY, ANY, VMEM, VMEM, ANY, ANY, ANY],
        out_specs=VMEM,
        scratch_shapes=scratch,
        compiler_params=pltpu.CompilerParams(collective_id=0, has_side_effects=True, vmem_limit_bytes=60 * MB),
        name="layer",
    )(
        lengths,
        expert_ids.T,
        gate_weights.T,
        replica_slot.T,
        jnp.swapaxes(queries, 1, 2),
        jnp.swapaxes(cache, 1, 2),
        w_uv[0],
        w_out,
        resid,
        norm_gain[None],
        w_gate[0],
        w_up[0],
        w_down[0],
    )
    return both[0], both[1]


def solution(mesh):
    return jax.shard_map(
        local,
        mesh=mesh,
        in_specs=(
            P(("side", "dev"), None, None),
            P(("side", "dev"), None, None),
            P(("side", "dev")),
            P(("side", "dev"), None, None),
            P(("side", "dev"), None),
            P(("side", "dev"), None),
            P(),
            P(("side", "dev"), None),
            P(("side", "dev"), None),
            P(),
            P(("side", "dev"), None, None),
            P(("side", "dev"), None, None),
            P(("side", "dev"), None, None),
        ),
        out_specs=(P(("side", "dev"), None), P(("side", "dev"), None)),
        check_vma=False,
    )
```
